32 devices in a mesh: dp: 8 (over z, y), seq: 4 (over x, core).
Axes of the slice: x: 2, y: 2, z: 4, core: 2. Of those that a mesh axis runs over, the one named last changes fastest.
Arguments:
- inputs: float32 [512, 64, 768], P('seq', 'dp'), may hold values from -6 to 6
- item_counts: int32 [8], P('dp'), may hold values from 4 to 8, as said below
- lengths: int32 [64], P('dp'), may hold values from 32 to 512, as said below
- gain_one: float32 [768], replicated, may hold values from 0.1 to 1.9
- shift_one: float32 [768], replicated, may hold values from -3 to 3
- weight_in: bfloat16 [768, 3072], replicated, may hold values from -0.21875 to 0.21875
- bias_in: float32 [3072], replicated, may hold values from -3 to 3
- weight_out: bfloat16 [3072, 768], replicated, may hold values from -0.15625 to 0.15625
- bias_out: float32 [768], replicated, may hold values from -3 to 3
- gain_two: float32 [768], replicated, may hold values from 0.1 to 1.9
- shift_two: float32 [768], replicated, may hold values from -3 to 3
- cotangent: float32 [512, 64, 768], P('seq', 'dp'), may hold values from -6 to 6
Outputs:
- layer_out: float32 [512, 64, 768], P('seq', 'dp')
- input_grad: float32 [512, 64, 768], P('seq', 'dp')
- gain_one_grad: float32 [768], replicated
- shift_one_grad: float32 [768], replicated
- weight_in_grad: float32 [768, 3072], replicated
- bias_in_grad: float32 [3072], replicated
- weight_out_grad: float32 [3072, 768], replicated
- bias_out_grad: float32 [768], replicated
- gain_two_grad: float32 [768], replicated
- shift_two_grad: float32 [768], replicated
The draws below stay inside these ranges and needn't reach their ends.
Inputs may be any that keep to these rules, and one draw needn't show every extreme that they name: `item_counts`: at least one index of dp has all 8 slots in use. `lengths`: slots at or beyond their device's count are empty whatever their length. On every index of dp one slot in use has length 512.
All inputs are finite; a program needn't handle non-finite values.
Results may differ from the reference program's by a relative error of at most 0.0075.
Values may be sent and summed in bfloat16 or wider, within the bound.
A program may use at most 192 MiB of HBM per device.

```python
import math
import jax
import jax.numpy as jnp
from jax import lax

D = 768
FF = 3072
SEQ = 512
ITEMS_DEV = 8
GROUPS = 8
ITEMS = 64


def shared_items(key):
    key_count, key_full, key_short, key_pick, key_slot = jax.random.split(key, 5)
    groups = ITEMS // ITEMS_DEV
    lowest = max(1, ITEMS_DEV // 2)
    counts = jax.random.randint(key_count, (groups,), lowest, ITEMS_DEV + 1)
    full_group = jax.random.randint(key_full, (), 0, groups)
    counts = jnp.where(jnp.arange(groups) == full_group, ITEMS_DEV, counts)
    short = jax.random.randint(key_short, (groups, ITEMS_DEV), max(1, SEQ // 16), SEQ // 4 + 1)
    pick = jax.random.randint(key_pick, (groups, ITEMS_DEV), 0, 5)
    sizes_drawn = jnp.where(pick == 0, SEQ, short)
    chosen = jax.random.randint(key_slot, (groups,), 0, counts)
    sizes_drawn = jnp.where(jnp.arange(ITEMS_DEV)[None, :] == chosen[:, None], SEQ, sizes_drawn)
    return (counts.astype(jnp.int32), sizes_drawn.reshape(ITEMS).astype(jnp.int32))


def draw_item_counts(key, part):
    return shared_items(key)[0]


def draw_lengths(key, part):
    return shared_items(key)[1]


def shard_levels(stream_key, extent, shards, smallest, high):
    def one(dim, shards_of):
        steps = jax.random.uniform(jax.random.fold_in(jax.random.fold_in(stream_key, 6), dim), (shards_of,), jnp.float32, smallest / len(shards), high / len(shards))
        return jnp.repeat(jnp.exp(steps), extent[dim] // shards_of).reshape((-1,) + (1,) * (len(extent) - dim - 1))

    level = one(*shards[0])
    for cut in shards[1:]:
        level = level * one(*cut)
    return level


def noise(rng, extent, scale, limit, cuts=(), kind=jnp.bfloat16):
    array = jax.random.normal(rng, extent, jnp.float32) * scale
    if len(cuts) > 0:
        array = shard_levels(rng, extent, cuts, -0.22, 0.18) * array
    return jnp.clip(array, min=-limit, max=limit).astype(kind)


def setup_inputs(seed: int = 0) -> dict:
    keys = jax.random.split(jax.random.key(seed), 13)
    return {
        "inputs": noise(keys[0], (SEQ, ITEMS, D), 1.0, 6.0, ((0, 4), (1, 8)), jnp.float32),
        "item_counts": draw_item_counts(jax.random.fold_in(keys[12], 71), 0),
        "lengths": draw_lengths(jax.random.fold_in(keys[12], 71), 0),
        "gain_one": jnp.clip(1.0 + 0.18 * jax.random.normal(keys[3], (D,), jnp.float32), 0.1, 1.9),
        "shift_one": noise(keys[4], (D,), 0.5, 3.0, (), jnp.float32),
        "weight_in": noise(keys[5], (D, FF), D ** -0.5, 0.21875),
        "bias_in": noise(keys[6], (FF,), 0.5, 3.0, (), jnp.float32),
        "weight_out": noise(keys[7], (FF, D), (FF // 2) ** -0.5, 0.15625),
        "bias_out": noise(keys[8], (D,), 0.5, 3.0, (), jnp.float32),
        "gain_two": jnp.clip(1.0 + 0.18 * jax.random.normal(keys[9], (D,), jnp.float32), 0.1, 1.9),
        "shift_two": noise(keys[10], (D,), 0.5, 3.0, (), jnp.float32),
        "cotangent": noise(keys[11], (SEQ, ITEMS, D), 1.0, 6.0, ((0, 4), (1, 8)), jnp.float32),
    }


EPSILON = 1e-05

@jax.custom_vjp
def low(v):
    return lax.optimization_barrier(v.astype(jnp.bfloat16)).astype(jnp.float32)

@jax.custom_vjp
def low_back(v):
    return v

def low_keep(v):
    return (low(v), None)

def low_pass(kept, grad):
    return (grad,)

def back_keep(v):
    return (v, None)

def back_low(kept, grad):
    return (low(grad),)
low.defvjp(low_keep, low_pass)
low_back.defvjp(back_keep, back_low)

def matmul(left, right):
    return jnp.dot(left, right, precision=lax.Precision.HIGHEST, preferred_element_type=jnp.float32)

def angle_table(count):
    index = jnp.arange(count, dtype=jnp.int32)
    product = index[:, None] * index[None, :] % count
    return product.astype(jnp.float32) * (2.0 * math.pi / count)

def layer_norm(values, gain, shift):
    center = values - lax.optimization_barrier(jnp.mean(values, axis=-1, keepdims=True))
    spread = lax.optimization_barrier(jnp.mean(center * center, axis=-1, keepdims=True))
    return center * lax.rsqrt(spread + EPSILON) * gain + shift

def block_forward(block, live_block, params, tables):
    gain_one, shift_one, weight_in, bias_in, weight_out, bias_out, gain_two, shift_two = params
    hidden_cos, hidden_sin, seq_cos, seq_sin = tables
    seq_len, group, features = block.shape
    masked = block * live_block[:, :, None]
    rounded = low(masked)
    flat = rounded.reshape(seq_len * group, features)
    cos_part = low(low_back(matmul(flat, hidden_cos))).reshape(seq_len, group * features)
    sin_part = low(low_back(matmul(flat, hidden_sin))).reshape(seq_len, group * features)
    mixed = (matmul(seq_cos, cos_part) - matmul(seq_sin, sin_part)) * (1.0 / math.sqrt(features * seq_len))
    mixed = low(low_back(mixed)).reshape(seq_len, group, features)
    summed = masked + mixed
    normed = layer_norm(summed, gain_one, shift_one).reshape(seq_len * group, features)
    hidden = low_back(matmul(low(normed), weight_in) + bias_in)
    active = low(jax.nn.gelu(hidden, approximate=False))
    branch = low_back(matmul(active, weight_out) + bias_out)
    second = summed + branch.reshape(seq_len, group, features)
    return layer_norm(second, gain_two, shift_two) * live_block[:, :, None]

def reference(inputs, item_counts, lengths, gain_one, shift_one, weight_in, bias_in, weight_out, bias_out, gain_two, shift_two, cotangent):
    params = (gain_one, shift_one, weight_in.astype(jnp.float32), bias_in, weight_out.astype(jnp.float32), bias_out, gain_two, shift_two)
    hidden_angle = angle_table(D)
    seq_angle = angle_table(SEQ)
    tables = (low(jnp.cos(hidden_angle)), low(jnp.sin(hidden_angle)), low(jnp.cos(seq_angle)), low(jnp.sin(seq_angle)))
    item_index = jnp.arange(ITEMS, dtype=jnp.int32)
    used_slot = item_index % ITEMS_DEV < item_counts[item_index // ITEMS_DEV]
    positions = jnp.arange(SEQ, dtype=jnp.int32)
    live = ((positions[:, None] < lengths[None, :]) & used_slot[None, :]).astype(jnp.float32)
    grouped_input = inputs.reshape(SEQ, GROUPS, ITEMS_DEV, D).transpose(1, 0, 2, 3)
    grouped_live = live.reshape(SEQ, GROUPS, ITEMS_DEV).transpose(1, 0, 2)
    grouped_cot = cotangent.reshape(SEQ, GROUPS, ITEMS_DEV, D).transpose(1, 0, 2, 3)

    def step(totals, pieces):
        block, live_block, cot_block = pieces

        def run(block_in, params_in):
            return block_forward(block_in, live_block, params_in, tables)
        output, pullback = jax.vjp(run, block, params)
        grad_block, grad_params = pullback(cot_block)
        return (jax.tree.map(jnp.add, totals, grad_params), (output, grad_block))
    zeros = jax.tree.map(jnp.zeros_like, params)
    totals, (outputs, grads) = lax.scan(step, zeros, (grouped_input, grouped_live, grouped_cot))
    layer_out = outputs.transpose(1, 0, 2, 3).reshape(SEQ, ITEMS, D)
    input_grad = grads.transpose(1, 0, 2, 3).reshape(SEQ, ITEMS, D)
    return (layer_out, input_grad, totals[0], totals[1], totals[2], totals[3], totals[4], totals[5], totals[6], totals[7])
```

```python
import functools
import math

import jax
import jax.numpy as jnp
from jax import lax
from jax.experimental import pallas as pl
from jax.experimental.pallas import tpu as pltpu
from jax.sharding import PartitionSpec as P

EPSILON = 1e-05
MESH = pl.DeviceIdType.MESH

def cube_bits(sizes):
    bits = []
    for axis, name in ((1, "seq"), (0, "dp")):
        k = 1
        while k < sizes[name]:
            bits.append((axis, k)); k *= 2
    return bits

def orders_of(bits):
    first, rest = bits[:1], bits[1:]
    return [first + rest, first + [rest[1], rest[0]] + rest[2:], first + [rest[2], rest[0], rest[1]] + rest[3:]]

class Cube:
    def __init__(self, sizes):
        self.me = (lax.axis_index("dp"), lax.axis_index("seq"))
        self.orders = orders_of(cube_bits(sizes))
        self.stages = len(self.orders[0])
    def value(self, bit):
        axis, k = bit
        return (self.me[axis] // k) % 2
    def partner(self, bit):
        axis, k = bit
        other = self.me[axis] + k * (1 - 2 * self.value(bit))
        return (other, self.me[1]) if axis == 0 else (self.me[0], other)
    def offset(self, order, level, rows):
        off = 0
        for s in range(level):
            off = off + self.value(self.orders[order][s]) * (rows >> (s + 1))
        return off

def ar_kernel(sizes, lags, x_ref, o_ref, buf, full, *rest):
    n_chunk, rows, _ = buf.shape
    cube = Cube(sizes)
    S = cube.stages
    recv = rest[:S]
    insem, outsem, rs_s, rs_r, ag_s, ag_r = rest[S:]
    bar = pltpu.get_barrier_semaphore()
    for bit in cube.orders[0]:
        pl.semaphore_signal(bar, inc=1, device_id=cube.partner(bit), device_id_type=MESH)
    pl.semaphore_wait(bar, S)
    def load(c): return pltpu.make_async_copy(x_ref.at[c], buf.at[c], insem.at[c])
    def out(c): return pltpu.make_async_copy(full.at[c], o_ref.at[c], outsem.at[c])
    def rs(c, o, s):
        bit = cube.orders[o][s]; h = rows >> (s + 1)
        off = cube.offset(o, s, rows) + (1 - cube.value(bit)) * h
        return pltpu.make_async_remote_copy(src_ref=buf.at[c, pl.ds(pl.multiple_of(off, 16), h)], dst_ref=recv[s].at[c],
            send_sem=rs_s.at[s, c], recv_sem=rs_r.at[s, c], device_id=cube.partner(bit), device_id_type=MESH)
    def ag(c, o, s):
        bit = cube.orders[o][s]; h = rows >> (s + 1)
        off = pl.multiple_of(cube.offset(o, s + 1, rows), 16)
        return pltpu.make_async_remote_copy(src_ref=full.at[c, pl.ds(off, h)], dst_ref=full.at[c, pl.ds(off, h)],
            send_sem=ag_s.at[s, c], recv_sem=ag_r.at[s, c], device_id=cube.partner(bit), device_id_type=MESH)
    def add(c, o, s):
        h = rows >> (s + 1)
        off = pl.multiple_of(cube.offset(o, s + 1, rows), 16)
        target = full if s == S - 1 else buf
        target[c, pl.ds(off, h), :] = (buf[c, pl.ds(off, h), :].astype(jnp.float32) + recv[s][c].astype(jnp.float32)).astype(jnp.bfloat16)
    def event(k, c, o):
        if k == 0:
            load(c).wait()
            rs(c, o, 0).start()
        elif k < S:
            rs(c, o, k - 1).wait()
            add(c, o, k - 1)
            rs(c, o, k).start()
        elif k == S:
            rs(c, o, S - 1).wait()
            add(c, o, S - 1)
            ag(c, o, S - 1).start()
        elif k < 2 * S:
            s = 2 * S - k
            ag(c, o, s).wait()
            ag(c, o, s - 1).start()
        else:
            ag(c, o, 0).wait()
            out(c).start()
    def pre(c, _):
        load(c).start(); return 0
    lax.fori_loop(0, n_chunk, pre, 0)
    when = [0]
    for l in lags: when.append(when[-1] + l)
    total = n_chunk + when[-1]
    def body(g, _):
        for j in range(3):
            for k in reversed(range(2 * S + 1)):
                c = 3 * g + j - when[k]
                o = (j - when[k]) % 3
                @pl.when((c >= 0) & (c < n_chunk))
                def _(): event(k, c, o)
        return 0
    lax.fori_loop(0, -(-total // 3), body, 0)
    def post(c, _):
        out(c).wait(); return 0
    lax.fori_loop(0, n_chunk, post, 0)

def all_reduce(x, sizes, lags, cid, name="ar"):
    n_chunk, rows, lanes = x.shape
    S = len(cube_bits(sizes))
    lags = (lags[: S] + [2] * S)[: S] + ([2] * S + lags[-S:])[-S:]
    return pl.pallas_call(functools.partial(ar_kernel, sizes, lags), name=name,
        out_shape=jax.ShapeDtypeStruct(x.shape, x.dtype),
        in_specs=[pl.BlockSpec(memory_space=pl.ANY)], out_specs=pl.BlockSpec(memory_space=pl.ANY),
        scratch_shapes=[pltpu.VMEM(x.shape, x.dtype)] * 2 + [pltpu.VMEM((n_chunk, rows >> (s + 1), lanes), x.dtype) for s in range(S)]
          + [pltpu.SemaphoreType.DMA((n_chunk,))] * 2 + [pltpu.SemaphoreType.DMA((S, n_chunk))] * 4,
        compiler_params=pltpu.CompilerParams(collective_id=cid, has_side_effects=True, vmem_limit_bytes=58 << 20))(x)


def dft_tables(count):
    index = jnp.arange(count, dtype=jnp.int32)
    angle = (index[:, None] * index[None, :] % count).astype(jnp.float32) * (2.0 * math.pi / count)
    return (jnp.cos(angle).astype(jnp.bfloat16), jnp.sin(angle).astype(jnp.bfloat16))


def normalize(values):
    center = values - jnp.mean(values, axis=-1, keepdims=True)
    spread = jnp.mean(center * center, axis=-1, keepdims=True)
    inverse = lax.rsqrt(spread + EPSILON)
    return (center * inverse, inverse)


def norm_back(grad_hat, normal, inverse):
    first = jnp.mean(grad_hat, axis=-1, keepdims=True)
    second = jnp.mean(grad_hat * normal, axis=-1, keepdims=True)
    return inverse * (grad_hat - first - normal * second)


def smooth_gate(values):
    return jax.nn.gelu(values, approximate=False)


def contract_rows(left, right):
    return lax.dot_general(
        left, right, (((0,), (0,)), ((), ())), preferred_element_type=jnp.float32
    )


def contract_cols(left, right):
    return lax.dot_general(
        left, right, (((1,), (1,)), ((), ())), preferred_element_type=jnp.float32
    )


def spectral(rounded, tables, again):
    hidden_cos, hidden_sin, seq_cos, seq_sin, dft_scale = tables
    row_count, item_count, features = rounded.shape
    flat = rounded.reshape(row_count * item_count, features)
    cos_part = (
        jnp.dot(flat, hidden_cos, preferred_element_type=jnp.float32)
        .astype(jnp.bfloat16)
        .reshape(row_count, item_count, features)
    )
    sin_part = (
        jnp.dot(flat, hidden_sin, preferred_element_type=jnp.float32)
        .astype(jnp.bfloat16)
        .reshape(row_count, item_count, features)
    )

    def transform(parts):
        cos_cols, sin_cols = parts
        seq_total = cos_cols.shape[0]
        joined = jnp.dot(
            seq_cos, cos_cols.reshape(seq_total, -1), preferred_element_type=jnp.float32
        )
        joined = joined - jnp.dot(
            seq_sin, sin_cols.reshape(seq_total, -1), preferred_element_type=jnp.float32
        )
        return (joined * dft_scale).astype(jnp.bfloat16).reshape(cos_cols.shape)

    if again:
        columns = transform(
            (
                lax.all_to_all(cos_part, "seq", split_axis=2, concat_axis=0, tiled=True),
                lax.all_to_all(sin_part, "seq", split_axis=2, concat_axis=0, tiled=True),
            )
        )
        mixed = lax.all_to_all(columns, "seq", split_axis=0, concat_axis=2, tiled=True)
    else:
        columns = transform(
            (
                lax.all_to_all(cos_part, "seq", split_axis=2, concat_axis=0, tiled=True),
                lax.all_to_all(sin_part, "seq", split_axis=2, concat_axis=0, tiled=True),
            )
        )
        mixed = lax.all_to_all(columns, "seq", split_axis=0, concat_axis=2, tiled=True)
    return mixed.astype(jnp.float32)


def dense_forward(masked_input, mixed, params):
    gain_one, shift_one, weight_in, bias_in, weight_out, bias_out = params
    features = masked_input.shape[2]
    summed = masked_input + mixed
    hat_one, inverse_one = normalize(summed)
    normed = (hat_one * gain_one + shift_one).astype(jnp.bfloat16).reshape(-1, features)
    hidden = jnp.dot(normed, weight_in, preferred_element_type=jnp.float32) + bias_in
    active = smooth_gate(hidden).astype(jnp.bfloat16)
    branch = jnp.dot(active, weight_out, preferred_element_type=jnp.float32) + bias_out
    second = summed + branch.reshape(summed.shape)
    hat_two, inverse_two = normalize(second)
    return (summed, hat_one, inverse_one, normed, hidden, active, hat_two, inverse_two)


def per_device(
    inputs,
    item_counts,
    lengths,
    gain_one,
    shift_one,
    weight_in,
    bias_in,
    weight_out,
    bias_out,
    gain_two,
    shift_two,
    cotangent,
):
    row_count, item_count, features = inputs.shape
    seq_total = row_count * lax.axis_size("seq")
    hidden_cos, hidden_sin = dft_tables(features)
    seq_cos, seq_sin = dft_tables(seq_total)
    tables = (hidden_cos, hidden_sin, seq_cos, seq_sin, 1.0 / math.sqrt(features * seq_total))
    positions = lax.axis_index("seq") * row_count + jnp.arange(row_count, dtype=jnp.int32)
    used_slot = jnp.arange(item_count, dtype=jnp.int32) < item_counts[0]
    live_mask = ((positions[:, None] < lengths[None, :]) & used_slot[None, :]).astype(jnp.float32)[
        :, :, None
    ]
    masked_input = inputs * live_mask
    rounded = masked_input.astype(jnp.bfloat16)
    params = (gain_one, shift_one, weight_in, bias_in, weight_out, bias_out)
    mixed = spectral(rounded, tables, False)
    summed, hat_one, inverse_one, normed, hidden, active, hat_two, inverse_two = dense_forward(
        masked_input, mixed, params
    )
    layer_out = (hat_two * gain_two + shift_two) * live_mask
    mixed_again = spectral(rounded, tables, True)
    summed, hat_one, inverse_one, normed, hidden, active, hat_two, inverse_two = dense_forward(
        masked_input, mixed_again, params
    )
    grad_out = cotangent * live_mask
    grad_gain_two = jnp.sum(grad_out * hat_two, axis=(0, 1))
    grad_shift_two = jnp.sum(grad_out, axis=(0, 1))
    grad_second = norm_back(grad_out * gain_two, hat_two, inverse_two)
    grad_branch = grad_second.astype(jnp.bfloat16).reshape(-1, features)
    grad_bias_out = jnp.sum(grad_branch.astype(jnp.float32), axis=0)
    grad_weight_out = contract_rows(active, grad_branch)
    grad_active = contract_cols(grad_branch, weight_out)
    gate_pull = jax.vjp(smooth_gate, hidden)[1]
    grad_hidden = gate_pull(grad_active)[0].astype(jnp.bfloat16)
    grad_bias_in = jnp.sum(grad_hidden.astype(jnp.float32), axis=0)
    grad_weight_in = contract_rows(normed, grad_hidden)
    grad_normed = contract_cols(grad_hidden, weight_in).reshape(summed.shape)
    grad_gain_one = jnp.sum(grad_normed * hat_one, axis=(0, 1))
    grad_shift_one = jnp.sum(grad_normed, axis=(0, 1))
    grad_summed = grad_second + norm_back(grad_normed * gain_one, hat_one, inverse_one)
    grad_mixed = grad_summed.astype(jnp.bfloat16)
    dft_scale = tables[4]
    piece = lax.all_to_all(grad_mixed, "seq", split_axis=2, concat_axis=0, tiled=True)
    flat_piece = piece.reshape(piece.shape[0], -1)
    grad_cos = (
        jnp.dot(seq_cos, flat_piece, preferred_element_type=jnp.float32) * dft_scale
    ).astype(jnp.bfloat16)
    grad_sin = (
        -(jnp.dot(seq_sin, flat_piece, preferred_element_type=jnp.float32) * dft_scale)
    ).astype(jnp.bfloat16)
    grad_cos_rows, grad_sin_rows = (
        lax.all_to_all(
            grad_cos.reshape(piece.shape), "seq", split_axis=0, concat_axis=2, tiled=True
        ),
        lax.all_to_all(
            grad_sin.reshape(piece.shape), "seq", split_axis=0, concat_axis=2, tiled=True
        ),
    )
    grad_rounded = jnp.dot(
        grad_cos_rows.reshape(-1, features), hidden_cos, preferred_element_type=jnp.float32
    )
    grad_rounded = grad_rounded + jnp.dot(
        grad_sin_rows.reshape(-1, features), hidden_sin, preferred_element_type=jnp.float32
    )
    input_grad = (grad_summed + grad_rounded.reshape(summed.shape)) * live_mask
    small = jnp.concatenate(
        [grad_gain_one, grad_shift_one, grad_bias_in, grad_bias_out, grad_gain_two, grad_shift_two]
    )
    small = lax.psum(small, ("dp", "seq"))
    sizes = {"dp": lax.axis_size("dp"), "seq": lax.axis_size("seq")}
    wide = grad_weight_in.shape[1]
    count = wide // 128
    left = grad_weight_in.astype(jnp.bfloat16).reshape(features, count, 128).transpose(1, 0, 2)
    right = grad_weight_out.astype(jnp.bfloat16).reshape(count, 128, features // 128, 128)
    right = right.transpose(0, 2, 1, 3).reshape(count, features, 128)
    packed = jnp.concatenate([left, right], axis=1)
    group = max(1, sizes["dp"] * sizes["seq"] * 16 // packed.shape[1])
    while packed.shape[1] * group % (sizes["dp"] * sizes["seq"] * 16):
        group += 1
    done = all_reduce(packed.reshape(count // group, -1, 128), sizes, [2, 4, 3, 2, 2, 2, 2, 3, 4, 2], 1)
    done = done.reshape(packed.shape)
    total_in = done[:, :features].transpose(1, 0, 2).reshape(features, wide).astype(jnp.float32)
    total_out = done[:, features:].reshape(count, features // 128, 128, 128).transpose(0, 2, 1, 3)
    total_out = total_out.reshape(wide, features).astype(jnp.float32)
    cuts = [features, 2 * features, 2 * features + wide, 3 * features + wide, 4 * features + wide]
    parts = jnp.split(small, cuts)
    return (
        layer_out,
        input_grad,
        parts[0],
        parts[1],
        total_in,
        parts[2],
        total_out,
        parts[3],
        parts[4],
        parts[5],
    )


def solution(mesh):
    placed = (
        P("seq", "dp", None),
        P("dp"),
        P("dp"),
        P(),
        P(),
        P(),
        P(),
        P(),
        P(),
        P(),
        P(),
        P("seq", "dp", None),
    )
    return jax.shard_map(
        per_device,
        mesh=mesh,
        in_specs=placed,
        out_specs=(
            P("seq", "dp", None),
            P("seq", "dp", None),
            P(),
            P(),
            P(),
            P(),
            P(),
            P(),
            P(),
            P(),
        ),
        check_vma=False,
    )
```

```python
import functools
import math

import jax
import jax.numpy as jnp
import numpy as np
from jax import lax
from jax.experimental import pallas as pl
from jax.experimental.pallas import tpu as pltpu
from jax.sharding import PartitionSpec as P

EPSILON = 1e-05
MESH = pl.DeviceIdType.MESH
LANES = 128
WIDE = 256
BF16 = jnp.bfloat16
F32 = jnp.float32


def dft_tables(count):
    index = np.arange(count, dtype=np.int64)
    turns = (index[:, None] * index[None, :] % count).astype(np.float32)
    angle = (turns * np.float32(2.0 * math.pi / count)).astype(np.float64)
    return np.cos(angle).astype(np.float32), np.sin(angle).astype(np.float32)


def aligned(value, step):
    return pl.multiple_of(value, step)


def bit_of(value, k):
    return (value // k) % 2


def flipped(value, k):
    return value + k * (1 - 2 * bit_of(value, k))


def axis_bits(axis, size):
    return [(axis, 1 << b) for b in range(size.bit_length() - 1)]


class Cube:
    def __init__(self, sizes):
        dp, seq = sizes
        bits = axis_bits(1, seq) + axis_bits(0, dp)
        first, rest = bits[:1], bits[1:]
        self.orders = [
            first + rest,
            first + [rest[1], rest[0]] + rest[2:],
            first + [rest[2], rest[0], rest[1]] + rest[3:],
        ]
        self.bits = bits
        self.stages = len(bits)
        self.me = (lax.axis_index("dp"), lax.axis_index("seq"))

    def value(self, bit):
        return bit_of(self.me[bit[0]], bit[1])

    def partner(self, bit):
        axis, k = bit
        other = flipped(self.me[axis], k)
        return (other, self.me[1]) if axis == 0 else (self.me[0], other)

    def offset(self, order, level, rows):
        total = 0
        for s in range(level):
            total = total + self.value(self.orders[order][s]) * (rows >> (s + 1))
        return total


class Exchange:
    def __init__(self, size, rows, buf, send, recv):
        self.size, self.rows, self.buf, self.send_sem, self.recv_sem = size, rows, buf, send, recv
        self.dp, self.q = lax.axis_index("dp"), lax.axis_index("seq")
        self.order = [1 << b for b in reversed(range(size.bit_length() - 1))]

    def owner(self, pattern):
        index = self.q
        for k in self.order:
            if pattern & k:
                index = flipped(index, k)
        return index

    def copy(self, slot, pattern):
        hop = pattern & -pattern
        place = pl.ds(aligned(self.owner(pattern - hop) * self.rows, self.rows), self.rows)
        ref = self.buf.at[slot, place]
        return pltpu.make_async_remote_copy(
            src_ref=ref,
            dst_ref=ref,
            send_sem=self.send_sem.at[slot, pattern],
            recv_sem=self.recv_sem.at[slot, pattern],
            device_id=(self.dp, flipped(self.q, hop)),
            device_id_type=MESH,
        )

    def patterns(self, far):
        return range(1, self.size) if far else range(1, 2)

    def start_own(self, slot, far):
        for pattern in self.patterns(far):
            if pattern & (pattern - 1) == 0:
                self.copy(slot, pattern).start()

    def forward(self, slot):
        for pattern in self.patterns(True):
            if pattern & 1 == 0:
                self.copy(slot, pattern).wait_recv()
                for k in self.order:
                    if k < (pattern & -pattern):
                        self.copy(slot, pattern | k).start()

    def wait_near(self, slot, far):
        for pattern in self.patterns(far):
            if pattern & 1:
                self.copy(slot, pattern).wait_recv()

    def wait_sends(self, slot, far):
        for pattern in self.patterns(far):
            self.copy(slot, pattern).wait_send()


def greet(partners):
    barrier = pltpu.get_barrier_semaphore()
    for partner in partners:
        pl.semaphore_signal(barrier, inc=1, device_id=partner, device_id_type=MESH)
    pl.semaphore_wait(barrier, len(partners))


def rank_slots(count_ref, length_ref, perm_s, slen_s, slots):
    count = count_ref[0]
    live = [jnp.where(i < count, length_ref[i], 0) for i in range(slots)]
    ranks = []
    for i in range(slots):
        rank = 0
        for k in range(slots):
            if k != i:
                ahead = live[k] >= live[i] if k < i else live[k] > live[i]
                rank = rank + jnp.where(ahead, 1, 0)
        ranks.append(rank)
    for j in range(slots):
        perm, length = 0, 0
        for i in range(slots):
            here = ranks[i] == j
            perm = perm + jnp.where(here, i, 0)
            length = length + jnp.where(here, live[i], 0)
        perm_s[j] = perm
        slen_s[j] = length


def live_rows(slen_s, slot, first, rows):
    position = first + lax.broadcasted_iota(jnp.int32, (rows, 1), 0)
    return position < slen_s[slot]


def fold8(values):
    rows, lanes = values.shape
    return values.reshape(rows // 8, 8, lanes).sum(axis=0)


def normalize(values):
    center = values - jnp.mean(values, axis=-1, keepdims=True)
    spread = jnp.mean(center * center, axis=-1, keepdims=True)
    inverse = lax.rsqrt(spread + EPSILON)
    return center * inverse, inverse


def norm_back(grad_hat, normal, inverse):
    first = jnp.mean(grad_hat, axis=-1, keepdims=True)
    second = jnp.mean(grad_hat * normal, axis=-1, keepdims=True)
    return inverse * (grad_hat - first - normal * second)


def mix_slot(slot, far, exchange, tables, buf, uv, place):
    rows = exchange.rows
    if far:
        table, block = tables[...], buf[slot]
    else:
        base = aligned(exchange.q // 2 * (2 * rows), 2 * rows)
        table, block = tables[:, pl.ds(base, 2 * rows)], buf[slot, pl.ds(base, 2 * rows), :]
    both = jnp.dot(table, block, preferred_element_type=F32).astype(BF16)
    width = both.shape[1]
    uv[pl.ds(place, rows), :width] = both[:rows]
    uv[pl.ds(place, rows), width:] = both[rows:]


def forward_kernel(cfg, *refs):
    sizes, far_slots, slots, group = cfg
    (
        count_ref, length_ref, gain_one, shift_one, bias_in, bias_out, gain_two, shift_two,
        x_hbm, cot_hbm, wi_hbm, wo_hbm, sc_hbm, hc_hbm,
        act_o, dg_o, nrm_o, sum_o, gs_o, lo_o, part_o,
        perm_s, slen_s, x_v, cot_v, wi_v, wo_v, sc_v, hc_v, buf, uv, sum_v, nrm_v, act_v, dg_v, gs_v, lo_v,
        load_sem, out_sem, send_sem, recv_sem,
    ) = refs
    rows, _, features = x_v.shape
    wide = wi_v.shape[1]
    seq_total = rows * sizes[1]
    scale = 1.0 / math.sqrt(features * seq_total)
    exchange = Exchange(sizes[1], rows, buf, send_sem, recv_sem)
    q = exchange.q
    first = q * rows
    loads = [
        pltpu.make_async_copy(x_hbm, x_v, load_sem.at[0]),
        pltpu.make_async_copy(sc_hbm.at[q], sc_v, load_sem.at[1]),
        pltpu.make_async_copy(hc_hbm, hc_v, load_sem.at[2]),
        pltpu.make_async_copy(wi_hbm, wi_v, load_sem.at[3]),
        pltpu.make_async_copy(wo_hbm, wo_v, load_sem.at[4]),
        pltpu.make_async_copy(cot_hbm, cot_v, load_sem.at[5]),
    ]
    for load in loads:
        load.start()
    rank_slots(count_ref, length_ref, perm_s, slen_s, slots)
    greet([(exchange.dp, flipped(q, k)) for k in exchange.order])
    loads[0].wait()

    def prepare(slot):
        value = jnp.where(live_rows(slen_s, slot, first, rows), x_v[:, perm_s[slot], :], 0.0)
        sum_v[pl.ds(aligned(slot * rows, rows), rows), :] = value
        buf[slot, pl.ds(aligned(first, rows), rows), :] = value.astype(BF16)

    def prepare_far(i, _):
        slot = far_slots - 1 - i
        prepare(slot)
        exchange.start_own(slot, True)
        return 0

    def prepare_near(i, _):
        prepare(far_slots + i)
        exchange.start_own(far_slots + i, False)
        return 0

    lax.fori_loop(0, far_slots, prepare_far, 0)
    lax.fori_loop(0, slots - far_slots, prepare_near, 0)
    part_o[...] = jnp.zeros_like(part_o)
    for load in loads[1:3]:
        load.wait()

    batch = group * rows
    span = min(3 * WIDE, wide)

    def outs(base):
        place = pl.ds(base, batch)
        copies = [
            pltpu.make_async_copy(nrm_v.at[place], nrm_o.at[place], out_sem.at[0]),
            pltpu.make_async_copy(sum_v.at[place], sum_o.at[place], out_sem.at[1]),
            pltpu.make_async_copy(gs_v.at[place], gs_o.at[place], out_sem.at[2]),
            pltpu.make_async_copy(lo_v.at[place], lo_o.at[place], out_sem.at[3]),
        ]
        for n in range(wide // WIDE):
            cut = pl.ds(n * WIDE, WIDE)
            copies.append(pltpu.make_async_copy(act_v.at[place, cut], act_o.at[n, place], out_sem.at[4]))
            copies.append(pltpu.make_async_copy(dg_v.at[place, cut], dg_o.at[n, place], out_sem.at[5]))
        return copies

    def mixing(slot0, flags):
        for i, far in enumerate(flags):
            exchange.wait_near(slot0 + i, far)
            mix_slot(slot0 + i, far, exchange, sc_v, buf, uv, i * rows)

    def dense(slot0):
        base = aligned(slot0 * rows, batch)
        place = pl.ds(base, batch)
        uv_out = jnp.dot(uv[...], hc_v[...], preferred_element_type=F32)
        sum_v[place, :] = sum_v[place, :] + (uv_out * scale).astype(BF16).astype(F32)

        def norm_one(i, _):
            here = pl.ds(aligned(base + i * rows, rows), rows)
            hat, _ = normalize(sum_v[here, :])
            nrm_v[here, :] = (hat * gain_one[...] + shift_one[...]).astype(BF16)
            return 0

        lax.fori_loop(0, group, norm_one, 0)

        def expand(n, _):
            cut = pl.ds(aligned(n * span, span), span)
            hidden = jnp.dot(nrm_v[place, :], wi_v[:, cut], preferred_element_type=F32) + bias_in[:, cut]
            gate = 0.5 + 0.5 * lax.erf(hidden * math.sqrt(0.5))
            slope = gate + hidden * (jnp.exp(hidden * hidden * -0.5) * (1.0 / math.sqrt(2.0 * math.pi)))
            act_v[place, cut] = (hidden * gate).astype(BF16)
            dg_v[place, cut] = slope.astype(BF16)
            return 0

        lax.fori_loop(0, wide // span, expand, 0)
        lo_v[place, :] = jnp.dot(act_v[place, :], wo_v[...], preferred_element_type=F32)

        def norm_two(i, _):
            here = pl.ds(aligned(base + i * rows, rows), rows)
            slot = slot0 + i
            live = live_rows(slen_s, slot, first, rows)
            hat, inverse = normalize(sum_v[here, :] + (lo_v[here, :] + bias_out[...]))
            grad = jnp.where(live, cot_v[:, perm_s[slot], :], 0.0)
            lo_v[here, :] = jnp.where(live, hat * gain_two[...] + shift_two[...], 0.0)
            part_o[0:8, :] = part_o[0:8, :] + fold8(grad * hat)
            part_o[8:16, :] = part_o[8:16, :] + fold8(grad)
            second = norm_back(grad * gain_two[...], hat, inverse)
            gs_v[here, :] = second
            part_o[16:24, :] = part_o[16:24, :] + fold8(second.astype(BF16).astype(F32))
            return 0

        lax.fori_loop(0, group, norm_two, 0)
        for copy in outs(base):
            copy.start()

    count = slots // group
    near_groups = (slots - far_slots) // group
    work = list(range(count - near_groups, count)) + list(range(count - near_groups - 1, -1, -1))
    ready = set()

    def bring(g):
        for slot in range(g * group + group - 1, g * group - 1, -1):
            if slot < far_slots and slot not in ready:
                ready.add(slot)
                exchange.forward(slot)

    for at, g in enumerate(work):
        bring(g)
        mixing(g * group, [g * group + i < far_slots for i in range(group)])
        if at == 0:
            for load in loads[3:]:
                load.wait()
        if at + 1 < len(work):
            bring(work[at + 1])
        dense(g * group)

    for slot in range(slots):
        exchange.wait_sends(slot, slot < far_slots)
    for g in range(count):
        for copy in outs(g * batch):
            copy.wait()


def backward_kernel(cfg, *refs):
    sizes, far_slots, slots, group, lags, plan = cfg
    cube = Cube(sizes)
    S = cube.stages
    (
        count_ref, length_ref, gain_one, part_ref,
        act_hbm, dg_hbm, nrm_hbm, sum_hbm, gs_hbm, wi_hbm, wo_hbm, sc_hbm, hc_hbm,
        full_o, ig_o, small_o,
        perm_s, slen_s, gs_v, sum_v, nrm_v, gb_v, gh_v, gn_v, act_v, dg_v, wi_v, wo_v, sc_v, hc_v, buf, uv, ig_v,
        bin_v, one_v, small_v, part_v, full,
    ) = refs[: 16 + 22]
    landed = refs[38 : 38 + S]
    (
        small_recv, load_sem, sum_sem, stream_sem, out_sem, ig_sem, send_sem, recv_sem,
        rs_s, rs_r, ag_s, ag_r, sm_s, sm_r,
    ) = refs[38 + S :]
    ticks, tick_rows, _ = part_v.shape
    parts = 3
    message = tick_rows // parts
    chunks = act_hbm.shape[0]
    per_tick = chunks // ticks
    total = ticks * parts
    features = nrm_v.shape[1]
    rows = gs_v.shape[0] // slots
    scale = 1.0 / math.sqrt(features * rows * sizes[1])
    exchange = Exchange(sizes[1], rows, buf, send_sem, recv_sem)
    q = exchange.q
    first = q * rows
    loads = [
        pltpu.make_async_copy(gs_hbm, gs_v, load_sem.at[0]),
        pltpu.make_async_copy(nrm_hbm, nrm_v, load_sem.at[1]),
        pltpu.make_async_copy(sc_hbm.at[q], sc_v, load_sem.at[2]),
        pltpu.make_async_copy(hc_hbm, hc_v, load_sem.at[3]),
    ]

    def sum_copy(i):
        slot = jnp.where(i < far_slots, far_slots - 1 - i, i)
        place = pl.ds(aligned(slot * rows, rows), rows)
        return pltpu.make_async_copy(sum_hbm.at[place], sum_v.at[i % 2], sum_sem.at[i % 2])

    def streams(n, slot):
        cut = pl.ds(aligned(n * WIDE, WIDE), WIDE)
        return [
            pltpu.make_async_copy(wo_hbm.at[cut], wo_v.at[slot], stream_sem.at[0, slot]),
            pltpu.make_async_copy(dg_hbm.at[n], dg_v.at[slot], stream_sem.at[1, slot]),
            pltpu.make_async_copy(act_hbm.at[n], act_v.at[slot], stream_sem.at[2, slot]),
            pltpu.make_async_copy(wi_hbm.at[:, cut], wi_v.at[slot], stream_sem.at[3, slot]),
        ]

    loads[0].start()
    for copy in streams(0, 0):
        copy.start()
    for load in loads[1:]:
        load.start()
    for i in range(2):
        sum_copy(i).start()
    rank_slots(count_ref, length_ref, perm_s, slen_s, slots)
    greet([cube.partner(bit) for bit in cube.bits])

    def rs(m, t, j, s):
        bit = cube.orders[j][s]
        half = message >> (s + 1)
        off = j * message + cube.offset(j, s, message) + (1 - cube.value(bit)) * half
        return pltpu.make_async_remote_copy(
            src_ref=part_v.at[t, pl.ds(aligned(off, 16), half)],
            dst_ref=landed[s].at[m],
            send_sem=rs_s.at[s, m],
            recv_sem=rs_r.at[s, m],
            device_id=cube.partner(bit),
            device_id_type=MESH,
        )

    def ag(m, t, j, s):
        bit = cube.orders[j][s]
        half = message >> (s + 1)
        off = j * message + cube.offset(j, s + 1, message)
        ref = full.at[t, pl.ds(aligned(off, 16), half)]
        return pltpu.make_async_remote_copy(
            src_ref=ref,
            dst_ref=ref,
            send_sem=ag_s.at[s, m],
            recv_sem=ag_r.at[s, m],
            device_id=cube.partner(bit),
            device_id_type=MESH,
        )

    def add(m, t, j, s):
        half = message >> (s + 1)
        place = pl.ds(aligned(j * message + cube.offset(j, s + 1, message), 16), half)
        sent = part_v[t, place, :].astype(F32) + landed[s][m].astype(F32)
        target = full if s == S - 1 else part_v
        target[t, place, :] = sent.astype(BF16)

    def out(t, j):
        place = pl.ds(j * message, message)
        return pltpu.make_async_copy(full.at[t, place], full_o.at[t, place], out_sem.at[t, j])

    def event(k, m, t, j):
        if k == 0:
            rs(m, t, j, 0).start()
        elif k <= S:
            rs(m, t, j, k - 1).wait()
            add(m, t, j, k - 1)
            (rs(m, t, j, k) if k < S else ag(m, t, j, S - 1)).start()
        elif k < 2 * S:
            s = 2 * S - k
            ag(m, t, j, s).wait()
            ag(m, t, j, s - 1).start()
        else:
            ag(m, t, j, 0).wait()
            out(t, j).start()

    when = [2]
    for lag in lags:
        when.append(when[-1] + lag)

    def events(tick, j):
        for k in reversed(range(2 * S + 1)):
            t = tick + (j - when[k]) // parts
            jj = (j - when[k]) % parts
            pl.when((t >= 0) & (t < ticks))(functools.partial(event, k, t * parts + jj, t, jj))

    bin_v[...] = jnp.zeros_like(bin_v)
    one_v[...] = jnp.zeros_like(one_v)
    gn_v[...] = jnp.zeros_like(gn_v)
    small_v[...] = jnp.zeros_like(small_v)
    loads[0].wait()
    gb_v[...] = gs_v[...].astype(BF16)

    def contract(left, right, dims):
        return lax.dot_general(left, right, ((dims, dims), ((), ())), preferred_element_type=F32)

    def pull(n, slot):
        wo_copy, dg_copy, _, _ = streams(n, slot)
        wo_copy.wait()
        dg_copy.wait()
        pulled = contract(gb_v[...], wo_v[slot], (1,)) * dg_v[slot].astype(F32)
        pulled = pulled.astype(BF16)
        gh_v[...] = pulled
        bin_v[n] = fold8(pulled.astype(F32))

    def weigh_out(n, slot, t, base):
        streams(n, slot)[2].wait()
        grad = contract(act_v[slot], gb_v[...], (0,)).astype(BF16)
        for i in range(features // LANES):
            part_v[t, pl.ds(base + 2 * features + i * WIDE, WIDE), :] = grad[:, i * LANES : (i + 1) * LANES]

    def weigh_in(n, slot, t, base):
        streams(n, slot)[3].wait()
        grad = contract(nrm_v[...], gh_v[...], (0,)).astype(BF16)
        for i in range(WIDE // LANES):
            part_v[t, pl.ds(base + i * features, features), :] = grad[:, i * LANES : (i + 1) * LANES]

        def spread(i, _):
            here = pl.ds(aligned(i * (slots // 2) * rows, rows), slots // 2 * rows)
            gn_v[here, :] = gn_v[here, :] + contract(gh_v[here, :], wi_v[slot], (1,))
            return 0

        lax.fori_loop(0, 2, spread, 0)

    def back_slot(slot, i):
        here = pl.ds(aligned(slot * rows, rows), rows)
        sum_copy(i).wait()
        hat, inverse = normalize(sum_v[i % 2])
        grad = gn_v[here, :]
        one_v[0:8, :] = one_v[0:8, :] + fold8(grad * hat)
        one_v[8:16, :] = one_v[8:16, :] + fold8(grad)
        grad = gs_v[here, :] + norm_back(grad * gain_one[...], hat, inverse)
        gs_v[here, :] = grad
        buf[slot, pl.ds(aligned(first, rows), rows), :] = grad.astype(BF16)
        pl.when(i + 2 < slots)(lambda: sum_copy(i + 2).start())

    def back_far(i, _):
        slot = far_slots - 1 - i
        back_slot(slot, i)
        exchange.start_own(slot, True)
        return 0

    def back_near(i, _):
        back_slot(far_slots + i, far_slots + i)
        exchange.start_own(far_slots + i, False)
        return 0

    def back_all():
        lax.fori_loop(0, far_slots, back_far, 0)
        lax.fori_loop(0, slots - far_slots, back_near, 0)

    def small_copy(s):
        return pltpu.make_async_remote_copy(
            src_ref=small_v.at[s],
            dst_ref=small_recv.at[s],
            send_sem=sm_s.at[s],
            recv_sem=sm_r.at[s],
            device_id=cube.partner(cube.bits[s]),
            device_id_type=MESH,
        )

    def small_start():
        row = 0
        vectors = [one_v[0:8, :], one_v[8:16, :]] + [bin_v[n] for n in range(chunks)]
        vectors += [part_ref[16:24, :], part_ref[0:8, :], part_ref[8:16, :]]
        for vector in vectors:
            vector = jnp.sum(vector, axis=0, keepdims=True)
            for i in range(vector.shape[1] // LANES):
                small_v[0, row : row + 1, :] = vector[:, i * LANES : (i + 1) * LANES]
                row += 1
        small_copy(0).start()

    def small_step(s):
        small_copy(s).wait()
        if s + 1 < S:
            small_v[s + 1] = small_v[s] + small_recv[s]
            small_copy(s + 1).start()
        else:
            small_o[...] = small_v[s] + small_recv[s]

    def grad_copy(g, i):
        return pltpu.make_async_copy(
            ig_v.at[i % 2], ig_o.at[pl.ds(aligned(g * group * rows, group * rows), group * rows)], ig_sem.at[i % 2]
        )

    def mixing(g, i):
        if i == 0:
            for load in loads[2:]:
                load.wait()
        if i >= 2:
            grad_copy(work[i - 2], i).wait()
        for k in range(group):
            far = g * group + k < far_slots
            exchange.wait_near(g * group + k, far)
            mix_slot(g * group + k, far, exchange, sc_v, buf, uv, k * rows)
        ig_v[i % 2] = jnp.dot(uv[...], hc_v[...], preferred_element_type=F32)

        def finish(k, _):
            slot = g * group + k
            here = pl.ds(aligned(slot * rows, rows), rows)
            local = pl.ds(aligned(k * rows, rows), rows)
            grad = gs_v[here, :] + ig_v[i % 2, local, :] * scale
            ig_v[i % 2, local, :] = jnp.where(live_rows(slen_s, slot, first, rows), grad, 0.0)
            return 0

        lax.fori_loop(0, group, finish, 0)
        grad_copy(g, i).start()

    count = slots // group
    near_groups = (slots - far_slots) // group
    work = list(range(count - near_groups, count)) + list(range(count - near_groups - 1, -1, -1))

    def forward_slots(g):
        for slot in range(g * group + group - 1, g * group - 1, -1):
            if slot < far_slots:
                exchange.forward(slot)

    tasks = {}

    def task(at, fn):
        tasks.setdefault(at, []).append(fn)

    task(ticks, back_all)
    task(ticks, small_start)
    for s in range(S):
        task(ticks + 1 + s, functools.partial(small_step, s))
    for i, g in enumerate(work):
        task(ticks + plan[i][0], functools.partial(forward_slots, g))
        task(ticks + plan[i][1], functools.partial(mixing, g, i))
    last = ticks + -(-(when[-1] + 1) // parts)
    last = max(last, max(tasks) + 1)

    def body(tick, _):
        def compute():
            for u in range(per_tick):
                n = tick * per_tick + u
                slot = lax.rem(n, 2)
                for copy in streams(n + 1, 1 - slot):
                    pl.when(n + 1 < chunks)(copy.start)
                base = u * (tick_rows // per_tick)
                pull(n, slot)
                if u == 0:
                    events(tick, 0)
                    pl.when(tick == 0)(loads[1].wait)
                weigh_in(n, slot, tick, base)
                if u == 0:
                    events(tick, 1)
                weigh_out(n, slot, tick, base)
            events(tick, 2)

        def drain():
            for j in range(parts):
                events(tick, j)
            for at, fns in sorted(tasks.items()):
                @pl.when(tick == at)
                def _():
                    for fn in fns:
                        fn()

        pl.when(tick < ticks)(compute)
        pl.when(tick >= ticks)(drain)
        return 0

    lax.fori_loop(0, last, body, 0)
    for slot in range(slots):
        exchange.wait_sends(slot, slot < far_slots)
    for i in range(max(0, count - 2), count):
        grad_copy(work[i], i).wait()

    def finish_out(t, _):
        for j in range(parts):
            out(t, j).wait()
        return 0

    lax.fori_loop(0, ticks, finish_out, 0)


def widen_kernel(full_ref, wi_ref, wo_ref):
    features = wi_ref.shape[0]
    for i in range(WIDE // LANES):
        wi_ref[:, i * LANES : (i + 1) * LANES] = full_ref[0, pl.ds(i * features, features), :].astype(F32)
    for i in range(features // LANES):
        start = 2 * features + i * WIDE
        wo_ref[:, i * LANES : (i + 1) * LANES] = full_ref[0, pl.ds(start, WIDE), :].astype(F32)


def restore_kernel(slots, count_ref, length_ref, lo_ref, ig_ref, lo_out, ig_out, perm_s, slen_s):
    rank_slots(count_ref, length_ref, perm_s, slen_s, slots)
    for j in range(slots):
        lo_out[:, perm_s[j], :] = lo_ref[j]
        ig_out[:, perm_s[j], :] = ig_ref[j]


LAGS = [3, 9, 6, 4, 3, 3, 4, 6, 9, 3]
ANY = pl.BlockSpec(memory_space=pl.ANY)
SMEM = pl.BlockSpec(memory_space=pltpu.SMEM)
VMEM = pl.BlockSpec(memory_space=pltpu.VMEM)
DMA = pltpu.SemaphoreType.DMA
PLAN = [(1, 3), (1, 4), (6, 8), (8, 10)]


def per_device(
    inputs, item_counts, lengths, gain_one, shift_one, weight_in, bias_in, weight_out, bias_out, gain_two, shift_two, cotangent
):
    rows, slots, features = inputs.shape
    wide = weight_in.shape[1]
    sizes = (lax.axis_size("dp"), lax.axis_size("seq"))
    devices = sizes[0] * sizes[1]
    seq_total = rows * sizes[1]
    flat = rows * slots
    far_slots, group = slots, 2
    chunks = wide // WIDE
    chunk_rows = 2 * features * WIDE // LANES
    per_tick = 1
    while chunks % per_tick or chunk_rows * per_tick % (devices * 16 * 3):
        per_tick += 1
    ticks = chunks // per_tick
    tick_rows = chunk_rows * per_tick
    message = tick_rows // 3

    seq_cos, seq_sin = dft_tables(seq_total)
    hid_cos, hid_sin = dft_tables(features)
    seq_table = np.concatenate([seq_cos.reshape(sizes[1], rows, seq_total), seq_sin.reshape(sizes[1], rows, seq_total)], axis=1)
    seq_table = jnp.asarray(seq_table.astype(jnp.bfloat16))
    hid_table = jnp.asarray(np.concatenate([hid_cos, -hid_sin], axis=0).astype(jnp.bfloat16))
    vec = lambda v: v.reshape(1, -1)
    shape = jax.ShapeDtypeStruct
    batch = group * rows

    act, dg, nrm, summed, second, lo, part = pl.pallas_call(
        functools.partial(forward_kernel, (sizes, far_slots, slots, group)),
        name="forward",
        out_shape=(
            shape((chunks, flat, WIDE), BF16),
            shape((chunks, flat, WIDE), BF16),
            shape((flat, features), BF16),
            shape((flat, features), F32),
            shape((flat, features), F32),
            shape((flat, features), F32),
            shape((24, features), F32),
        ),
        in_specs=[SMEM] * 2 + [VMEM] * 6 + [ANY] * 6,
        out_specs=[ANY] * 6 + [VMEM],
        scratch_shapes=[
            pltpu.SMEM((slots,), jnp.int32),
            pltpu.SMEM((slots,), jnp.int32),
            pltpu.VMEM((rows, slots, features), F32),
            pltpu.VMEM((rows, slots, features), F32),
            pltpu.VMEM((features, wide), BF16),
            pltpu.VMEM((wide, features), BF16),
            pltpu.VMEM((2 * rows, seq_total), BF16),
            pltpu.VMEM((2 * features, features), BF16),
            pltpu.VMEM((slots, seq_total, features), BF16),
            pltpu.VMEM((batch, 2 * features), BF16),
            pltpu.VMEM((flat, features), F32),
            pltpu.VMEM((flat, features), BF16),
            pltpu.VMEM((flat, wide), BF16),
            pltpu.VMEM((flat, wide), BF16),
            pltpu.VMEM((flat, features), F32),
            pltpu.VMEM((flat, features), F32),
            DMA((6,)),
            DMA((6,)),
            DMA((slots, sizes[1])),
            DMA((slots, sizes[1])),
        ],
        compiler_params=pltpu.CompilerParams(collective_id=1, has_side_effects=True, vmem_limit_bytes=62 << 20),
    )(
        item_counts, lengths, vec(gain_one), vec(shift_one), vec(bias_in), vec(bias_out), vec(gain_two), vec(shift_two),
        inputs, cotangent, weight_in, weight_out, seq_table, hid_table,
    )

    stages = (devices).bit_length() - 1
    lags = (LAGS[:stages] + [2] * stages)[:stages] + ([2] * stages + LAGS[-stages:])[-stages:]
    full, grad, small = pl.pallas_call(
        functools.partial(backward_kernel, (sizes, far_slots, slots, group, lags, PLAN)),
        name="backward",
        out_shape=(
            shape((ticks, tick_rows, LANES), BF16),
            shape((flat, features), F32),
            shape((64, LANES), F32),
        ),
        in_specs=[SMEM] * 2 + [VMEM] * 2 + [ANY] * 9,
        out_specs=[ANY] * 2 + [VMEM],
        scratch_shapes=[
            pltpu.SMEM((slots,), jnp.int32),
            pltpu.SMEM((slots,), jnp.int32),
            pltpu.VMEM((flat, features), F32),
            pltpu.VMEM((2, rows, features), F32),
            pltpu.VMEM((flat, features), BF16),
            pltpu.VMEM((flat, features), BF16),
            pltpu.VMEM((flat, WIDE), BF16),
            pltpu.VMEM((flat, features), F32),
            pltpu.VMEM((2, flat, WIDE), BF16),
            pltpu.VMEM((2, flat, WIDE), BF16),
            pltpu.VMEM((2, features, WIDE), BF16),
            pltpu.VMEM((2, WIDE, features), BF16),
            pltpu.VMEM((2 * rows, seq_total), BF16),
            pltpu.VMEM((2 * features, features), BF16),
            pltpu.VMEM((slots, seq_total, features), BF16),
            pltpu.VMEM((batch, 2 * features), BF16),
            pltpu.VMEM((2, batch, features), F32),
            pltpu.VMEM((chunks, 8, WIDE), F32),
            pltpu.VMEM((16, features), F32),
            pltpu.VMEM((stages, 64, LANES), F32),
            pltpu.VMEM((ticks, tick_rows, LANES), BF16),
            pltpu.VMEM((ticks, tick_rows, LANES), BF16),
        ]
        + [pltpu.VMEM((ticks * 3, message >> (s + 1), LANES), BF16) for s in range(stages)]
        + [
            pltpu.VMEM((stages, 64, LANES), F32),
            DMA((4,)),
            DMA((2,)),
            DMA((4, 2)),
            DMA((ticks, 3)),
            DMA((2,)),
            DMA((slots, sizes[1])),
            DMA((slots, sizes[1])),
            DMA((stages, ticks * 3)),
            DMA((stages, ticks * 3)),
            DMA((stages, ticks * 3)),
            DMA((stages, ticks * 3)),
            DMA((stages,)),
            DMA((stages,)),
        ],
        compiler_params=pltpu.CompilerParams(collective_id=2, has_side_effects=True, vmem_limit_bytes=62 << 20),
    )(
        item_counts, lengths, vec(gain_one), part, act, dg, nrm, summed, second, weight_in, weight_out, seq_table, hid_table,
    )

    wi_grad, wo_grad = pl.pallas_call(
        widen_kernel,
        name="widen",
        grid=(chunks,),
        out_shape=(shape((features, wide), F32), shape((wide, features), F32)),
        in_specs=[pl.BlockSpec((1, chunk_rows, LANES), lambda n: (n, 0, 0))],
        out_specs=(
            pl.BlockSpec((features, WIDE), lambda n: (0, n)),
            pl.BlockSpec((WIDE, features), lambda n: (n, 0)),
        ),
    )(full.reshape(chunks, chunk_rows, LANES))

    step = 16
    lo, grad = lo.reshape(slots, rows, features), grad.reshape(slots, rows, features)
    layer_out, input_grad = pl.pallas_call(
        functools.partial(restore_kernel, slots),
        name="restore",
        grid=(rows // step,),
        out_shape=(shape(inputs.shape, F32), shape(inputs.shape, F32)),
        in_specs=[SMEM] * 2 + [pl.BlockSpec((slots, step, features), lambda n: (0, n, 0))] * 2,
        out_specs=[pl.BlockSpec((step, slots, features), lambda n: (n, 0, 0))] * 2,
        scratch_shapes=[pltpu.SMEM((slots,), jnp.int32), pltpu.SMEM((slots,), jnp.int32)],
    )(item_counts, lengths, lo, grad)

    small = small.reshape(-1)
    cuts = [features, features, wide, features, features, features]
    vectors, start = [], 0
    for cut in cuts:
        vectors.append(small[start : start + cut])
        start += cut
    gain_one_grad, shift_one_grad, bias_in_grad, bias_out_grad, gain_two_grad, shift_two_grad = vectors
    return (
        layer_out, input_grad, gain_one_grad, shift_one_grad, wi_grad, bias_in_grad, wo_grad, bias_out_grad, gain_two_grad, shift_two_grad,
    )


def solution(mesh):
    placed = (
        P("seq", "dp", None), P("dp"), P("dp"), P(), P(), P(), P(), P(), P(), P(), P(), P("seq", "dp", None),
    )
    wide = P("seq", "dp", None)
    return jax.shard_map(
        per_device,
        mesh=mesh,
        in_specs=placed,
        out_specs=(wide, wide, P(), P(), P(), P(), P(), P(), P(), P()),
        check_vma=False,
    )
```

```python
import functools
import math

import jax
import jax.numpy as jnp
import numpy as np
from jax import lax
from jax.experimental import pallas as pl
from jax.experimental.pallas import tpu as pltpu
from jax.sharding import PartitionSpec as P

EPSILON = 1e-05
MESH = pl.DeviceIdType.MESH
LANES = 128
WIDE = 512
BF16 = jnp.bfloat16
F32 = jnp.float32


def dft_tables(count):
    index = np.arange(count, dtype=np.int64)
    turns = (index[:, None] * index[None, :] % count).astype(np.float32)
    angle = (turns * np.float32(2.0 * math.pi / count)).astype(np.float64)
    return np.cos(angle).astype(np.float32), np.sin(angle).astype(np.float32)


def aligned(value, step):
    return pl.multiple_of(value, step)


def bit_of(value, k):
    return (value // k) % 2


def flipped(value, k):
    return value + k * (1 - 2 * bit_of(value, k))


def axis_bits(axis, size):
    return [(axis, 1 << b) for b in range(size.bit_length() - 1)]


class Cube:
    def __init__(self, sizes, mids):
        dp, seq = sizes
        bits = axis_bits(1, seq) + axis_bits(0, dp)
        first, near, rest = bits[:1], bits[1:4], bits[4:]
        self.orders = [first + [near[i] for i in mid] + rest for mid in mids]
        self.bits = bits
        self.stages = len(bits)
        self.me = (lax.axis_index("dp"), lax.axis_index("seq"))
        self.values = {bit: self.value(bit) for bit in bits}
        self.partners = {bit: self.partner(bit) for bit in bits}

    def value(self, bit):
        return bit_of(self.me[bit[0]], bit[1])

    def partner(self, bit):
        axis, k = bit
        other = flipped(self.me[axis], k)
        return (other, self.me[1]) if axis == 0 else (self.me[0], other)

    def offset(self, order, level, rows):
        total = 0
        for s in range(level):
            total = total + self.values[self.orders[order][s]] * (rows >> (s + 1))
        return total


class Exchange:
    def __init__(self, size, rows, buf, send, recv):
        self.size, self.rows, self.buf, self.send_sem, self.recv_sem = size, rows, buf, send, recv
        self.dp, self.q = lax.axis_index("dp"), lax.axis_index("seq")
        self.order = [1 << b for b in reversed(range(size.bit_length() - 1))]

    def owner(self, pattern):
        index = self.q
        for k in self.order:
            if pattern & k:
                index = flipped(index, k)
        return index

    def copy(self, slot, pattern):
        hop = pattern & -pattern
        place = pl.ds(aligned(self.owner(pattern - hop) * self.rows, self.rows), self.rows)
        ref = self.buf.at[slot, place]
        return pltpu.make_async_remote_copy(
            src_ref=ref,
            dst_ref=ref,
            send_sem=self.send_sem.at[slot, pattern],
            recv_sem=self.recv_sem.at[slot, pattern],
            device_id=(self.dp, flipped(self.q, hop)),
            device_id_type=MESH,
        )

    def patterns(self, far):
        return range(1, self.size) if far else range(1, 2)

    def start_own(self, slot, far):
        for pattern in self.patterns(far):
            if pattern & (pattern - 1) == 0:
                self.copy(slot, pattern).start()

    def forward(self, slot):
        for pattern in self.patterns(True):
            if pattern & 1 == 0:
                self.copy(slot, pattern).wait_recv()
                for k in self.order:
                    if k < (pattern & -pattern):
                        self.copy(slot, pattern | k).start()

    def wait_near(self, slot, far):
        for pattern in self.patterns(far):
            if pattern & 1:
                self.copy(slot, pattern).wait_recv()

    def wait_sends(self, slot, far):
        for pattern in self.patterns(far):
            self.copy(slot, pattern).wait_send()


def greet(partners):
    barrier = pltpu.get_barrier_semaphore()
    for partner in partners:
        pl.semaphore_signal(barrier, inc=1, device_id=partner, device_id_type=MESH)
    pl.semaphore_wait(barrier, len(partners))


def rank_slots(count_ref, length_ref, perm_s, slen_s, slots):
    count = count_ref[0]
    live = [jnp.where(i < count, length_ref[i], 0) for i in range(slots)]
    ranks = []
    for i in range(slots):
        rank = 0
        for k in range(slots):
            if k != i:
                ahead = live[k] >= live[i] if k < i else live[k] > live[i]
                rank = rank + jnp.where(ahead, 1, 0)
        ranks.append(rank)
    for j in range(slots):
        perm, length = 0, 0
        for i in range(slots):
            here = ranks[i] == j
            perm = perm + jnp.where(here, i, 0)
            length = length + jnp.where(here, live[i], 0)
        perm_s[j] = perm
        slen_s[j] = length


def live_rows(slen_s, slot, first, rows):
    position = first + lax.broadcasted_iota(jnp.int32, (rows, 1), 0)
    return position < slen_s[slot]


def fold8(values):
    rows, lanes = values.shape
    return values.reshape(rows // 8, 8, lanes).sum(axis=0)


def normalize(values):
    center = values - jnp.mean(values, axis=-1, keepdims=True)
    spread = jnp.mean(center * center, axis=-1, keepdims=True)
    inverse = lax.rsqrt(spread + EPSILON)
    return center * inverse, inverse


def norm_back(grad_hat, normal, inverse):
    first = jnp.mean(grad_hat, axis=-1, keepdims=True)
    second = jnp.mean(grad_hat * normal, axis=-1, keepdims=True)
    return inverse * (grad_hat - first - normal * second)


def mix_slot(slot, far, exchange, tables, buf, uv, place):
    rows = exchange.rows
    if far:
        table, block = tables[...], buf[slot]
    else:
        base = aligned(exchange.q // 2 * (2 * rows), 2 * rows)
        table, block = tables[:, pl.ds(base, 2 * rows)], buf[slot, pl.ds(base, 2 * rows), :]
    both = jnp.dot(table, block, preferred_element_type=F32).astype(BF16)
    width = both.shape[1]
    uv[pl.ds(place, rows), :width] = both[:rows]
    uv[pl.ds(place, rows), width:] = both[rows:]


def group_at(i, near_groups, count):
    if near_groups == 0:
        return count - 1 - i
    return jnp.where(i < near_groups, count - near_groups + i, count - 1 - i)


def forward_kernel(cfg, *refs):
    sizes, far_slots, slots, group = cfg
    (
        count_ref, length_ref, vec_ref, x_hbm, cot_hbm, wi_hbm, wo_hbm, sc_hbm, hc_hbm,
        act_o, dg_o, nrm_o, sum_o, gs_o, gb_o, lo_o, part_o,
        perm_s, slen_s, x_v, cot_v, wi_v, wo_v, sc_v, hc_v, buf, uv, sum_v, nrm_v, act_v, dg_v, gs_v, gb_v, lo_v, br_v,
        load_sem, out_sem, send_sem, recv_sem,
    ) = refs
    rows, _, features = x_v.shape
    wide = wi_v.shape[1]
    seq_total = rows * sizes[1]
    scale = 1.0 / math.sqrt(features * seq_total)
    exchange = Exchange(sizes[1], rows, buf, send_sem, recv_sem)
    q = exchange.q
    first = q * rows
    gain_one, shift_one, bias_out, gain_two, shift_two = (lambda i=i: vec_ref[i : i + 1, :] for i in range(5))
    loads = [
        pltpu.make_async_copy(x_hbm, x_v, load_sem.at[0]),
        pltpu.make_async_copy(sc_hbm.at[q], sc_v, load_sem.at[1]),
        pltpu.make_async_copy(hc_hbm, hc_v, load_sem.at[2]),
        pltpu.make_async_copy(wi_hbm, wi_v, load_sem.at[3]),
        pltpu.make_async_copy(wo_hbm, wo_v, load_sem.at[4]),
        pltpu.make_async_copy(cot_hbm, cot_v, load_sem.at[5]),
    ]
    loads[0].start()
    rank_slots(count_ref, length_ref, perm_s, slen_s, slots)
    greet([(exchange.dp, flipped(q, k)) for k in exchange.order])
    loads[0].wait()
    for load in loads[1:]:
        load.start()

    def prepare(i, _):
        slot = jnp.where(i < far_slots, far_slots - 1 - i, i) if far_slots < slots else slots - 1 - i
        value = jnp.where(live_rows(slen_s, slot, first, rows), x_v[:, perm_s[slot], :], 0.0)
        sum_v[pl.ds(aligned(slot * rows, rows), rows), :] = value
        buf[slot, pl.ds(aligned(first, rows), rows), :] = value.astype(BF16)
        pl.when(i < far_slots)(lambda: exchange.start_own(slot, True))
        if far_slots < slots:
            pl.when(i >= far_slots)(lambda: exchange.start_own(slot, False))
        return 0

    lax.fori_loop(0, slots, prepare, 0)
    part_o[...] = jnp.zeros_like(part_o)
    for load in loads[1:3]:
        load.wait()

    batch = group * rows
    span = features
    count = slots // group
    near_groups = (slots - far_slots) // group

    def outs(base):
        place = pl.ds(base, batch)
        copies = [
            pltpu.make_async_copy(nrm_v.at[place], nrm_o.at[place], out_sem.at[0]),
            pltpu.make_async_copy(sum_v.at[place], sum_o.at[place], out_sem.at[1]),
            pltpu.make_async_copy(gs_v.at[place], gs_o.at[place], out_sem.at[2]),
            pltpu.make_async_copy(lo_v.at[place], lo_o.at[place], out_sem.at[3]),
            pltpu.make_async_copy(gb_v.at[place], gb_o.at[place], out_sem.at[6]),
        ]
        for n in range(wide // WIDE):
            cut = pl.ds(n * WIDE, WIDE)
            copies.append(pltpu.make_async_copy(act_v.at[place, cut], act_o.at[n, place], out_sem.at[4]))
            copies.append(pltpu.make_async_copy(dg_v.at[place, cut], dg_o.at[n, place], out_sem.at[5]))
        return copies

    def bring(slot0):
        for k in reversed(range(group)):
            exchange.forward(slot0 + k)

    def mixing(slot0, far):
        for k in reversed(range(group)):
            exchange.wait_near(slot0 + k, far)
            mix_slot(slot0 + k, far, exchange, sc_v, buf, uv, k * rows)

    def work(i, _):
        slot0 = group_at(i, near_groups, count) * group
        base = aligned(slot0 * rows, batch)
        place = pl.ds(base, batch)
        if near_groups < count:
            pl.when(i >= near_groups)(lambda: mixing(slot0, True))
        if near_groups > 0:
            pl.when(i < near_groups)(lambda: mixing(slot0, False))
        mixed = jnp.dot(uv[...], hc_v[...], preferred_element_type=F32)
        sum_v[place, :] = sum_v[place, :] + (mixed * scale).astype(BF16).astype(F32)

        def norm_one(k, _):
            here = pl.ds(aligned(base + k * rows, rows), rows)
            hat, _ = normalize(sum_v[here, :])
            nrm_v[here, :] = (hat * gain_one() + shift_one()).astype(BF16)
            return 0

        lax.fori_loop(0, group, norm_one, 0)

        @pl.when(i == 0)
        def _():
            for load in loads[3:]:
                load.wait()

        def expand(n, _):
            cut = pl.ds(aligned(n * span, span), span)
            hidden = jnp.dot(nrm_v[place, :], wi_v[:, cut], preferred_element_type=F32) + vec_ref[pl.ds(5 + n, 1), :]
            gate = 0.5 + 0.5 * lax.erf(hidden * math.sqrt(0.5))
            slope = gate + hidden * (jnp.exp(hidden * hidden * -0.5) * (1.0 / math.sqrt(2.0 * math.pi)))
            act_v[place, cut] = (hidden * gate).astype(BF16)
            dg_v[place, cut] = slope.astype(BF16)
            return 0

        lax.fori_loop(0, wide // span, expand, 0)
        br_v[...] = jnp.dot(act_v[place, :], wo_v[...], preferred_element_type=F32)

        def norm_two(k, _):
            here = pl.ds(aligned(base + k * rows, rows), rows)
            local = pl.ds(aligned(k * rows, rows), rows)
            slot = slot0 + k
            live = live_rows(slen_s, slot, first, rows)
            hat, inverse = normalize(sum_v[here, :] + (br_v[local, :] + bias_out()))
            grad = jnp.where(live, cot_v[:, perm_s[slot], :], 0.0)
            lo_v[here, :] = jnp.where(live, hat * gain_two() + shift_two(), 0.0)
            part_o[0:8, :] = part_o[0:8, :] + fold8(grad * hat)
            part_o[8:16, :] = part_o[8:16, :] + fold8(grad)
            second = norm_back(grad * gain_two(), hat, inverse)
            low = second.astype(BF16)
            gs_v[here, :] = second
            gb_v[here, :] = low
            part_o[16:24, :] = part_o[16:24, :] + fold8(low.astype(F32))
            return 0

        lax.fori_loop(0, group, norm_two, 0)
        for copy in outs(base):
            copy.start()
        if near_groups < count:

            @pl.when((i + 1 >= near_groups) & (i + 1 < count))
            def _():
                bring(group_at(i + 1, near_groups, count) * group)

        return 0

    if near_groups == 0:
        bring((count - 1) * group)
    lax.fori_loop(0, count, work, 0)

    def finish(slot, _):
        pl.when(slot < far_slots)(lambda: exchange.wait_sends(slot, True))
        if far_slots < slots:
            pl.when(slot >= far_slots)(lambda: exchange.wait_sends(slot, False))
        return 0

    lax.fori_loop(0, slots, finish, 0)

    def flush(g, _):
        for copy in outs(aligned(g * batch, batch)):
            copy.wait()
        return 0

    lax.fori_loop(0, count, flush, 0)


def backward_kernel(cfg, *refs):
    sizes, far_slots, slots, group, parts, mids, lags, plan = cfg
    cube = Cube(sizes, mids)
    S = cube.stages
    (
        count_ref, length_ref, vec_ref, part_ref,
        act_hbm, dg_hbm, nrm_hbm, sum_hbm, gs_hbm, gb_hbm, wi_hbm, wo_hbm, sc_hbm, hc_hbm,
        full_o, ig_o, small_o,
        perm_s, slen_s, gs_v, sum_v, nrm_v, gb_v, gh_v, gn_v, act_v, dg_v, wi_v, wo_v, sc_v, hc_v, buf, uv, ig_v,
        bin_v, one_v, small_v, part_v, full,
    ) = refs[:39]
    landed = refs[39 : 39 + S]
    (
        small_recv, load_sem, sum_sem, stream_sem, out_sem, ig_sem, send_sem, recv_sem,
        rs_s, rs_r, ag_s, ag_r, sm_s, sm_r,
    ) = refs[39 + S :]
    ticks, tick_rows, _ = part_v.shape
    message = tick_rows // parts
    chunks = act_hbm.shape[0]
    per_tick = chunks // ticks
    features = nrm_v.shape[1]
    rows = gs_v.shape[0] // slots
    batch = group * rows
    scale = 1.0 / math.sqrt(features * rows * sizes[1])
    exchange = Exchange(sizes[1], rows, buf, send_sem, recv_sem)
    q = exchange.q
    first = q * rows
    loads = [
        pltpu.make_async_copy(gb_hbm, gb_v, load_sem.at[0]),
        pltpu.make_async_copy(nrm_hbm, nrm_v, load_sem.at[1]),
        pltpu.make_async_copy(gs_hbm, gs_v, load_sem.at[2]),
        pltpu.make_async_copy(sc_hbm.at[q], sc_v, load_sem.at[3]),
        pltpu.make_async_copy(hc_hbm, hc_v, load_sem.at[4]),
    ]

    def turn(i):
        return jnp.where(i < far_slots, far_slots - 1 - i, i) if far_slots < slots else slots - 1 - i

    def sum_copy(i):
        place = pl.ds(aligned(turn(i) * rows, rows), rows)
        return pltpu.make_async_copy(sum_hbm.at[place], sum_v.at[lax.rem(i, 2)], sum_sem.at[lax.rem(i, 2)])

    def streams(n, slot):
        cut = pl.ds(aligned(n * WIDE, WIDE), WIDE)
        return [
            pltpu.make_async_copy(act_hbm.at[n], act_v.at[slot], stream_sem.at[0, slot]),
            pltpu.make_async_copy(wo_hbm.at[cut], wo_v.at[slot], stream_sem.at[1, slot]),
            pltpu.make_async_copy(dg_hbm.at[n], dg_v.at[slot], stream_sem.at[2, slot]),
            pltpu.make_async_copy(wi_hbm.at[:, cut], wi_v.at[slot], stream_sem.at[3, slot]),
        ]

    loads[0].start()
    for copy in streams(0, 0):
        copy.start()
    for load in loads[1:]:
        load.start()
    for i in range(2):
        sum_copy(i).start()
    rank_slots(count_ref, length_ref, perm_s, slen_s, slots)
    greet([cube.partner(bit) for bit in cube.bits])

    starts = [[j * message + cube.offset(j, level, message) for level in range(S + 1)] for j in range(parts)]

    def rs(m, t, j, s):
        bit = cube.orders[j][s]
        half = message >> (s + 1)
        off = starts[j][s] + (1 - cube.values[bit]) * half
        return pltpu.make_async_remote_copy(
            src_ref=part_v.at[t, pl.ds(aligned(off, 16), half)],
            dst_ref=landed[s].at[m],
            send_sem=rs_s.at[s],
            recv_sem=rs_r.at[s, m],
            device_id=cube.partners[bit],
            device_id_type=MESH,
        )

    def ag(m, t, j, s):
        bit = cube.orders[j][s]
        half = message >> (s + 1)
        ref = full.at[t, pl.ds(aligned(starts[j][s + 1], 16), half)]
        return pltpu.make_async_remote_copy(
            src_ref=ref,
            dst_ref=ref,
            send_sem=ag_s.at[s],
            recv_sem=ag_r.at[s, m],
            device_id=cube.partners[bit],
            device_id_type=MESH,
        )

    def add(m, t, j, s):
        half = message >> (s + 1)
        place = pl.ds(aligned(starts[j][s + 1], 16), half)
        total = part_v[t, place, :].astype(F32) + landed[s][m].astype(F32)
        target = full if s == S - 1 else part_v
        target[t, place, :] = total.astype(BF16)

    def out(t, j):
        place = pl.ds(j * message, message)
        return pltpu.make_async_copy(full.at[t, place], full_o.at[t, place], out_sem.at[t, j])

    def event(k, m, t, j):
        if k == 0:
            rs(m, t, j, 0).start()
        elif k <= S:
            rs(m, t, j, k - 1).wait_recv()
            add(m, t, j, k - 1)
            (rs(m, t, j, k) if k < S else ag(m, t, j, S - 1)).start()
        elif k < 2 * S:
            s = 2 * S - k
            ag(m, t, j, s).wait_recv()
            ag(m, t, j, s - 1).start()
        else:
            ag(m, t, j, 0).wait_recv()
            out(t, j).start()

    def sends_done():
        for s in range(S):
            for sem in (rs_s.at[s], ag_s.at[s]):
                pltpu.make_async_copy(landed[s], landed[s], sem).wait()

    when = [0 if per_tick == 1 and parts == 4 else parts]
    for lag in lags:
        when.append(when[-1] + lag)

    def events(tick, j):
        for k in reversed(range(2 * S + 1)):
            t = tick + (j - when[k]) // parts
            jj = (j - when[k]) % parts
            pl.when((t >= 0) & (t < ticks))(functools.partial(event, k, t * parts + jj, t, jj))

    bin_v[...] = jnp.zeros_like(bin_v)
    one_v[...] = jnp.zeros_like(one_v)
    gn_v[...] = jnp.zeros_like(gn_v)
    small_v[...] = jnp.zeros_like(small_v)
    loads[0].wait()

    def contract(left, right, dims):
        return lax.dot_general(left, right, ((dims, dims), ((), ())), preferred_element_type=F32)

    def weigh_out(n, slot, t, base):
        streams(n, slot)[0].wait()
        grad = contract(act_v[slot], gb_v[...], (0,)).astype(BF16)
        for i in range(features // LANES):
            part_v[t, pl.ds(base + i * WIDE, WIDE), :] = grad[:, i * LANES : (i + 1) * LANES]

    def pull(n, slot, t, base):
        streams(n, slot)[1].wait()
        streams(n, slot)[2].wait()
        pulled = contract(gb_v[...], wo_v[slot], (1,)) * dg_v[slot].astype(F32)
        pulled = pulled.astype(BF16)
        gh_v[...] = pulled
        bin_v[n] = fold8(pulled.astype(F32))

    def weigh_in(n, slot, t, base):
        pl.when(n == 0)(loads[1].wait)
        grad = contract(nrm_v[...], gh_v[...], (0,)).astype(BF16)
        for i in range(WIDE // LANES):
            place = pl.ds(base + features // LANES * WIDE + i * features, features)
            part_v[t, place, :] = grad[:, i * LANES : (i + 1) * LANES]

    def spread(n, slot, t, base):
        streams(n, slot)[3].wait()
        for i in range(2):
            here = pl.ds(i * (slots // 2) * rows, slots // 2 * rows)
            gn_v[here, :] = gn_v[here, :] + contract(gh_v[here, :], wi_v[slot], (1,))

    steps = [weigh_out, pull, weigh_in, spread]

    def compute(tick, j):
        if per_tick == 1 and parts == 4:
            slot = lax.rem(tick, 2)
            if j == 0:
                for copy in streams(tick + 1, 1 - slot):
                    pl.when(tick + 1 < chunks)(copy.start)
            steps[j](tick, slot, tick, 0)
        elif j == 0:

            def whole(u, _):
                n = tick * per_tick + u
                slot = lax.rem(n, 2)
                for copy in streams(n + 1, 1 - slot):
                    pl.when(n + 1 < chunks)(copy.start)
                for step in steps:
                    step(n, slot, tick, aligned(u * (tick_rows // per_tick), LANES))
                return 0

            lax.fori_loop(0, per_tick, whole, 0)

    def back(i, _):
        slot = turn(i)
        here = pl.ds(aligned(slot * rows, rows), rows)
        pl.when(i == 0)(loads[2].wait)
        sum_copy(i).wait()
        hat, inverse = normalize(sum_v[lax.rem(i, 2)])
        grad = gn_v[here, :]
        one_v[0:8, :] = one_v[0:8, :] + fold8(grad * hat)
        one_v[8:16, :] = one_v[8:16, :] + fold8(grad)
        grad = gs_v[here, :] + norm_back(grad * vec_ref[0:1, :], hat, inverse)
        gs_v[here, :] = grad
        buf[slot, pl.ds(aligned(first, rows), rows), :] = grad.astype(BF16)
        pl.when(i < far_slots)(lambda: exchange.start_own(slot, True))
        if far_slots < slots:
            pl.when(i >= far_slots)(lambda: exchange.start_own(slot, False))
        pl.when(i + 2 < slots)(lambda: sum_copy(i + 2).start())
        return 0

    def small_copy(s):
        return pltpu.make_async_remote_copy(
            src_ref=small_v.at[s],
            dst_ref=small_recv.at[s],
            send_sem=sm_s.at[s],
            recv_sem=sm_r.at[s],
            device_id=cube.partners[cube.bits[s]],
            device_id_type=MESH,
        )

    def small_start():
        row = 0
        vectors = [one_v[0:8, :], one_v[8:16, :]] + [bin_v[n] for n in range(chunks)]
        vectors += [part_ref[16:24, :], part_ref[0:8, :], part_ref[8:16, :]]
        for vector in vectors:
            vector = jnp.sum(vector, axis=0, keepdims=True)
            for i in range(vector.shape[1] // LANES):
                small_v[0, row : row + 1, :] = vector[:, i * LANES : (i + 1) * LANES]
                row += 1
        small_copy(0).start()

    def small_step(s):
        small_copy(s).wait()
        if s + 1 < S:
            small_v[s + 1] = small_v[s] + small_recv[s]
            small_copy(s + 1).start()
        else:
            small_o[...] = small_v[s] + small_recv[s]

    count = slots // group
    near_groups = (slots - far_slots) // group

    def grad_copy(i):
        base = aligned(group_at(i, near_groups, count) * batch, batch)
        return pltpu.make_async_copy(ig_v.at[lax.rem(i, 2)], ig_o.at[pl.ds(base, batch)], ig_sem.at[lax.rem(i, 2)])

    def mixing(i, k, far):
        slot = group_at(i, near_groups, count) * group + k
        exchange.wait_near(slot, far)
        mix_slot(slot, far, exchange, sc_v, buf, uv, k * rows)

    def hidden_mix(i):
        pl.when(i >= 2)(lambda: grad_copy(i - 2).wait())
        ig_v[lax.rem(i, 2)] = jnp.dot(uv[...], hc_v[...], preferred_element_type=F32)

    def finish(i):
        for k in range(group):
            slot = group_at(i, near_groups, count) * group + k
            here = pl.ds(aligned(slot * rows, rows), rows)
            local = pl.ds(k * rows, rows)
            grad = gs_v[here, :] + ig_v[lax.rem(i, 2), local, :] * scale
            ig_v[lax.rem(i, 2), local, :] = jnp.where(live_rows(slen_s, slot, first, rows), grad, 0.0)
        grad_copy(i).start()

    def bring(i):
        for k in reversed(range(group)):
            exchange.forward(group_at(i, near_groups, count) * group + k)

    small_at, near_at, far_at, lead = plan

    def drain(tick, j):
        d = tick - ticks

        @pl.when(d == 0)
        def _():
            share = -(-slots // parts)
            lax.fori_loop(min(j * share, slots), min((j + 1) * share, slots), back, 0)

        here = lambda at: pl.when(d * parts + j == at)
        if j == small_at % parts:
            here(small_at)(small_start)
        for s in range(S):
            at = small_at + 3 * (s + 1)
            if j == at % parts:
                here(at)(functools.partial(small_step, s))
        if j == 0:

            @pl.when(d == 1)
            def _():
                for load in loads[3:]:
                    load.wait()

        for far, start, low, high in ((False, near_at, 0, near_groups), (True, far_at, near_groups, count)):
            if low == high:
                continue
            i = d - start + low

            @pl.when((i >= low) & (i < high))
            def _():
                subs = [
                    lambda: mixing(i, 0, far),
                    lambda: [mixing(i, k, far) for k in range(1, group)],
                    lambda: hidden_mix(i),
                    lambda: finish(i),
                ]
                for at, sub in enumerate(subs):
                    if min(at, parts - 1) == j:
                        sub()

            if far and j == parts - 1:
                ahead = i + lead
                pl.when((ahead >= low) & (ahead < high))(lambda: bring(ahead))

    last = ticks + max(
        -(-(when[-1] + 1) // parts),
        (small_at + 3 * S) // parts + 1,
        near_at + near_groups,
        far_at + count - near_groups,
    )

    def body(tick, _):
        for j in range(parts):
            pl.when(tick < ticks)(lambda: compute(tick, j))
            events(tick, j)
            pl.when(tick >= ticks)(lambda: drain(tick, j))
        return 0

    lax.fori_loop(0, last, body, 0)

    def settle(slot, _):
        pl.when(slot < far_slots)(lambda: exchange.wait_sends(slot, True))
        if far_slots < slots:
            pl.when(slot >= far_slots)(lambda: exchange.wait_sends(slot, False))
        return 0

    lax.fori_loop(0, slots, settle, 0)
    for i in range(max(0, count - 2), count):
        grad_copy(i).wait()

    def finish_out(t, _):
        for j in range(parts):
            out(t, j).wait()
        return 0

    lax.fori_loop(0, ticks, finish_out, 0)
    sends_done()


def widen_kernel(full_ref, wi_ref, wo_ref):
    features = wi_ref.shape[0]
    for u in range(full_ref.shape[0]):
        for i in range(features // LANES):
            place = slice(u * WIDE, (u + 1) * WIDE)
            wo_ref[place, i * LANES : (i + 1) * LANES] = full_ref[u, pl.ds(i * WIDE, WIDE), :].astype(F32)
        for i in range(WIDE // LANES):
            start = features // LANES * WIDE + i * features
            place = slice(u * WIDE + i * LANES, u * WIDE + (i + 1) * LANES)
            wi_ref[:, place] = full_ref[u, pl.ds(start, features), :].astype(F32)


def restore_kernel(slots, count_ref, length_ref, lo_ref, ig_ref, lo_out, ig_out, perm_s, slen_s):
    rank_slots(count_ref, length_ref, perm_s, slen_s, slots)
    for j in range(slots):
        lo_out[:, perm_s[j], :] = lo_ref[j]
        ig_out[:, perm_s[j], :] = ig_ref[j]


ANY = pl.BlockSpec(memory_space=pl.ANY)
SMEM = pl.BlockSpec(memory_space=pltpu.SMEM)
VMEM = pl.BlockSpec(memory_space=pltpu.VMEM)
DMA = pltpu.SemaphoreType.DMA
LAGS = [4, 4, 4, 4, 4, 4, 4, 4, 4, 4]
PLAN = (4, 1, 4, 1)
FAR_PLAN = (4, 1, 4, 1)
MIDS = ((0, 1, 2), (1, 0, 2), (2, 0, 1), (1, 2, 0))
FAR_MIDS = ((1, 2, 0), (2, 1, 0), (1, 0, 2), (2, 0, 1))


def run_forward(sizes, far_slots, slots, *operands, group=2, name="forward", cid=1):
    rows, _, features = operands[3].shape
    wide = operands[5].shape[1]
    seq_total = rows * sizes[1]
    flat, batch, chunks = rows * slots, group * rows, wide // WIDE
    shape = jax.ShapeDtypeStruct
    return pl.pallas_call(
        functools.partial(forward_kernel, (sizes, far_slots, slots, group)),
        name=name,
        out_shape=(
            shape((chunks, flat, WIDE), BF16),
            shape((chunks, flat, WIDE), BF16),
            shape((flat, features), BF16),
            shape((flat, features), F32),
            shape((flat, features), F32),
            shape((flat, features), BF16),
            shape((flat, features), F32),
            shape((24, features), F32),
        ),
        in_specs=[SMEM] * 2 + [VMEM] + [ANY] * 6,
        out_specs=[ANY] * 7 + [VMEM],
        scratch_shapes=[
            pltpu.SMEM((slots,), jnp.int32),
            pltpu.SMEM((slots,), jnp.int32),
            pltpu.VMEM((rows, slots, features), F32),
            pltpu.VMEM((rows, slots, features), F32),
            pltpu.VMEM((features, wide), BF16),
            pltpu.VMEM((wide, features), BF16),
            pltpu.VMEM((2 * rows, seq_total), BF16),
            pltpu.VMEM((2 * features, features), BF16),
            pltpu.VMEM((slots, seq_total, features), BF16),
            pltpu.VMEM((batch, 2 * features), BF16),
            pltpu.VMEM((flat, features), F32),
            pltpu.VMEM((flat, features), BF16),
            pltpu.VMEM((flat, wide), BF16),
            pltpu.VMEM((flat, wide), BF16),
            pltpu.VMEM((flat, features), F32),
            pltpu.VMEM((flat, features), BF16),
            pltpu.VMEM((flat, features), F32),
            pltpu.VMEM((batch, features), F32),
            DMA((6,)),
            DMA((7,)),
            DMA((slots, sizes[1])),
            DMA((slots, sizes[1])),
        ],
        compiler_params=pltpu.CompilerParams(collective_id=cid, has_side_effects=True, vmem_limit_bytes=62 << 20),
    )(*operands)


def run_backward(sizes, far_slots, slots, ticks, tick_rows, parts, *operands, group=2, mids=None, lags=None, plan=None, name="backward", cid=2):
    devices = sizes[0] * sizes[1]
    chunks, flat, _ = operands[4].shape
    features, wide = operands[10].shape
    rows = flat // slots
    seq_total = rows * sizes[1]
    batch = group * rows
    message = tick_rows // parts
    shape = jax.ShapeDtypeStruct
    mostly_far = far_slots > slots * 5 // 8
    mids = mids or (FAR_MIDS if mostly_far else MIDS)
    plan = plan or (FAR_PLAN if mostly_far else PLAN)
    lags = lags or LAGS
    stages = devices.bit_length() - 1
    lags = (lags[:stages] + [2] * stages)[:stages] + ([2] * stages + lags[-stages:])[-stages:]
    return pl.pallas_call(
        functools.partial(backward_kernel, (sizes, far_slots, slots, group, parts, mids, lags, plan)),
        name=name,
        out_shape=(
            shape((ticks, tick_rows, LANES), BF16),
            shape((flat, features), F32),
            shape((64, LANES), F32),
        ),
        in_specs=[SMEM] * 2 + [VMEM] * 2 + [ANY] * 10,
        out_specs=[ANY] * 2 + [VMEM],
        scratch_shapes=[
            pltpu.SMEM((slots,), jnp.int32),
            pltpu.SMEM((slots,), jnp.int32),
            pltpu.VMEM((flat, features), F32),
            pltpu.VMEM((2, rows, features), F32),
            pltpu.VMEM((flat, features), BF16),
            pltpu.VMEM((flat, features), BF16),
            pltpu.VMEM((flat, WIDE), BF16),
            pltpu.VMEM((flat, features), F32),
            pltpu.VMEM((2, flat, WIDE), BF16),
            pltpu.VMEM((2, flat, WIDE), BF16),
            pltpu.VMEM((2, features, WIDE), BF16),
            pltpu.VMEM((2, WIDE, features), BF16),
            pltpu.VMEM((2 * rows, seq_total), BF16),
            pltpu.VMEM((2 * features, features), BF16),
            pltpu.VMEM((slots, seq_total, features), BF16),
            pltpu.VMEM((batch, 2 * features), BF16),
            pltpu.VMEM((2, batch, features), F32),
            pltpu.VMEM((chunks, 8, WIDE), F32),
            pltpu.VMEM((16, features), F32),
            pltpu.VMEM((stages, 64, LANES), F32),
            pltpu.VMEM((ticks, tick_rows, LANES), BF16),
            pltpu.VMEM((ticks, tick_rows, LANES), BF16),
        ]
        + [pltpu.VMEM((ticks * parts, message >> (s + 1), LANES), BF16) for s in range(stages)]
        + [
            pltpu.VMEM((stages, 64, LANES), F32),
            DMA((5,)),
            DMA((2,)),
            DMA((4, 2)),
            DMA((ticks, parts)),
            DMA((2,)),
            DMA((slots, sizes[1])),
            DMA((slots, sizes[1])),
            DMA((stages,)),
            DMA((stages, ticks * parts)),
            DMA((stages,)),
            DMA((stages, ticks * parts)),
            DMA((stages,)),
            DMA((stages,)),
        ],
        compiler_params=pltpu.CompilerParams(collective_id=cid, has_side_effects=True, vmem_limit_bytes=62 << 20),
    )(*operands)


def cut_messages(devices, chunks, chunk_rows):
    per_tick, parts = min(
        (count, -cut)
        for count in range(1, chunks + 1)
        for cut in range(1, 5)
        if chunks % count == 0 and chunk_rows * count % (devices * 16 * cut) == 0
    )
    return per_tick, -parts


def layer(far_slots, index, sizes, inputs, item_counts, lengths, vectors, weight_in, weight_out, cotangent, seq_table, hid_table):
    rows, slots, features = inputs.shape
    wide = weight_in.shape[1]
    chunks = wide // WIDE
    chunk_rows = 2 * features * WIDE // LANES
    per_tick, parts = cut_messages(sizes[0] * sizes[1], chunks, chunk_rows)
    act, dg, nrm, summed, second, low, lo, part = run_forward(
        sizes, far_slots, slots,
        item_counts, lengths, vectors, inputs, cotangent, weight_in, weight_out, seq_table, hid_table,
        cid=2 * index + 2,
    )
    full, grad, small = run_backward(
        sizes, far_slots, slots, chunks // per_tick, chunk_rows * per_tick, parts,
        item_counts, lengths, vectors, part, act, dg, nrm, summed, second, low, weight_in, weight_out, seq_table, hid_table,
        cid=2 * index + 3,
    )
    return full, grad, small, lo


def per_device(
    inputs, item_counts, lengths, gain_one, shift_one, weight_in, bias_in, weight_out, bias_out, gain_two, shift_two, cotangent
):
    rows, slots, features = inputs.shape
    wide = weight_in.shape[1]
    sizes = (lax.axis_size("dp"), lax.axis_size("seq"))
    seq_total = rows * sizes[1]
    chunks = wide // WIDE
    chunk_rows = 2 * features * WIDE // LANES
    shape = jax.ShapeDtypeStruct

    seq_cos, seq_sin = dft_tables(seq_total)
    hid_cos, hid_sin = dft_tables(features)
    seq_table = [table.reshape(sizes[1], rows, seq_total) for table in (seq_cos, seq_sin)]
    seq_table = jnp.asarray(np.concatenate(seq_table, axis=1).astype(jnp.bfloat16))
    hid_table = jnp.asarray(np.concatenate([hid_cos, -hid_sin], axis=0).astype(jnp.bfloat16))
    vectors = jnp.concatenate([gain_one, shift_one, bias_out, gain_two, shift_two, bias_in]).reshape(-1, features)
    operands = (inputs, item_counts, lengths, vectors, weight_in, weight_out, cotangent, seq_table, hid_table)

    full, grad, small, lo = layer(slots, 0, sizes, *operands)

    side = 2 if chunks % 2 == 0 else 1
    wi_grad, wo_grad = pl.pallas_call(
        widen_kernel,
        name="widen",
        grid=(chunks // side,),
        out_shape=(shape((features, wide), F32), shape((wide, features), F32)),
        in_specs=[pl.BlockSpec((side, chunk_rows, LANES), lambda n: (n, 0, 0))],
        out_specs=(
            pl.BlockSpec((features, side * WIDE), lambda n: (0, n)),
            pl.BlockSpec((side * WIDE, features), lambda n: (n, 0)),
        ),
        compiler_params=pltpu.CompilerParams(vmem_limit_bytes=50 << 20),
    )(full.reshape(chunks, chunk_rows, LANES))

    step = rows // 2
    lo, grad = lo.reshape(slots, rows, features), grad.reshape(slots, rows, features)
    layer_out, input_grad = pl.pallas_call(
        functools.partial(restore_kernel, slots),
        name="restore",
        grid=(rows // step,),
        out_shape=(shape(inputs.shape, F32), shape(inputs.shape, F32)),
        in_specs=[SMEM] * 2 + [pl.BlockSpec((slots, step, features), lambda n: (0, n, 0))] * 2,
        out_specs=[pl.BlockSpec((step, slots, features), lambda n: (n, 0, 0))] * 2,
        scratch_shapes=[pltpu.SMEM((slots,), jnp.int32), pltpu.SMEM((slots,), jnp.int32)],
        compiler_params=pltpu.CompilerParams(vmem_limit_bytes=50 << 20),
    )(item_counts, lengths, lo, grad)

    small = small.reshape(-1)
    cuts = np.cumsum([features, features, wide, features, features, features])
    parts = [small[end - size : end] for end, size in zip(cuts, np.diff(cuts, prepend=0))]
    gain_one_grad, shift_one_grad, bias_in_grad, bias_out_grad, gain_two_grad, shift_two_grad = parts
    return (
        layer_out, input_grad, gain_one_grad, shift_one_grad, wi_grad, bias_in_grad, wo_grad, bias_out_grad, gain_two_grad, shift_two_grad,
    )


def solution(mesh):
    placed = (
        P("seq", "dp", None), P("dp"), P("dp"), P(), P(), P(), P(), P(), P(), P(), P(), P("seq", "dp", None),
    )
    wide = P("seq", "dp", None)
    return jax.shard_map(
        per_device,
        mesh=mesh,
        in_specs=placed,
        out_specs=(wide, wide, P(), P(), P(), P(), P(), P(), P(), P()),
        check_vma=False,
    )
```

```python
import functools
import math

import jax
import jax.numpy as jnp
import numpy as np
from jax import lax
from jax.experimental import pallas as pl
from jax.experimental.pallas import tpu as pltpu
from jax.sharding import PartitionSpec as P

EPSILON = 1e-05
MESH = pl.DeviceIdType.MESH
LANES = 128
WIDE = 512
BF16 = jnp.bfloat16
F32 = jnp.float32


def dft_tables(count):
    index = np.arange(count, dtype=np.int64)
    turns = (index[:, None] * index[None, :] % count).astype(np.float32)
    angle = (turns * np.float32(2.0 * math.pi / count)).astype(np.float64)
    return np.cos(angle).astype(np.float32), np.sin(angle).astype(np.float32)


def aligned(value, step):
    return pl.multiple_of(value, step)


def bit_of(value, k):
    return (value // k) % 2


def flipped(value, k):
    return value + k * (1 - 2 * bit_of(value, k))


def axis_bits(axis, size):
    return [(axis, 1 << b) for b in range(size.bit_length() - 1)]


class Cube:
    def __init__(self, sizes, mids):
        dp, seq = sizes
        bits = axis_bits(1, seq) + axis_bits(0, dp)
        first, near, rest = bits[:1], bits[1:4], bits[4:]
        self.orders = [first + [near[i] for i in mid] + rest for mid in mids]
        self.bits = bits
        self.stages = len(bits)
        self.me = (lax.axis_index("dp"), lax.axis_index("seq"))
        self.values = {bit: self.value(bit) for bit in bits}
        self.partners = {bit: self.partner(bit) for bit in bits}

    def value(self, bit):
        return bit_of(self.me[bit[0]], bit[1])

    def partner(self, bit):
        axis, k = bit
        other = flipped(self.me[axis], k)
        return (other, self.me[1]) if axis == 0 else (self.me[0], other)

    def offset(self, order, level, rows):
        total = 0
        for s in range(level):
            total = total + self.values[self.orders[order][s]] * (rows >> (s + 1))
        return total


class Exchange:
    def __init__(self, size, rows, buf, send, recv):
        self.size, self.rows, self.buf, self.send_sem, self.recv_sem = size, rows, buf, send, recv
        self.dp, self.q = lax.axis_index("dp"), lax.axis_index("seq")
        self.order = [1 << b for b in reversed(range(size.bit_length() - 1))]

    def owner(self, pattern):
        index = self.q
        for k in self.order:
            if pattern & k:
                index = flipped(index, k)
        return index

    def copy(self, slot, pattern):
        hop = pattern & -pattern
        place = pl.ds(aligned(self.owner(pattern - hop) * self.rows, self.rows), self.rows)
        ref = self.buf.at[slot, place]
        return pltpu.make_async_remote_copy(
            src_ref=ref,
            dst_ref=ref,
            send_sem=self.send_sem.at[slot, pattern],
            recv_sem=self.recv_sem.at[slot, pattern],
            device_id=(self.dp, flipped(self.q, hop)),
            device_id_type=MESH,
        )

    def patterns(self, far):
        return range(1, self.size) if far else range(1, 2)

    def start_own(self, slot, far):
        for pattern in self.patterns(far):
            if pattern & (pattern - 1) == 0:
                self.copy(slot, pattern).start()

    def forward(self, slot):
        for pattern in self.patterns(True):
            if pattern & 1 == 0:
                self.copy(slot, pattern).wait_recv()
                for k in self.order:
                    if k < (pattern & -pattern):
                        self.copy(slot, pattern | k).start()

    def wait_near(self, slot, far):
        for pattern in self.patterns(far):
            if pattern & 1:
                self.copy(slot, pattern).wait_recv()

    def wait_sends(self, slot, far):
        for pattern in self.patterns(far):
            self.copy(slot, pattern).wait_send()


def greet(partners):
    barrier = pltpu.get_barrier_semaphore()
    for partner in partners:
        pl.semaphore_signal(barrier, inc=1, device_id=partner, device_id_type=MESH)
    pl.semaphore_wait(barrier, len(partners))


def rank_slots(count_ref, length_ref, perm_s, slen_s, slots):
    count = count_ref[0]
    live = [jnp.where(i < count, length_ref[i], 0) for i in range(slots)]
    ranks = []
    for i in range(slots):
        rank = 0
        for k in range(slots):
            if k != i:
                ahead = live[k] >= live[i] if k < i else live[k] > live[i]
                rank = rank + jnp.where(ahead, 1, 0)
        ranks.append(rank)
    for j in range(slots):
        perm, length = 0, 0
        for i in range(slots):
            here = ranks[i] == j
            perm = perm + jnp.where(here, i, 0)
            length = length + jnp.where(here, live[i], 0)
        perm_s[j] = perm
        slen_s[j] = length


def live_rows(slen_s, slot, first, rows):
    position = first + lax.broadcasted_iota(jnp.int32, (rows, 1), 0)
    return position < slen_s[slot]


def fold8(values):
    rows, lanes = values.shape
    return values.reshape(rows // 8, 8, lanes).sum(axis=0)


def normalize(values):
    center = values - jnp.mean(values, axis=-1, keepdims=True)
    spread = jnp.mean(center * center, axis=-1, keepdims=True)
    inverse = lax.rsqrt(spread + EPSILON)
    return center * inverse, inverse


def norm_back(grad_hat, normal, inverse):
    first = jnp.mean(grad_hat, axis=-1, keepdims=True)
    second = jnp.mean(grad_hat * normal, axis=-1, keepdims=True)
    return inverse * (grad_hat - first - normal * second)


def mix_slot(slot, far, exchange, tables, buf, uv, place):
    rows = exchange.rows
    if far:
        table, block = tables[...], buf[slot]
    else:
        base = aligned(exchange.q // 2 * (2 * rows), 2 * rows)
        table, block = tables[:, pl.ds(base, 2 * rows)], buf[slot, pl.ds(base, 2 * rows), :]
    both = jnp.dot(table, block, preferred_element_type=F32).astype(BF16)
    width = both.shape[1]
    uv[pl.ds(place, rows), :width] = both[:rows]
    uv[pl.ds(place, rows), width:] = both[rows:]


def group_at(i, near_groups, count):
    if near_groups == 0:
        return count - 1 - i
    return jnp.where(i < near_groups, count - near_groups + i, count - 1 - i)


def forward_kernel(cfg, *refs):
    sizes, far_slots, slots, group = cfg
    vec_refs, refs = refs[2:8], refs[:2] + refs[8:]
    (
        count_ref, length_ref, x_hbm, cot_hbm, wi_hbm, wo_hbm, sc_hbm, hc_hbm,
        act_o, dg_o, nrm_o, sum_o, gs_o, gb_o, lo_o, part_o,
        perm_s, slen_s, x_v, cot_v, wi_v, wo_v, sc_v, hc_v, buf, uv, sum_v, nrm_v, act_v, dg_v, gs_v, gb_v, lo_v, br_v, vec_ref,
        load_sem, out_sem, send_sem, recv_sem,
    ) = refs
    rows, _, features = x_v.shape
    wide = wi_v.shape[1]
    seq_total = rows * sizes[1]
    scale = 1.0 / math.sqrt(features * seq_total)
    exchange = Exchange(sizes[1], rows, buf, send_sem, recv_sem)
    q = exchange.q
    first = q * rows
    gain_one, shift_one, bias_out, gain_two, shift_two = (lambda i=i: vec_ref[i : i + 1, :] for i in range(5))
    loads = [
        pltpu.make_async_copy(x_hbm, x_v, load_sem.at[0]),
        pltpu.make_async_copy(sc_hbm.at[q], sc_v, load_sem.at[1]),
        pltpu.make_async_copy(hc_hbm, hc_v, load_sem.at[2]),
        pltpu.make_async_copy(wi_hbm, wi_v, load_sem.at[3]),
        pltpu.make_async_copy(wo_hbm, wo_v, load_sem.at[4]),
        pltpu.make_async_copy(cot_hbm, cot_v, load_sem.at[5]),
    ]
    loads[0].start()
    row = 0
    for vec in vec_refs:
        for i in range(vec.shape[0] // features):
            vec_ref[row : row + 1, :] = vec[pl.ds(i * features, features)].reshape(1, features)
            row += 1
    rank_slots(count_ref, length_ref, perm_s, slen_s, slots)
    greet([(exchange.dp, flipped(q, k)) for k in exchange.order])
    loads[0].wait()
    for load in loads[1:]:
        load.start()

    def prepare(i, _):
        slot = jnp.where(i < far_slots, far_slots - 1 - i, i) if far_slots < slots else slots - 1 - i
        value = jnp.where(live_rows(slen_s, slot, first, rows), x_v[:, perm_s[slot], :], 0.0)
        sum_v[pl.ds(aligned(slot * rows, rows), rows), :] = value
        buf[slot, pl.ds(aligned(first, rows), rows), :] = value.astype(BF16)
        pl.when(i < far_slots)(lambda: exchange.start_own(slot, True))
        if far_slots < slots:
            pl.when(i >= far_slots)(lambda: exchange.start_own(slot, False))
        return 0

    lax.fori_loop(0, slots, prepare, 0)
    part_o[...] = jnp.zeros_like(part_o)
    for load in loads[1:3]:
        load.wait()

    batch = group * rows
    span = features
    count = slots // group
    near_groups = (slots - far_slots) // group

    def outs(base):
        place = pl.ds(base, batch)
        copies = [
            pltpu.make_async_copy(nrm_v.at[place], nrm_o.at[place], out_sem.at[0]),
            pltpu.make_async_copy(sum_v.at[place], sum_o.at[place], out_sem.at[1]),
            pltpu.make_async_copy(gs_v.at[place], gs_o.at[place], out_sem.at[2]),
            pltpu.make_async_copy(lo_v.at[place], lo_o.at[place], out_sem.at[3]),
            pltpu.make_async_copy(gb_v.at[place], gb_o.at[place], out_sem.at[6]),
        ]
        for n in range(wide // WIDE):
            cut = pl.ds(n * WIDE, WIDE)
            copies.append(pltpu.make_async_copy(act_v.at[place, cut], act_o.at[n, place], out_sem.at[4]))
            copies.append(pltpu.make_async_copy(dg_v.at[place, cut], dg_o.at[n, place], out_sem.at[5]))
        return copies

    def bring(slot0):
        for k in reversed(range(group)):
            exchange.forward(slot0 + k)

    def mixing(slot0, far):
        for k in reversed(range(group)):
            exchange.wait_near(slot0 + k, far)
            mix_slot(slot0 + k, far, exchange, sc_v, buf, uv, k * rows)

    def work(i, _):
        slot0 = group_at(i, near_groups, count) * group
        base = aligned(slot0 * rows, batch)
        place = pl.ds(base, batch)
        if near_groups < count:
            pl.when(i >= near_groups)(lambda: mixing(slot0, True))
        if near_groups > 0:
            pl.when(i < near_groups)(lambda: mixing(slot0, False))
        mixed = jnp.dot(uv[...], hc_v[...], preferred_element_type=F32)
        sum_v[place, :] = sum_v[place, :] + (mixed * scale).astype(BF16).astype(F32)

        def norm_one(k, _):
            here = pl.ds(aligned(base + k * rows, rows), rows)
            hat, _ = normalize(sum_v[here, :])
            nrm_v[here, :] = (hat * gain_one() + shift_one()).astype(BF16)
            return 0

        lax.fori_loop(0, group, norm_one, 0)

        @pl.when(i == 0)
        def _():
            for load in loads[3:]:
                load.wait()

        def expand(n, _):
            cut = pl.ds(aligned(n * span, span), span)
            hidden = jnp.dot(nrm_v[place, :], wi_v[:, cut], preferred_element_type=F32) + vec_ref[pl.ds(5 + n, 1), :]
            gate = 0.5 + 0.5 * lax.erf(hidden * math.sqrt(0.5))
            slope = gate + hidden * (jnp.exp(hidden * hidden * -0.5) * (1.0 / math.sqrt(2.0 * math.pi)))
            act_v[place, cut] = (hidden * gate).astype(BF16)
            dg_v[place, cut] = slope.astype(BF16)
            return 0

        lax.fori_loop(0, wide // span, expand, 0)
        br_v[...] = jnp.dot(act_v[place, :], wo_v[...], preferred_element_type=F32)

        def norm_two(k, _):
            here = pl.ds(aligned(base + k * rows, rows), rows)
            local = pl.ds(aligned(k * rows, rows), rows)
            slot = slot0 + k
            live = live_rows(slen_s, slot, first, rows)
            hat, inverse = normalize(sum_v[here, :] + (br_v[local, :] + bias_out()))
            grad = jnp.where(live, cot_v[:, perm_s[slot], :], 0.0)
            lo_v[here, :] = jnp.where(live, hat * gain_two() + shift_two(), 0.0)
            part_o[0:8, :] = part_o[0:8, :] + fold8(grad * hat)
            part_o[8:16, :] = part_o[8:16, :] + fold8(grad)
            second = norm_back(grad * gain_two(), hat, inverse)
            low = second.astype(BF16)
            gs_v[here, :] = second
            gb_v[here, :] = low
            part_o[16:24, :] = part_o[16:24, :] + fold8(low.astype(F32))
            return 0

        lax.fori_loop(0, group, norm_two, 0)
        for copy in outs(base):
            copy.start()
        if near_groups < count:

            @pl.when((i + 1 >= near_groups) & (i + 1 < count))
            def _():
                bring(group_at(i + 1, near_groups, count) * group)

        return 0

    if near_groups == 0:
        bring((count - 1) * group)
    lax.fori_loop(0, count, work, 0)

    def finish(slot, _):
        pl.when(slot < far_slots)(lambda: exchange.wait_sends(slot, True))
        if far_slots < slots:
            pl.when(slot >= far_slots)(lambda: exchange.wait_sends(slot, False))
        return 0

    lax.fori_loop(0, slots, finish, 0)

    def flush(g, _):
        for copy in outs(aligned(g * batch, batch)):
            copy.wait()
        return 0

    lax.fori_loop(0, count, flush, 0)


def backward_kernel(cfg, *refs):
    sizes, far_slots, slots, group, parts, mids, lags, plan = cfg
    cube = Cube(sizes, mids)
    S = cube.stages
    (
        count_ref, length_ref, gain_ref, part_ref,
        act_hbm, dg_hbm, nrm_hbm, sum_hbm, gs_hbm, gb_hbm, wi_hbm, wo_hbm, sc_hbm, hc_hbm,
        full_o, ig_o, small_o,
        perm_s, slen_s, gs_v, sum_v, nrm_v, gb_v, gh_v, gn_v, act_v, dg_v, wi_v, wo_v, sc_v, hc_v, buf, uv, ig_v,
        bin_v, one_v, small_v, gain_v, part_v, full,
    ) = refs[:40]
    landed = refs[40 : 40 + S]
    (
        small_recv, load_sem, sum_sem, stream_sem, out_sem, ig_sem, send_sem, recv_sem,
        rs_s, rs_r, ag_s, ag_r, sm_s, sm_r,
    ) = refs[40 + S :]
    ticks, tick_rows, _ = part_v.shape
    message = tick_rows // parts
    chunks = act_hbm.shape[0]
    per_tick = chunks // ticks
    features = nrm_v.shape[1]
    rows = gs_v.shape[0] // slots
    batch = group * rows
    scale = 1.0 / math.sqrt(features * rows * sizes[1])
    exchange = Exchange(sizes[1], rows, buf, send_sem, recv_sem)
    q = exchange.q
    first = q * rows
    loads = [
        pltpu.make_async_copy(gb_hbm, gb_v, load_sem.at[0]),
        pltpu.make_async_copy(nrm_hbm, nrm_v, load_sem.at[1]),
        pltpu.make_async_copy(gs_hbm, gs_v, load_sem.at[2]),
        pltpu.make_async_copy(sc_hbm.at[q], sc_v, load_sem.at[3]),
        pltpu.make_async_copy(hc_hbm, hc_v, load_sem.at[4]),
    ]

    def turn(i):
        return jnp.where(i < far_slots, far_slots - 1 - i, i) if far_slots < slots else slots - 1 - i

    def sum_copy(i):
        place = pl.ds(aligned(turn(i) * rows, rows), rows)
        return pltpu.make_async_copy(sum_hbm.at[place], sum_v.at[lax.rem(i, 2)], sum_sem.at[lax.rem(i, 2)])

    def streams(n, slot):
        cut = pl.ds(aligned(n * WIDE, WIDE), WIDE)
        return [
            pltpu.make_async_copy(act_hbm.at[n], act_v.at[slot], stream_sem.at[0, slot]),
            pltpu.make_async_copy(wo_hbm.at[cut], wo_v.at[slot], stream_sem.at[1, slot]),
            pltpu.make_async_copy(dg_hbm.at[n], dg_v.at[slot], stream_sem.at[2, slot]),
            pltpu.make_async_copy(wi_hbm.at[:, cut], wi_v.at[slot], stream_sem.at[3, slot]),
        ]

    loads[0].start()
    for copy in streams(0, 0):
        copy.start()
    for load in loads[1:]:
        load.start()
    for i in range(2):
        sum_copy(i).start()
    rank_slots(count_ref, length_ref, perm_s, slen_s, slots)
    greet([cube.partner(bit) for bit in cube.bits])

    starts = [[j * message + cube.offset(j, level, message) for level in range(S + 1)] for j in range(parts)]

    def rs(m, t, j, s):
        bit = cube.orders[j][s]
        half = message >> (s + 1)
        off = starts[j][s] + (1 - cube.values[bit]) * half
        return pltpu.make_async_remote_copy(
            src_ref=part_v.at[t, pl.ds(aligned(off, 16), half)],
            dst_ref=landed[s].at[m],
            send_sem=rs_s.at[s],
            recv_sem=rs_r.at[s, m],
            device_id=cube.partners[bit],
            device_id_type=MESH,
        )

    def ag(m, t, j, s):
        bit = cube.orders[j][s]
        half = message >> (s + 1)
        ref = full.at[t, pl.ds(aligned(starts[j][s + 1], 16), half)]
        return pltpu.make_async_remote_copy(
            src_ref=ref,
            dst_ref=ref,
            send_sem=ag_s.at[s],
            recv_sem=ag_r.at[s, m],
            device_id=cube.partners[bit],
            device_id_type=MESH,
        )

    def add(m, t, j, s):
        half = message >> (s + 1)
        place = pl.ds(aligned(starts[j][s + 1], 16), half)
        total = part_v[t, place, :].astype(F32) + landed[s][m].astype(F32)
        target = full if s == S - 1 else part_v
        target[t, place, :] = total.astype(BF16)

    def out(t, j):
        place = pl.ds(j * message, message)
        return pltpu.make_async_copy(full.at[t, place], full_o.at[t, place], out_sem.at[t, j])

    def event(k, m, t, j):
        if k == 0:
            rs(m, t, j, 0).start()
        elif k <= S:
            rs(m, t, j, k - 1).wait_recv()
            add(m, t, j, k - 1)
            (rs(m, t, j, k) if k < S else ag(m, t, j, S - 1)).start()
        elif k < 2 * S:
            s = 2 * S - k
            ag(m, t, j, s).wait_recv()
            ag(m, t, j, s - 1).start()
        else:
            ag(m, t, j, 0).wait_recv()
            out(t, j).start()

    def sends_done():
        for s in range(S):
            for sem in (rs_s.at[s], ag_s.at[s]):
                pltpu.make_async_copy(landed[s], landed[s], sem).wait()

    when = [0 if per_tick == 1 and parts == 4 else parts]
    for lag in lags:
        when.append(when[-1] + lag)

    def events(tick, j):
        for k in reversed(range(2 * S + 1)):
            t = tick + (j - when[k]) // parts
            jj = (j - when[k]) % parts
            pl.when((t >= 0) & (t < ticks))(functools.partial(event, k, t * parts + jj, t, jj))

    bin_v[...] = jnp.zeros_like(bin_v)
    one_v[...] = jnp.zeros_like(one_v)
    gain_v[...] = gain_ref[...].reshape(1, features)
    gn_v[...] = jnp.zeros_like(gn_v)
    small_v[...] = jnp.zeros_like(small_v)
    loads[0].wait()

    def contract(left, right, dims):
        return lax.dot_general(left, right, ((dims, dims), ((), ())), preferred_element_type=F32)

    def weigh_out(n, slot, t, base):
        streams(n, slot)[0].wait()
        grad = contract(act_v[slot], gb_v[...], (0,)).astype(BF16)
        for i in range(features // LANES):
            part_v[t, pl.ds(base + i * WIDE, WIDE), :] = grad[:, i * LANES : (i + 1) * LANES]

    def pull(n, slot, t, base):
        streams(n, slot)[1].wait()
        streams(n, slot)[2].wait()
        pulled = contract(gb_v[...], wo_v[slot], (1,)) * dg_v[slot].astype(F32)
        pulled = pulled.astype(BF16)
        gh_v[...] = pulled
        bin_v[n] = fold8(pulled.astype(F32))

    def weigh_in(n, slot, t, base):
        pl.when(n == 0)(loads[1].wait)
        grad = contract(nrm_v[...], gh_v[...], (0,)).astype(BF16)
        for i in range(WIDE // LANES):
            place = pl.ds(base + features // LANES * WIDE + i * features, features)
            part_v[t, place, :] = grad[:, i * LANES : (i + 1) * LANES]

    def spread(n, slot, t, base):
        streams(n, slot)[3].wait()
        for i in range(2):
            here = pl.ds(i * (slots // 2) * rows, slots // 2 * rows)
            gn_v[here, :] = gn_v[here, :] + contract(gh_v[here, :], wi_v[slot], (1,))

    steps = [weigh_out, pull, weigh_in, spread]

    def compute(tick, j):
        if per_tick == 1 and parts == 4:
            slot = lax.rem(tick, 2)
            if j == 0:
                for copy in streams(tick + 1, 1 - slot):
                    pl.when(tick + 1 < chunks)(copy.start)
            steps[j](tick, slot, tick, 0)
        elif j == 0:

            def whole(u, _):
                n = tick * per_tick + u
                slot = lax.rem(n, 2)
                for copy in streams(n + 1, 1 - slot):
                    pl.when(n + 1 < chunks)(copy.start)
                for step in steps:
                    step(n, slot, tick, aligned(u * (tick_rows // per_tick), LANES))
                return 0

            lax.fori_loop(0, per_tick, whole, 0)

    def back(i, _):
        slot = turn(i)
        here = pl.ds(aligned(slot * rows, rows), rows)
        pl.when(i == 0)(loads[2].wait)
        sum_copy(i).wait()
        hat, inverse = normalize(sum_v[lax.rem(i, 2)])
        grad = gn_v[here, :]
        one_v[0:8, :] = one_v[0:8, :] + fold8(grad * hat)
        one_v[8:16, :] = one_v[8:16, :] + fold8(grad)
        grad = gs_v[here, :] + norm_back(grad * gain_v[...], hat, inverse)
        gs_v[here, :] = grad
        buf[slot, pl.ds(aligned(first, rows), rows), :] = grad.astype(BF16)
        pl.when(i < far_slots)(lambda: exchange.start_own(slot, True))
        if far_slots < slots:
            pl.when(i >= far_slots)(lambda: exchange.start_own(slot, False))
        pl.when(i + 2 < slots)(lambda: sum_copy(i + 2).start())
        return 0

    def small_copy(s):
        return pltpu.make_async_remote_copy(
            src_ref=small_v.at[s],
            dst_ref=small_recv.at[s],
            send_sem=sm_s.at[s],
            recv_sem=sm_r.at[s],
            device_id=cube.partners[cube.bits[s]],
            device_id_type=MESH,
        )

    def small_start():
        row = 0
        vectors = [one_v[0:8, :], one_v[8:16, :]] + [bin_v[n] for n in range(chunks)]
        vectors += [part_ref[16:24, :], part_ref[0:8, :], part_ref[8:16, :]]
        for vector in vectors:
            vector = jnp.sum(vector, axis=0, keepdims=True)
            for i in range(vector.shape[1] // LANES):
                small_v[0, row : row + 1, :] = vector[:, i * LANES : (i + 1) * LANES]
                row += 1
        small_copy(0).start()

    def small_step(s):
        small_copy(s).wait()
        if s + 1 < S:
            small_v[s + 1] = small_v[s] + small_recv[s]
            small_copy(s + 1).start()
        else:
            small_o[...] = small_v[s] + small_recv[s]

    count = slots // group
    near_groups = (slots - far_slots) // group

    def grad_copy(i):
        base = aligned(group_at(i, near_groups, count) * batch, batch)
        return pltpu.make_async_copy(ig_v.at[lax.rem(i, 2)], ig_o.at[pl.ds(base, batch)], ig_sem.at[lax.rem(i, 2)])

    def mixing(i, k, far):
        slot = group_at(i, near_groups, count) * group + k
        exchange.wait_near(slot, far)
        mix_slot(slot, far, exchange, sc_v, buf, uv, k * rows)

    def hidden_mix(i):
        pl.when(i >= 2)(lambda: grad_copy(i - 2).wait())
        ig_v[lax.rem(i, 2)] = jnp.dot(uv[...], hc_v[...], preferred_element_type=F32)

    def finish(i):
        for k in range(group):
            slot = group_at(i, near_groups, count) * group + k
            here = pl.ds(aligned(slot * rows, rows), rows)
            local = pl.ds(k * rows, rows)
            grad = gs_v[here, :] + ig_v[lax.rem(i, 2), local, :] * scale
            ig_v[lax.rem(i, 2), local, :] = jnp.where(live_rows(slen_s, slot, first, rows), grad, 0.0)
        grad_copy(i).start()

    def bring(i):
        for k in reversed(range(group)):
            exchange.forward(group_at(i, near_groups, count) * group + k)

    small_at, near_at, far_at, lead = plan

    def drain(tick, j):
        d = tick - ticks

        @pl.when(d == 0)
        def _():
            share = -(-slots // parts)
            lax.fori_loop(min(j * share, slots), min((j + 1) * share, slots), back, 0)

        here = lambda at: pl.when(d * parts + j == at)
        if j == small_at % parts:
            here(small_at)(small_start)
        for s in range(S):
            at = small_at + 3 * (s + 1)
            if j == at % parts:
                here(at)(functools.partial(small_step, s))
        if j == 0:

            @pl.when(d == 1)
            def _():
                for load in loads[3:]:
                    load.wait()

        for far, start, low, high in ((False, near_at, 0, near_groups), (True, far_at, near_groups, count)):
            if low == high:
                continue
            i = d - start + low

            @pl.when((i >= low) & (i < high))
            def _():
                subs = [
                    lambda: mixing(i, 0, far),
                    lambda: [mixing(i, k, far) for k in range(1, group)],
                    lambda: hidden_mix(i),
                    lambda: finish(i),
                ]
                for at, sub in enumerate(subs):
                    if min(at, parts - 1) == j:
                        sub()

            if far and j == parts - 1:
                ahead = i + lead
                pl.when((ahead >= low) & (ahead < high))(lambda: bring(ahead))

    last = ticks + max(
        -(-(when[-1] + 1) // parts),
        (small_at + 3 * S) // parts + 1,
        near_at + near_groups,
        far_at + count - near_groups,
    )

    def body(tick, _):
        for j in range(parts):
            pl.when(tick < ticks)(lambda: compute(tick, j))
            events(tick, j)
            pl.when(tick >= ticks)(lambda: drain(tick, j))
        return 0

    lax.fori_loop(0, last, body, 0)

    def settle(slot, _):
        pl.when(slot < far_slots)(lambda: exchange.wait_sends(slot, True))
        if far_slots < slots:
            pl.when(slot >= far_slots)(lambda: exchange.wait_sends(slot, False))
        return 0

    lax.fori_loop(0, slots, settle, 0)
    for i in range(max(0, count - 2), count):
        grad_copy(i).wait()

    def finish_out(t, _):
        for j in range(parts):
            out(t, j).wait()
        return 0

    lax.fori_loop(0, ticks, finish_out, 0)
    sends_done()


def output_kernel(slots, cuts, places, count_ref, length_ref, full_ref, lo_ref, ig_ref, small_ref, *refs):
    wi_ref, wo_ref, lo_out, ig_out = refs[:4]
    vector_refs, (perm_s, slen_s) = refs[4:-2], refs[-2:]
    step = pl.program_id(0)
    features = wi_ref.shape[0]
    for i in range(features // LANES):
        wo_ref[:, i * LANES : (i + 1) * LANES] = full_ref[0, pl.ds(i * WIDE, WIDE), :].astype(F32)
    for i in range(WIDE // LANES):
        start = features // LANES * WIDE + i * features
        wi_ref[:, i * LANES : (i + 1) * LANES] = full_ref[0, pl.ds(start, features), :].astype(F32)

    @pl.when(step == 0)
    def _():
        rank_slots(count_ref, length_ref, perm_s, slen_s, slots)
        for ref, start in zip(vector_refs, cuts):
            ref[...] = small_ref[start : start + ref.shape[0], :]

    @pl.when(step < places)
    def _():
        for j in range(slots):
            lo_out[:, perm_s[j], :] = lo_ref[j]
            ig_out[:, perm_s[j], :] = ig_ref[j]


ANY = pl.BlockSpec(memory_space=pl.ANY)
SMEM = pl.BlockSpec(memory_space=pltpu.SMEM)
VMEM = pl.BlockSpec(memory_space=pltpu.VMEM)
DMA = pltpu.SemaphoreType.DMA
LAGS = [4, 4, 4, 4, 4, 4, 4, 4, 4, 4]
PLAN = (4, 1, 4, 1)
FAR_PLAN = (4, 1, 4, 1)
MIDS = ((0, 1, 2), (1, 0, 2), (2, 0, 1), (1, 2, 0))
FAR_MIDS = ((1, 2, 0), (2, 1, 0), (1, 0, 2), (2, 0, 1))


def run_forward(sizes, far_slots, slots, *operands, group=2, name="forward", cid=1):
    rows, _, features = operands[8].shape
    wide = operands[10].shape[1]
    seq_total = rows * sizes[1]
    flat, batch, chunks = rows * slots, group * rows, wide // WIDE
    shape = jax.ShapeDtypeStruct
    return pl.pallas_call(
        functools.partial(forward_kernel, (sizes, far_slots, slots, group)),
        name=name,
        out_shape=(
            shape((chunks, flat, WIDE), BF16),
            shape((chunks, flat, WIDE), BF16),
            shape((flat, features), BF16),
            shape((flat, features), F32),
            shape((flat, features), F32),
            shape((flat, features), BF16),
            shape((flat, features), F32),
            shape((24, features), F32),
        ),
        in_specs=[SMEM] * 2 + [VMEM] * 6 + [ANY] * 6,
        out_specs=[ANY] * 7 + [VMEM],
        scratch_shapes=[
            pltpu.SMEM((slots,), jnp.int32),
            pltpu.SMEM((slots,), jnp.int32),
            pltpu.VMEM((rows, slots, features), F32),
            pltpu.VMEM((rows, slots, features), F32),
            pltpu.VMEM((features, wide), BF16),
            pltpu.VMEM((wide, features), BF16),
            pltpu.VMEM((2 * rows, seq_total), BF16),
            pltpu.VMEM((2 * features, features), BF16),
            pltpu.VMEM((slots, seq_total, features), BF16),
            pltpu.VMEM((batch, 2 * features), BF16),
            pltpu.VMEM((flat, features), F32),
            pltpu.VMEM((flat, features), BF16),
            pltpu.VMEM((flat, wide), BF16),
            pltpu.VMEM((flat, wide), BF16),
            pltpu.VMEM((flat, features), F32),
            pltpu.VMEM((flat, features), BF16),
            pltpu.VMEM((flat, features), F32),
            pltpu.VMEM((batch, features), F32),
            pltpu.VMEM((5 + wide // features, features), F32),
            DMA((6,)),
            DMA((7,)),
            DMA((slots, sizes[1])),
            DMA((slots, sizes[1])),
        ],
        compiler_params=pltpu.CompilerParams(collective_id=cid, has_side_effects=True, vmem_limit_bytes=62 << 20),
    )(*operands)


def run_backward(sizes, far_slots, slots, ticks, tick_rows, parts, *operands, group=2, mids=None, lags=None, plan=None, name="backward", cid=2):
    devices = sizes[0] * sizes[1]
    chunks, flat, _ = operands[4].shape
    features, wide = operands[10].shape
    rows = flat // slots
    seq_total = rows * sizes[1]
    batch = group * rows
    message = tick_rows // parts
    shape = jax.ShapeDtypeStruct
    mostly_far = far_slots > slots * 5 // 8
    mids = mids or (FAR_MIDS if mostly_far else MIDS)
    plan = plan or (FAR_PLAN if mostly_far else PLAN)
    lags = lags or LAGS
    stages = devices.bit_length() - 1
    lags = (lags[:stages] + [2] * stages)[:stages] + ([2] * stages + lags[-stages:])[-stages:]
    return pl.pallas_call(
        functools.partial(backward_kernel, (sizes, far_slots, slots, group, parts, mids, lags, plan)),
        name=name,
        out_shape=(
            shape((ticks, tick_rows, LANES), BF16),
            shape((flat, features), F32),
            shape((64, LANES), F32),
        ),
        in_specs=[SMEM] * 2 + [VMEM] * 2 + [ANY] * 10,
        out_specs=[ANY] * 2 + [VMEM],
        scratch_shapes=[
            pltpu.SMEM((slots,), jnp.int32),
            pltpu.SMEM((slots,), jnp.int32),
            pltpu.VMEM((flat, features), F32),
            pltpu.VMEM((2, rows, features), F32),
            pltpu.VMEM((flat, features), BF16),
            pltpu.VMEM((flat, features), BF16),
            pltpu.VMEM((flat, WIDE), BF16),
            pltpu.VMEM((flat, features), F32),
            pltpu.VMEM((2, flat, WIDE), BF16),
            pltpu.VMEM((2, flat, WIDE), BF16),
            pltpu.VMEM((2, features, WIDE), BF16),
            pltpu.VMEM((2, WIDE, features), BF16),
            pltpu.VMEM((2 * rows, seq_total), BF16),
            pltpu.VMEM((2 * features, features), BF16),
            pltpu.VMEM((slots, seq_total, features), BF16),
            pltpu.VMEM((batch, 2 * features), BF16),
            pltpu.VMEM((2, batch, features), F32),
            pltpu.VMEM((chunks, 8, WIDE), F32),
            pltpu.VMEM((16, features), F32),
            pltpu.VMEM((stages, 64, LANES), F32),
            pltpu.VMEM((1, features), F32),
            pltpu.VMEM((ticks, tick_rows, LANES), BF16),
            pltpu.VMEM((ticks, tick_rows, LANES), BF16),
        ]
        + [pltpu.VMEM((ticks * parts, message >> (s + 1), LANES), BF16) for s in range(stages)]
        + [
            pltpu.VMEM((stages, 64, LANES), F32),
            DMA((5,)),
            DMA((2,)),
            DMA((4, 2)),
            DMA((ticks, parts)),
            DMA((2,)),
            DMA((slots, sizes[1])),
            DMA((slots, sizes[1])),
            DMA((stages,)),
            DMA((stages, ticks * parts)),
            DMA((stages,)),
            DMA((stages, ticks * parts)),
            DMA((stages,)),
            DMA((stages,)),
        ],
        compiler_params=pltpu.CompilerParams(collective_id=cid, has_side_effects=True, vmem_limit_bytes=62 << 20),
    )(*operands)


def agree_kernel(groups, choices, span, count_ref, length_ref, choice_o, mine, theirs, send_sem, recv_sem):
    dp, q = lax.axis_index("dp"), lax.axis_index("seq")

    def peer(i):
        return lax.rem(dp + i, groups)

    def copy(i):
        return pltpu.make_async_remote_copy(
            src_ref=mine,
            dst_ref=theirs.at[i],
            send_sem=send_sem.at[i],
            recv_sem=recv_sem.at[i],
            device_id=(peer(i), q),
            device_id_type=MESH,
        )

    greet([(peer(i), q) for i in range(1, groups)])
    far = 0
    for i in range(length_ref.shape[0]):
        far = far + jnp.where((i < count_ref[0]) & (length_ref[i] > span), 1, 0)
    need = jnp.full(mine.shape, far, jnp.int32)
    mine[...] = need.astype(F32)
    theirs[0] = need.astype(F32)
    for i in range(1, groups):
        copy(i).start()
    for i in range(1, groups):
        copy(i).wait()
    most = jnp.max(theirs[...])
    place = 0
    for far in choices[:-1]:
        place = place + jnp.where(most > far, 1, 0)
    choice_o[0] = place


def cut_messages(devices, chunks, chunk_rows):
    per_tick, parts = min(
        (count, -cut)
        for count in range(1, chunks + 1)
        for cut in range(1, 5)
        if chunks % count == 0 and chunk_rows * count % (devices * 16 * cut) == 0
    )
    return per_tick, -parts


def layer(far_slots, index, sizes, inputs, item_counts, lengths, vectors, weight_in, weight_out, cotangent, seq_table, hid_table):
    rows, slots, features = inputs.shape
    wide = weight_in.shape[1]
    chunks = wide // WIDE
    chunk_rows = 2 * features * WIDE // LANES
    per_tick, parts = cut_messages(sizes[0] * sizes[1], chunks, chunk_rows)
    act, dg, nrm, summed, second, low, lo, part = run_forward(
        sizes, far_slots, slots,
        item_counts, lengths, *vectors, inputs, cotangent, weight_in, weight_out, seq_table, hid_table,
        cid=2 * index + 2,
    )
    full, grad, small = run_backward(
        sizes, far_slots, slots, chunks // per_tick, chunk_rows * per_tick, parts,
        item_counts, lengths, vectors[0], part, act, dg, nrm, summed, second, low, weight_in, weight_out, seq_table, hid_table,
        cid=2 * index + 3,
    )
    shape = jax.ShapeDtypeStruct
    places = 1 << min(chunks.bit_length() - 1, 3)
    step = rows // places
    lo, grad = lo.reshape(slots, rows, features), grad.reshape(slots, rows, features)
    heights = [size // LANES for size in (features, features, wide, features, features, features)]
    cuts = [sum(heights[:i]) for i in range(len(heights))]
    slot_first = pl.BlockSpec((slots, step, features), lambda n: (0, jnp.minimum(n, places - 1), 0))
    place_first = pl.BlockSpec((step, slots, features), lambda n: (jnp.minimum(n, places - 1), 0, 0))
    wi_grad, wo_grad, layer_out, input_grad, *vectors = pl.pallas_call(
        functools.partial(output_kernel, slots, cuts, places),
        name="output",
        grid=(chunks,),
        out_shape=(
            shape((features, wide), F32),
            shape((wide, features), F32),
            shape(inputs.shape, F32),
            shape(inputs.shape, F32),
            *(shape((height, LANES), F32) for height in heights),
        ),
        in_specs=[SMEM] * 2 + [pl.BlockSpec((1, chunk_rows, LANES), lambda n: (n, 0, 0))] + [slot_first] * 2 + [VMEM],
        out_specs=(
            pl.BlockSpec((features, WIDE), lambda n: (0, n)),
            pl.BlockSpec((WIDE, features), lambda n: (n, 0)),
            place_first,
            place_first,
            *([VMEM] * len(heights)),
        ),
        scratch_shapes=[pltpu.SMEM((slots,), jnp.int32), pltpu.SMEM((slots,), jnp.int32)],
        compiler_params=pltpu.CompilerParams(vmem_limit_bytes=60 << 20),
    )(item_counts, lengths, full.reshape(chunks, chunk_rows, LANES), lo, grad, small)
    gain_one_grad, shift_one_grad, bias_in_grad, bias_out_grad, gain_two_grad, shift_two_grad = [v.reshape(-1) for v in vectors]
    return (
        layer_out, input_grad, gain_one_grad, shift_one_grad, wi_grad, bias_in_grad, wo_grad, bias_out_grad, gain_two_grad, shift_two_grad,
    )


def per_device(
    inputs, item_counts, lengths, gain_one, shift_one, weight_in, bias_in, weight_out, bias_out, gain_two, shift_two, cotangent
):
    rows, slots, features = inputs.shape
    wide = weight_in.shape[1]
    sizes = (lax.axis_size("dp"), lax.axis_size("seq"))
    seq_total = rows * sizes[1]
    chunks = wide // WIDE
    chunk_rows = 2 * features * WIDE // LANES
    shape = jax.ShapeDtypeStruct

    seq_cos, seq_sin = dft_tables(seq_total)
    hid_cos, hid_sin = dft_tables(features)
    seq_table = [table.reshape(sizes[1], rows, seq_total) for table in (seq_cos, seq_sin)]
    seq_table = jnp.asarray(np.concatenate(seq_table, axis=1).astype(jnp.bfloat16))
    hid_table = jnp.asarray(np.concatenate([hid_cos, -hid_sin], axis=0).astype(jnp.bfloat16))
    vectors = (gain_one, shift_one, bias_out, gain_two, shift_two, bias_in)
    operands = (inputs, item_counts, lengths, vectors, weight_in, weight_out, cotangent, seq_table, hid_table)

    choices = sorted({slots // 2, slots})
    choice = pl.pallas_call(
        functools.partial(agree_kernel, sizes[0], choices, 2 * rows),
        name="agree",
        out_shape=shape((1,), jnp.int32),
        in_specs=[SMEM] * 2,
        out_specs=SMEM,
        scratch_shapes=[
            pltpu.VMEM((8, LANES), F32),
            pltpu.VMEM((sizes[0], 8, LANES), F32),
            DMA((sizes[0],)),
            DMA((sizes[0],)),
        ],
        compiler_params=pltpu.CompilerParams(collective_id=1, has_side_effects=True),
    )(item_counts, lengths)
    branches = [functools.partial(layer, far, index, sizes) for index, far in enumerate(choices)]

    return lax.switch(choice[0], branches, *operands)


def solution(mesh):
    placed = (
        P("seq", "dp", None), P("dp"), P("dp"), P(), P(), P(), P(), P(), P(), P(), P(), P("seq", "dp", None),
    )
    wide = P("seq", "dp", None)
    return jax.shard_map(
        per_device,
        mesh=mesh,
        in_specs=placed,
        out_specs=(wide, wide, P(), P(), P(), P(), P(), P(), P(), P()),
        check_vma=False,
    )
```

```python
import functools
import math

import jax
import jax.numpy as jnp
import numpy as np
from jax import lax
from jax.experimental import pallas as pl
from jax.experimental.pallas import tpu as pltpu
from jax.sharding import PartitionSpec as P

EPSILON = 1e-05
MESH = pl.DeviceIdType.MESH
LANES = 128
WIDE = 512
BF16 = jnp.bfloat16
F32 = jnp.float32


def dft_tables(count):
    index = np.arange(count, dtype=np.int64)
    turns = (index[:, None] * index[None, :] % count).astype(np.float32)
    angle = (turns * np.float32(2.0 * math.pi / count)).astype(np.float64)
    return np.cos(angle).astype(np.float32), np.sin(angle).astype(np.float32)


def aligned(value, step):
    return pl.multiple_of(value, step)


def bit_of(value, k):
    return (value // k) % 2


def flipped(value, k):
    return value + k * (1 - 2 * bit_of(value, k))


def axis_bits(axis, size):
    return [(axis, 1 << b) for b in range(size.bit_length() - 1)]


class Cube:
    def __init__(self, sizes, mids):
        dp, seq = sizes
        bits = axis_bits(1, seq) + axis_bits(0, dp)
        first, near, rest = bits[:1], bits[1:4], bits[4:]
        self.orders = [first + [near[i] for i in mid] + rest for mid in mids]
        self.bits = bits
        self.stages = len(bits)
        self.me = (lax.axis_index("dp"), lax.axis_index("seq"))
        self.values = {bit: self.value(bit) for bit in bits}
        self.partners = {bit: self.partner(bit) for bit in bits}

    def value(self, bit):
        return bit_of(self.me[bit[0]], bit[1])

    def partner(self, bit):
        axis, k = bit
        other = flipped(self.me[axis], k)
        return (other, self.me[1]) if axis == 0 else (self.me[0], other)

    def offset(self, order, level, rows):
        total = 0
        for s in range(level):
            total = total + self.values[self.orders[order][s]] * (rows >> (s + 1))
        return total


class Exchange:
    def __init__(self, size, rows, buf, send, recv):
        self.size, self.rows, self.buf, self.send_sem, self.recv_sem = size, rows, buf, send, recv
        self.dp, self.q = lax.axis_index("dp"), lax.axis_index("seq")
        self.order = [1 << b for b in reversed(range(size.bit_length() - 1))]

    def owner(self, pattern):
        index = self.q
        for k in self.order:
            if pattern & k:
                index = flipped(index, k)
        return index

    def copy(self, slot, pattern):
        hop = pattern & -pattern
        place = pl.ds(aligned(self.owner(pattern - hop) * self.rows, self.rows), self.rows)
        ref = self.buf.at[slot, place]
        return pltpu.make_async_remote_copy(
            src_ref=ref,
            dst_ref=ref,
            send_sem=self.send_sem.at[slot, pattern],
            recv_sem=self.recv_sem.at[slot, pattern],
            device_id=(self.dp, flipped(self.q, hop)),
            device_id_type=MESH,
        )

    def patterns(self, far):
        return range(1, self.size) if far else range(1, 2)

    def start_own(self, slot, far):
        for pattern in self.patterns(far):
            if pattern & (pattern - 1) == 0:
                self.copy(slot, pattern).start()

    def forward(self, slot):
        for pattern in self.patterns(True):
            if pattern & 1 == 0:
                self.copy(slot, pattern).wait_recv()
                for k in self.order:
                    if k < (pattern & -pattern):
                        self.copy(slot, pattern | k).start()

    def wait_near(self, slot, far):
        for pattern in self.patterns(far):
            if pattern & 1:
                self.copy(slot, pattern).wait_recv()

    def wait_sends(self, slot, far):
        for pattern in self.patterns(far):
            self.copy(slot, pattern).wait_send()


def greet(partners):
    barrier = pltpu.get_barrier_semaphore()
    for partner in partners:
        pl.semaphore_signal(barrier, inc=1, device_id=partner, device_id_type=MESH)
    return lambda: pl.semaphore_wait(barrier, len(partners))


def rank_slots(count_ref, length_ref, perm_s, slen_s, slots):
    count = count_ref[0]
    live = [jnp.where(i < count, length_ref[i], 0) for i in range(slots)]
    ranks = []
    for i in range(slots):
        rank = 0
        for k in range(slots):
            if k != i:
                ahead = live[k] >= live[i] if k < i else live[k] > live[i]
                rank = rank + jnp.where(ahead, 1, 0)
        ranks.append(rank)
    for j in range(slots):
        perm, length = 0, 0
        for i in range(slots):
            here = ranks[i] == j
            perm = perm + jnp.where(here, i, 0)
            length = length + jnp.where(here, live[i], 0)
        perm_s[j] = perm
        slen_s[j] = length


def live_rows(slen_s, slot, first, rows):
    position = first + lax.broadcasted_iota(jnp.int32, (rows, 1), 0)
    return position < slen_s[slot]


def fold8(values):
    rows, lanes = values.shape
    return values.reshape(rows // 8, 8, lanes).sum(axis=0)


def normalize(values):
    center = values - jnp.mean(values, axis=-1, keepdims=True)
    spread = jnp.mean(center * center, axis=-1, keepdims=True)
    inverse = lax.rsqrt(spread + EPSILON)
    return center * inverse, inverse


def norm_back(grad_hat, normal, inverse):
    first = jnp.mean(grad_hat, axis=-1, keepdims=True)
    second = jnp.mean(grad_hat * normal, axis=-1, keepdims=True)
    return inverse * (grad_hat - first - normal * second)


def mix_slot(slot, far, exchange, tables, buf, uv, place):
    rows = exchange.rows
    if far:
        table, block = tables[...], buf[slot]
    else:
        base = aligned(exchange.q // 2 * (2 * rows), 2 * rows)
        table, block = tables[:, pl.ds(base, 2 * rows)], buf[slot, pl.ds(base, 2 * rows), :]
    both = jnp.dot(table, block, preferred_element_type=F32).astype(BF16)
    width = both.shape[1]
    uv[pl.ds(place, rows), :width] = both[:rows]
    uv[pl.ds(place, rows), width:] = both[rows:]


def group_at(i, near_groups, count):
    if near_groups == 0:
        return count - 1 - i
    return jnp.where(i < near_groups, count - near_groups + i, count - 1 - i)


def forward_kernel(cfg, *refs):
    sizes, far_slots, slots, group = cfg
    vec_refs, refs = refs[2:8], refs[:2] + refs[8:]
    (
        count_ref, length_ref, low_hbm, x_hbm, cot_hbm, wi_hbm, wo_hbm, sc_hbm, hc_hbm,
        act_o, dg_o, nrm_o, sum_o, gs_o, gb_o, lo_o, part_o,
        perm_s, slen_s, x_v, cot_v, wi_v, wo_v, sc_v, hc_v, buf, uv, sum_v, nrm_v, act_v, dg_v, gs_v, gb_v, lo_v, br_v, vec_ref,
        load_sem, out_sem, send_sem, recv_sem,
    ) = refs
    rows, _, features = x_v.shape
    wide = wi_v.shape[1]
    seq_total = rows * sizes[1]
    scale = 1.0 / math.sqrt(features * seq_total)
    exchange = Exchange(sizes[1], rows, buf, send_sem, recv_sem)
    q = exchange.q
    first = q * rows
    gain_one, shift_one, bias_out, gain_two, shift_two = (lambda i=i: vec_ref[i : i + 1, :] for i in range(5))
    loads = [
        pltpu.make_async_copy(low_hbm, buf.at[:, pl.ds(aligned(first, rows), rows), :], load_sem.at[0]),
        pltpu.make_async_copy(sc_hbm.at[q], sc_v, load_sem.at[1]),
        pltpu.make_async_copy(hc_hbm, hc_v, load_sem.at[2]),
        pltpu.make_async_copy(x_hbm, x_v, load_sem.at[6]),
        pltpu.make_async_copy(wi_hbm, wi_v, load_sem.at[3]),
        pltpu.make_async_copy(wo_hbm, wo_v, load_sem.at[4]),
        pltpu.make_async_copy(cot_hbm, cot_v, load_sem.at[5]),
    ]
    loads[0].start()
    met = greet([(exchange.dp, flipped(q, k)) for k in exchange.order])
    row = 0
    for vec in vec_refs:
        for i in range(vec.shape[0] // features):
            vec_ref[row : row + 1, :] = vec[pl.ds(i * features, features)].reshape(1, features)
            row += 1
    rank_slots(count_ref, length_ref, perm_s, slen_s, slots)
    for load in loads[1:3]:
        load.start()
    loads[0].wait()
    for load in loads[3:5]:
        load.start()
    met()

    def prepare(i, _):
        slot = jnp.where(i < far_slots, far_slots - 1 - i, i) if far_slots < slots else slots - 1 - i
        pl.when(i < far_slots)(lambda: exchange.start_own(slot, True))
        if far_slots < slots:
            pl.when(i >= far_slots)(lambda: exchange.start_own(slot, False))
        return 0

    lax.fori_loop(0, slots, prepare, 0)
    part_o[...] = jnp.zeros_like(part_o)
    for load in loads[1:3]:
        load.wait()

    batch = group * rows
    span = features
    count = slots // group
    near_groups = (slots - far_slots) // group

    def outs(base):
        place = pl.ds(base, batch)
        early = [
            pltpu.make_async_copy(nrm_v.at[place], nrm_o.at[place], out_sem.at[0]),
            pltpu.make_async_copy(sum_v.at[place], sum_o.at[place], out_sem.at[1]),
        ]
        for n in range(wide // WIDE):
            cut = pl.ds(n * WIDE, WIDE)
            early.append(pltpu.make_async_copy(act_v.at[place, cut], act_o.at[n, place], out_sem.at[4]))
            early.append(pltpu.make_async_copy(dg_v.at[place, cut], dg_o.at[n, place], out_sem.at[5]))
        late = [
            pltpu.make_async_copy(gs_v.at[place], gs_o.at[place], out_sem.at[2]),
            pltpu.make_async_copy(lo_v.at[place], lo_o.at[place], out_sem.at[3]),
            pltpu.make_async_copy(gb_v.at[place], gb_o.at[place], out_sem.at[6]),
        ]
        return early, late

    def bring(slot0):
        for k in reversed(range(group)):
            exchange.forward(slot0 + k)

    def mixing(slot0, far):
        for k in reversed(range(group)):
            exchange.wait_near(slot0 + k, far)
            mix_slot(slot0 + k, far, exchange, sc_v, buf, uv, k * rows)

    def work(i, _):
        slot0 = group_at(i, near_groups, count) * group
        base = aligned(slot0 * rows, batch)
        place = pl.ds(base, batch)
        if near_groups < count:
            pl.when(i >= near_groups)(lambda: mixing(slot0, True))
        if near_groups > 0:
            pl.when(i < near_groups)(lambda: mixing(slot0, False))
        br_v[...] = jnp.dot(uv[...], hc_v[...], preferred_element_type=F32)
        pl.when(i == 0)(loads[3].wait)

        def norm_one(k, _):
            here = pl.ds(aligned(base + k * rows, rows), rows)
            mixed = (br_v[pl.ds(aligned(k * rows, rows), rows), :] * scale).astype(BF16).astype(F32)
            live = live_rows(slen_s, slot0 + k, first, rows)
            total = jnp.where(live, x_v[:, perm_s[slot0 + k], :], 0.0) + mixed
            sum_v[here, :] = total
            hat, _ = normalize(total)
            nrm_v[here, :] = (hat * gain_one() + shift_one()).astype(BF16)
            return 0

        lax.fori_loop(0, group, norm_one, 0)

        @pl.when(i == 0)
        def _():
            loads[4].wait()
            for load in loads[5:]:
                load.start()

        def expand(n, _):
            cut = pl.ds(aligned(n * span, span), span)
            hidden = jnp.dot(nrm_v[place, :], wi_v[:, cut], preferred_element_type=F32) + vec_ref[pl.ds(5 + n, 1), :]
            gate = 0.5 + 0.5 * lax.erf(hidden * math.sqrt(0.5))
            slope = gate + hidden * (jnp.exp(hidden * hidden * -0.5) * (1.0 / math.sqrt(2.0 * math.pi)))
            act_v[place, cut] = (hidden * gate).astype(BF16)
            dg_v[place, cut] = slope.astype(BF16)
            return 0

        lax.fori_loop(0, wide // span, expand, 0)
        for copy in outs(base)[0]:
            copy.start()
        if near_groups < count:

            @pl.when((i + 1 >= near_groups) & (i + 1 < count))
            def _():
                bring(group_at(i + 1, near_groups, count) * group)

        pl.when(i == 0)(loads[5].wait)
        br_v[...] = jnp.dot(act_v[place, :], wo_v[...], preferred_element_type=F32)

        def norm_two(k, _):
            here = pl.ds(aligned(base + k * rows, rows), rows)
            local = pl.ds(aligned(k * rows, rows), rows)
            slot = slot0 + k
            live = live_rows(slen_s, slot, first, rows)
            hat, inverse = normalize(sum_v[here, :] + (br_v[local, :] + bias_out()))
            grad = jnp.where(live, cot_v[:, perm_s[slot], :], 0.0)
            lo_v[here, :] = jnp.where(live, hat * gain_two() + shift_two(), 0.0)
            part_o[0:8, :] = part_o[0:8, :] + fold8(grad * hat)
            part_o[8:16, :] = part_o[8:16, :] + fold8(grad)
            second = norm_back(grad * gain_two(), hat, inverse)
            low = second.astype(BF16)
            gs_v[here, :] = second
            gb_v[here, :] = low
            part_o[16:24, :] = part_o[16:24, :] + fold8(low.astype(F32))
            return 0

        pl.when(i == 0)(loads[6].wait)
        lax.fori_loop(0, group, norm_two, 0)
        for copy in outs(base)[1]:
            copy.start()
        return 0

    if near_groups == 0:
        bring((count - 1) * group)
    lax.fori_loop(0, count, work, 0)

    def finish(slot, _):
        pl.when(slot < far_slots)(lambda: exchange.wait_sends(slot, True))
        if far_slots < slots:
            pl.when(slot >= far_slots)(lambda: exchange.wait_sends(slot, False))
        return 0

    lax.fori_loop(0, slots, finish, 0)

    def flush(g, _):
        for copies in outs(aligned(g * batch, batch)):
            for copy in copies:
                copy.wait()
        return 0

    lax.fori_loop(0, count, flush, 0)


def backward_kernel(cfg, *refs):
    sizes, far_slots, slots, group, parts, mids, lags, plan = cfg
    cube = Cube(sizes, mids)
    S = cube.stages
    (
        count_ref, length_ref, gain_ref, part_ref,
        act_hbm, dg_hbm, nrm_hbm, sum_hbm, gs_hbm, gb_hbm, wi_hbm, wo_hbm, sc_hbm, hc_hbm,
        full_o, ig_o, small_o,
        perm_s, slen_s, gs_v, sum_v, nrm_v, gb_v, gh_v, gn_v, act_v, dg_v, wi_v, wo_v, sc_v, hc_v, buf, uv, ig_v,
        bin_v, one_v, small_v, gain_v, part_v, full,
    ) = refs[:40]
    landed = refs[40 : 40 + S]
    (
        small_recv, load_sem, sum_sem, stream_sem, out_sem, ig_sem, send_sem, recv_sem,
        rs_s, rs_r, ag_s, ag_r, sm_s, sm_r,
    ) = refs[40 + S :]
    ticks, tick_rows, _ = part_v.shape
    message = tick_rows // parts
    chunks = act_hbm.shape[0]
    per_tick = chunks // ticks
    features = nrm_v.shape[1]
    rows = gs_v.shape[0] // slots
    batch = group * rows
    scale = 1.0 / math.sqrt(features * rows * sizes[1])
    exchange = Exchange(sizes[1], rows, buf, send_sem, recv_sem)
    q = exchange.q
    first = q * rows
    loads = [
        pltpu.make_async_copy(gb_hbm, gb_v, load_sem.at[0]),
        pltpu.make_async_copy(nrm_hbm, nrm_v, load_sem.at[1]),
        pltpu.make_async_copy(gs_hbm, gs_v, load_sem.at[2]),
        pltpu.make_async_copy(sc_hbm.at[q], sc_v, load_sem.at[3]),
        pltpu.make_async_copy(hc_hbm, hc_v, load_sem.at[4]),
    ]

    def turn(i):
        return jnp.where(i < far_slots, far_slots - 1 - i, i) if far_slots < slots else slots - 1 - i

    def sum_copy(i):
        place = pl.ds(aligned(turn(i) * rows, rows), rows)
        return pltpu.make_async_copy(sum_hbm.at[place], sum_v.at[lax.rem(i, 2)], sum_sem.at[lax.rem(i, 2)])

    def streams(n, slot):
        cut = pl.ds(aligned(n * WIDE, WIDE), WIDE)
        return [
            pltpu.make_async_copy(act_hbm.at[n], act_v.at[slot], stream_sem.at[0, slot]),
            pltpu.make_async_copy(wo_hbm.at[cut], wo_v.at[slot], stream_sem.at[1, slot]),
            pltpu.make_async_copy(dg_hbm.at[n], dg_v.at[slot], stream_sem.at[2, slot]),
            pltpu.make_async_copy(wi_hbm.at[:, cut], wi_v.at[slot], stream_sem.at[3, slot]),
        ]

    loads[0].start()
    streams(0, 0)[0].start()
    met = greet([cube.partner(bit) for bit in cube.bits])
    rank_slots(count_ref, length_ref, perm_s, slen_s, slots)

    starts = [[j * message + cube.offset(j, level, message) for level in range(S + 1)] for j in range(parts)]

    def rs(m, t, j, s):
        bit = cube.orders[j][s]
        half = message >> (s + 1)
        off = starts[j][s] + (1 - cube.values[bit]) * half
        return pltpu.make_async_remote_copy(
            src_ref=part_v.at[t, pl.ds(aligned(off, 16), half)],
            dst_ref=landed[s].at[m],
            send_sem=rs_s.at[s],
            recv_sem=rs_r.at[s, m],
            device_id=cube.partners[bit],
            device_id_type=MESH,
        )

    def ag(m, t, j, s):
        bit = cube.orders[j][s]
        half = message >> (s + 1)
        ref = full.at[t, pl.ds(aligned(starts[j][s + 1], 16), half)]
        return pltpu.make_async_remote_copy(
            src_ref=ref,
            dst_ref=ref,
            send_sem=ag_s.at[s],
            recv_sem=ag_r.at[s, m],
            device_id=cube.partners[bit],
            device_id_type=MESH,
        )

    def add(m, t, j, s):
        half = message >> (s + 1)
        place = pl.ds(aligned(starts[j][s + 1], 16), half)
        total = part_v[t, place, :].astype(F32) + landed[s][m].astype(F32)
        target = full if s == S - 1 else part_v
        target[t, place, :] = total.astype(BF16)

    def out(t, j):
        place = pl.ds(j * message, message)
        return pltpu.make_async_copy(full.at[t, place], full_o.at[t, place], out_sem.at[t, j])

    def event(k, m, t, j):
        if k == 0:
            rs(m, t, j, 0).start()
        elif k <= S:
            rs(m, t, j, k - 1).wait_recv()
            add(m, t, j, k - 1)
            (rs(m, t, j, k) if k < S else ag(m, t, j, S - 1)).start()
        elif k < 2 * S:
            s = 2 * S - k
            ag(m, t, j, s).wait_recv()
            ag(m, t, j, s - 1).start()
        else:
            ag(m, t, j, 0).wait_recv()
            out(t, j).start()

    def sends_done():
        for s in range(S):
            for sem in (rs_s.at[s], ag_s.at[s]):
                pltpu.make_async_copy(landed[s], landed[s], sem).wait()

    when = [0 if per_tick == 1 and parts == 4 else parts]
    for lag in lags:
        when.append(when[-1] + lag)

    def events(tick, j):
        for k in reversed(range(2 * S + 1)):
            t = tick + (j - when[k]) // parts
            jj = (j - when[k]) % parts
            pl.when((t >= 0) & (t < ticks))(functools.partial(event, k, t * parts + jj, t, jj))

    bin_v[...] = jnp.zeros_like(bin_v)
    one_v[...] = jnp.zeros_like(one_v)
    gain_v[...] = gain_ref[...].reshape(1, features)
    gn_v[...] = jnp.zeros_like(gn_v)
    small_v[...] = jnp.zeros_like(small_v)
    loads[0].wait()
    for copy in streams(0, 0)[1:]:
        copy.start()
    loads[1].start()
    met()

    def load_rest():
        for load in loads[2:]:
            load.start()
        for i in range(2):
            sum_copy(i).start()


    def contract(left, right, dims):
        return lax.dot_general(left, right, ((dims, dims), ((), ())), preferred_element_type=F32)

    def weigh_out(n, slot, t, base):
        streams(n, slot)[0].wait()
        grad = contract(act_v[slot], gb_v[...], (0,)).astype(BF16)
        for i in range(features // LANES):
            part_v[t, pl.ds(base + i * WIDE, WIDE), :] = grad[:, i * LANES : (i + 1) * LANES]

    def pull(n, slot, t, base):
        streams(n, slot)[1].wait()
        streams(n, slot)[2].wait()
        pulled = contract(gb_v[...], wo_v[slot], (1,)) * dg_v[slot].astype(F32)
        pulled = pulled.astype(BF16)
        gh_v[...] = pulled
        bin_v[n] = fold8(pulled.astype(F32))

    def weigh_in(n, slot, t, base):
        pl.when(n == 0)(loads[1].wait)
        grad = contract(nrm_v[...], gh_v[...], (0,)).astype(BF16)
        for i in range(WIDE // LANES):
            place = pl.ds(base + features // LANES * WIDE + i * features, features)
            part_v[t, place, :] = grad[:, i * LANES : (i + 1) * LANES]

    def spread(n, slot, t, base):
        streams(n, slot)[3].wait()
        for i in range(2):
            here = pl.ds(i * (slots // 2) * rows, slots // 2 * rows)
            gn_v[here, :] = gn_v[here, :] + contract(gh_v[here, :], wi_v[slot], (1,))

    steps = [weigh_out, pull, weigh_in, spread]

    def compute(tick, j):
        if per_tick == 1 and parts == 4:
            slot = lax.rem(tick, 2)
            if j == 0:
                for copy in streams(tick + 1, 1 - slot):
                    pl.when(tick + 1 < chunks)(copy.start)
            steps[j](tick, slot, tick, 0)
        elif j == 0:

            def whole(u, _):
                n = tick * per_tick + u
                slot = lax.rem(n, 2)
                for copy in streams(n + 1, 1 - slot):
                    pl.when(n + 1 < chunks)(copy.start)
                for step in steps:
                    step(n, slot, tick, aligned(u * (tick_rows // per_tick), LANES))
                return 0

            lax.fori_loop(0, per_tick, whole, 0)

    def back(i, _):
        slot = turn(i)
        here = pl.ds(aligned(slot * rows, rows), rows)
        pl.when(i == 0)(loads[2].wait)
        sum_copy(i).wait()
        hat, inverse = normalize(sum_v[lax.rem(i, 2)])
        grad = gn_v[here, :]
        one_v[0:8, :] = one_v[0:8, :] + fold8(grad * hat)
        one_v[8:16, :] = one_v[8:16, :] + fold8(grad)
        grad = gs_v[here, :] + norm_back(grad * gain_v[...], hat, inverse)
        gs_v[here, :] = grad
        buf[slot, pl.ds(aligned(first, rows), rows), :] = grad.astype(BF16)
        pl.when(i < far_slots)(lambda: exchange.start_own(slot, True))
        if far_slots < slots:
            pl.when(i >= far_slots)(lambda: exchange.start_own(slot, False))
        pl.when(i + 2 < slots)(lambda: sum_copy(i + 2).start())
        return 0

    def small_copy(s):
        return pltpu.make_async_remote_copy(
            src_ref=small_v.at[s],
            dst_ref=small_recv.at[s],
            send_sem=sm_s.at[s],
            recv_sem=sm_r.at[s],
            device_id=cube.partners[cube.bits[s]],
            device_id_type=MESH,
        )

    def small_start():
        row = 0
        vectors = [one_v[0:8, :], one_v[8:16, :]] + [bin_v[n] for n in range(chunks)]
        vectors += [part_ref[16:24, :], part_ref[0:8, :], part_ref[8:16, :]]
        for vector in vectors:
            vector = jnp.sum(vector, axis=0, keepdims=True)
            for i in range(vector.shape[1] // LANES):
                small_v[0, row : row + 1, :] = vector[:, i * LANES : (i + 1) * LANES]
                row += 1
        small_copy(0).start()

    def small_step(s):
        small_copy(s).wait()
        if s + 1 < S:
            small_v[s + 1] = small_v[s] + small_recv[s]
            small_copy(s + 1).start()
        else:
            small_o[...] = small_v[s] + small_recv[s]

    count = slots // group
    near_groups = (slots - far_slots) // group

    def grad_copy(i):
        base = aligned(group_at(i, near_groups, count) * batch, batch)
        return pltpu.make_async_copy(ig_v.at[lax.rem(i, 2)], ig_o.at[pl.ds(base, batch)], ig_sem.at[lax.rem(i, 2)])

    def mixing(i, k, far):
        slot = group_at(i, near_groups, count) * group + k
        exchange.wait_near(slot, far)
        mix_slot(slot, far, exchange, sc_v, buf, uv, k * rows)

    def hidden_mix(i):
        pl.when(i >= 2)(lambda: grad_copy(i - 2).wait())
        ig_v[lax.rem(i, 2)] = jnp.dot(uv[...], hc_v[...], preferred_element_type=F32)

    def finish(i):
        for k in range(group):
            slot = group_at(i, near_groups, count) * group + k
            here = pl.ds(aligned(slot * rows, rows), rows)
            local = pl.ds(k * rows, rows)
            grad = gs_v[here, :] + ig_v[lax.rem(i, 2), local, :] * scale
            ig_v[lax.rem(i, 2), local, :] = jnp.where(live_rows(slen_s, slot, first, rows), grad, 0.0)
        grad_copy(i).start()

    def bring(i):
        for k in reversed(range(group)):
            exchange.forward(group_at(i, near_groups, count) * group + k)

    small_at, near_at, far_at, lead = plan

    def drain(tick, j):
        d = tick - ticks

        @pl.when(d == 0)
        def _():
            share = -(-slots // parts)
            lax.fori_loop(min(j * share, slots), min((j + 1) * share, slots), back, 0)

        here = lambda at: pl.when(d * parts + j == at)
        if j == small_at % parts:
            here(small_at)(small_start)
        for s in range(S):
            at = small_at + 3 * (s + 1)
            if j == at % parts:
                here(at)(functools.partial(small_step, s))
        if j == 0:

            @pl.when(d == 1)
            def _():
                for load in loads[3:]:
                    load.wait()

        for far, start, low, high in ((False, near_at, 0, near_groups), (True, far_at, near_groups, count)):
            if low == high:
                continue
            i = d - start + low

            @pl.when((i >= low) & (i < high))
            def _():
                subs = [
                    lambda: mixing(i, 0, far),
                    lambda: [mixing(i, k, far) for k in range(1, group)],
                    lambda: hidden_mix(i),
                    lambda: finish(i),
                ]
                for at, sub in enumerate(subs):
                    if min(at, parts - 1) == j:
                        sub()

            if far and j == parts - 1:
                ahead = i + lead
                pl.when((ahead >= low) & (ahead < high))(lambda: bring(ahead))

    last = ticks + max(
        -(-(when[-1] + 1) // parts),
        (small_at + 3 * S) // parts + 1,
        near_at + near_groups,
        far_at + count - near_groups,
    )

    def body(tick, _):
        pl.when(tick == 1)(load_rest)
        for j in range(parts):
            pl.when(tick < ticks)(lambda: compute(tick, j))
            events(tick, j)
            pl.when(tick >= ticks)(lambda: drain(tick, j))
        return 0

    lax.fori_loop(0, last, body, 0)

    def settle(slot, _):
        pl.when(slot < far_slots)(lambda: exchange.wait_sends(slot, True))
        if far_slots < slots:
            pl.when(slot >= far_slots)(lambda: exchange.wait_sends(slot, False))
        return 0

    lax.fori_loop(0, slots, settle, 0)
    for i in range(max(0, count - 2), count):
        grad_copy(i).wait()

    def finish_out(t, _):
        for j in range(parts):
            out(t, j).wait()
        return 0

    lax.fori_loop(0, ticks, finish_out, 0)
    sends_done()


def output_kernel(slots, cuts, places, count_ref, length_ref, full_ref, lo_ref, ig_ref, small_ref, *refs):
    wi_ref, wo_ref, lo_out, ig_out = refs[:4]
    vector_refs, (perm_s, slen_s) = refs[4:-2], refs[-2:]
    step = pl.program_id(0)
    features = wi_ref.shape[0]
    for i in range(features // LANES):
        wo_ref[:, i * LANES : (i + 1) * LANES] = full_ref[0, pl.ds(i * WIDE, WIDE), :].astype(F32)
    for i in range(WIDE // LANES):
        start = features // LANES * WIDE + i * features
        wi_ref[:, i * LANES : (i + 1) * LANES] = full_ref[0, pl.ds(start, features), :].astype(F32)

    @pl.when(step == 0)
    def _():
        rank_slots(count_ref, length_ref, perm_s, slen_s, slots)
        for ref, start in zip(vector_refs, cuts):
            ref[...] = small_ref[start : start + ref.shape[0], :]

    @pl.when(step < places)
    def _():
        for j in range(slots):
            lo_out[:, perm_s[j], :] = lo_ref[j]
            ig_out[:, perm_s[j], :] = ig_ref[j]


ANY = pl.BlockSpec(memory_space=pl.ANY)
SMEM = pl.BlockSpec(memory_space=pltpu.SMEM)
VMEM = pl.BlockSpec(memory_space=pltpu.VMEM)
DMA = pltpu.SemaphoreType.DMA
LAGS = [3, 5, 4, 3, 3, 3, 3, 4, 6, 3]
PLAN = (4, 1, 4, 1)
FAR_PLAN = (4, 1, 4, 1)
MIDS = ((0, 1, 2), (1, 0, 2), (2, 0, 1), (1, 2, 0))
FAR_MIDS = ((1, 2, 0), (2, 1, 0), (1, 0, 2), (2, 0, 1))


def run_forward(sizes, far_slots, slots, *operands, group=2, name="forward", cid=1):
    rows, _, features = operands[9].shape
    wide = operands[11].shape[1]
    seq_total = rows * sizes[1]
    flat, batch, chunks = rows * slots, group * rows, wide // WIDE
    shape = jax.ShapeDtypeStruct
    return pl.pallas_call(
        functools.partial(forward_kernel, (sizes, far_slots, slots, group)),
        name=name,
        out_shape=(
            shape((chunks, flat, WIDE), BF16),
            shape((chunks, flat, WIDE), BF16),
            shape((flat, features), BF16),
            shape((flat, features), F32),
            shape((flat, features), F32),
            shape((flat, features), BF16),
            shape((flat, features), F32),
            shape((24, features), F32),
        ),
        in_specs=[SMEM] * 2 + [VMEM] * 6 + [ANY] * 7,
        out_specs=[ANY] * 7 + [VMEM],
        scratch_shapes=[
            pltpu.SMEM((slots,), jnp.int32),
            pltpu.SMEM((slots,), jnp.int32),
            pltpu.VMEM((rows, slots, features), F32),
            pltpu.VMEM((rows, slots, features), F32),
            pltpu.VMEM((features, wide), BF16),
            pltpu.VMEM((wide, features), BF16),
            pltpu.VMEM((2 * rows, seq_total), BF16),
            pltpu.VMEM((2 * features, features), BF16),
            pltpu.VMEM((slots, seq_total, features), BF16),
            pltpu.VMEM((batch, 2 * features), BF16),
            pltpu.VMEM((flat, features), F32),
            pltpu.VMEM((flat, features), BF16),
            pltpu.VMEM((flat, wide), BF16),
            pltpu.VMEM((flat, wide), BF16),
            pltpu.VMEM((flat, features), F32),
            pltpu.VMEM((flat, features), BF16),
            pltpu.VMEM((flat, features), F32),
            pltpu.VMEM((batch, features), F32),
            pltpu.VMEM((5 + wide // features, features), F32),
            DMA((7,)),
            DMA((7,)),
            DMA((slots, sizes[1])),
            DMA((slots, sizes[1])),
        ],
        compiler_params=pltpu.CompilerParams(collective_id=cid, has_side_effects=True, vmem_limit_bytes=62 << 20),
    )(*operands)


def run_backward(sizes, far_slots, slots, ticks, tick_rows, parts, *operands, group=2, mids=None, lags=None, plan=None, name="backward", cid=2):
    devices = sizes[0] * sizes[1]
    chunks, flat, _ = operands[4].shape
    features, wide = operands[10].shape
    rows = flat // slots
    seq_total = rows * sizes[1]
    batch = group * rows
    message = tick_rows // parts
    shape = jax.ShapeDtypeStruct
    mostly_far = far_slots > slots * 5 // 8
    mids = mids or (FAR_MIDS if mostly_far else MIDS)
    plan = plan or (FAR_PLAN if mostly_far else PLAN)
    lags = lags or LAGS
    stages = devices.bit_length() - 1
    lags = (lags[:stages] + [2] * stages)[:stages] + ([2] * stages + lags[-stages:])[-stages:]
    return pl.pallas_call(
        functools.partial(backward_kernel, (sizes, far_slots, slots, group, parts, mids, lags, plan)),
        name=name,
        out_shape=(
            shape((ticks, tick_rows, LANES), BF16),
            shape((flat, features), F32),
            shape((64, LANES), F32),
        ),
        in_specs=[SMEM] * 2 + [VMEM] * 2 + [ANY] * 10,
        out_specs=[ANY] * 2 + [VMEM],
        scratch_shapes=[
            pltpu.SMEM((slots,), jnp.int32),
            pltpu.SMEM((slots,), jnp.int32),
            pltpu.VMEM((flat, features), F32),
            pltpu.VMEM((2, rows, features), F32),
            pltpu.VMEM((flat, features), BF16),
            pltpu.VMEM((flat, features), BF16),
            pltpu.VMEM((flat, WIDE), BF16),
            pltpu.VMEM((flat, features), F32),
            pltpu.VMEM((2, flat, WIDE), BF16),
            pltpu.VMEM((2, flat, WIDE), BF16),
            pltpu.VMEM((2, features, WIDE), BF16),
            pltpu.VMEM((2, WIDE, features), BF16),
            pltpu.VMEM((2 * rows, seq_total), BF16),
            pltpu.VMEM((2 * features, features), BF16),
            pltpu.VMEM((slots, seq_total, features), BF16),
            pltpu.VMEM((batch, 2 * features), BF16),
            pltpu.VMEM((2, batch, features), F32),
            pltpu.VMEM((chunks, 8, WIDE), F32),
            pltpu.VMEM((16, features), F32),
            pltpu.VMEM((stages, 64, LANES), F32),
            pltpu.VMEM((1, features), F32),
            pltpu.VMEM((ticks, tick_rows, LANES), BF16),
            pltpu.VMEM((ticks, tick_rows, LANES), BF16),
        ]
        + [pltpu.VMEM((ticks * parts, message >> (s + 1), LANES), BF16) for s in range(stages)]
        + [
            pltpu.VMEM((stages, 64, LANES), F32),
            DMA((5,)),
            DMA((2,)),
            DMA((4, 2)),
            DMA((ticks, parts)),
            DMA((2,)),
            DMA((slots, sizes[1])),
            DMA((slots, sizes[1])),
            DMA((stages,)),
            DMA((stages, ticks * parts)),
            DMA((stages,)),
            DMA((stages, ticks * parts)),
            DMA((stages,)),
            DMA((stages,)),
        ],
        compiler_params=pltpu.CompilerParams(collective_id=cid, has_side_effects=True, vmem_limit_bytes=62 << 20),
    )(*operands)


def agree_kernel(
    groups, choices, span, count_ref, length_ref, x_hbm, choice_o, low_o, x_v, low_v, perm_s, slen_s, mine, theirs, load_sem, send_sem, recv_sem
):
    dp, q = lax.axis_index("dp"), lax.axis_index("seq")
    rows, slots, _ = x_v.shape
    load = pltpu.make_async_copy(x_hbm, x_v, load_sem.at[0])
    load.start()

    def peer(i):
        return lax.rem(dp + i, groups)

    def copy(i):
        return pltpu.make_async_remote_copy(
            src_ref=mine,
            dst_ref=theirs.at[i],
            send_sem=send_sem.at[i],
            recv_sem=recv_sem.at[i],
            device_id=(peer(i), q),
            device_id_type=MESH,
        )

    met = greet([(peer(i), q) for i in range(1, groups)])
    far = 0
    for i in range(length_ref.shape[0]):
        far = far + jnp.where((i < count_ref[0]) & (length_ref[i] > span), 1, 0)
    need = jnp.full(mine.shape, far, jnp.int32)
    mine[...] = need.astype(F32)
    theirs[0] = need.astype(F32)
    met()
    for i in range(1, groups):
        copy(i).start()
    rank_slots(count_ref, length_ref, perm_s, slen_s, slots)
    load.wait()
    store = pltpu.make_async_copy(low_v, low_o, load_sem.at[1])

    def prepare(slot, _):
        live = live_rows(slen_s, slot, q * rows, rows)
        low_v[slot] = jnp.where(live, x_v[:, perm_s[slot], :], 0.0).astype(BF16)
        return 0

    lax.fori_loop(0, slots, prepare, 0)
    store.start()
    for i in range(1, groups):
        copy(i).wait()
    most = jnp.max(theirs[...])
    place = 0
    for far in choices[:-1]:
        place = place + jnp.where(most > far, 1, 0)
    choice_o[0] = place
    store.wait()


def cut_messages(devices, chunks, chunk_rows):
    per_tick, parts = min(
        (count, -cut)
        for count in range(1, chunks + 1)
        for cut in range(1, 5)
        if chunks % count == 0 and chunk_rows * count % (devices * 16 * cut) == 0
    )
    return per_tick, -parts


def layer(far_slots, index, sizes, low_input, inputs, item_counts, lengths, vectors, weight_in, weight_out, cotangent, seq_table, hid_table):
    rows, slots, features = inputs.shape
    wide = weight_in.shape[1]
    chunks = wide // WIDE
    chunk_rows = 2 * features * WIDE // LANES
    per_tick, parts = cut_messages(sizes[0] * sizes[1], chunks, chunk_rows)
    act, dg, nrm, summed, second, low, lo, part = run_forward(
        sizes, far_slots, slots,
        item_counts, lengths, *vectors, low_input, inputs, cotangent, weight_in, weight_out, seq_table, hid_table,
        cid=2 * index + 2,
    )
    full, grad, small = run_backward(
        sizes, far_slots, slots, chunks // per_tick, chunk_rows * per_tick, parts,
        item_counts, lengths, vectors[0], part, act, dg, nrm, summed, second, low, weight_in, weight_out, seq_table, hid_table,
        cid=2 * index + 3,
    )
    shape = jax.ShapeDtypeStruct
    places = 1 << min(chunks.bit_length() - 1, 3)
    step = rows // places
    lo, grad = lo.reshape(slots, rows, features), grad.reshape(slots, rows, features)
    heights = [size // LANES for size in (features, features, wide, features, features, features)]
    cuts = [sum(heights[:i]) for i in range(len(heights))]
    slot_first = pl.BlockSpec((slots, step, features), lambda n: (0, jnp.minimum(n, places - 1), 0))
    place_first = pl.BlockSpec((step, slots, features), lambda n: (jnp.minimum(n, places - 1), 0, 0))
    wi_grad, wo_grad, layer_out, input_grad, *vectors = pl.pallas_call(
        functools.partial(output_kernel, slots, cuts, places),
        name="output",
        grid=(chunks,),
        out_shape=(
            shape((features, wide), F32),
            shape((wide, features), F32),
            shape(inputs.shape, F32),
            shape(inputs.shape, F32),
            *(shape((height, LANES), F32) for height in heights),
        ),
        in_specs=[SMEM] * 2 + [pl.BlockSpec((1, chunk_rows, LANES), lambda n: (n, 0, 0))] + [slot_first] * 2 + [VMEM],
        out_specs=(
            pl.BlockSpec((features, WIDE), lambda n: (0, n)),
            pl.BlockSpec((WIDE, features), lambda n: (n, 0)),
            place_first,
            place_first,
            *([VMEM] * len(heights)),
        ),
        scratch_shapes=[pltpu.SMEM((slots,), jnp.int32), pltpu.SMEM((slots,), jnp.int32)],
        compiler_params=pltpu.CompilerParams(vmem_limit_bytes=60 << 20),
    )(item_counts, lengths, full.reshape(chunks, chunk_rows, LANES), lo, grad, small)
    gain_one_grad, shift_one_grad, bias_in_grad, bias_out_grad, gain_two_grad, shift_two_grad = [v.reshape(-1) for v in vectors]
    return (
        layer_out, input_grad, gain_one_grad, shift_one_grad, wi_grad, bias_in_grad, wo_grad, bias_out_grad, gain_two_grad, shift_two_grad,
    )


def per_device(
    inputs, item_counts, lengths, gain_one, shift_one, weight_in, bias_in, weight_out, bias_out, gain_two, shift_two, cotangent
):
    rows, slots, features = inputs.shape
    wide = weight_in.shape[1]
    sizes = (lax.axis_size("dp"), lax.axis_size("seq"))
    seq_total = rows * sizes[1]
    chunks = wide // WIDE
    chunk_rows = 2 * features * WIDE // LANES
    shape = jax.ShapeDtypeStruct

    seq_cos, seq_sin = dft_tables(seq_total)
    hid_cos, hid_sin = dft_tables(features)
    seq_table = [table.reshape(sizes[1], rows, seq_total) for table in (seq_cos, seq_sin)]
    seq_table = jnp.asarray(np.concatenate(seq_table, axis=1).astype(jnp.bfloat16))
    hid_table = jnp.asarray(np.concatenate([hid_cos, -hid_sin], axis=0).astype(jnp.bfloat16))
    vectors = (gain_one, shift_one, bias_out, gain_two, shift_two, bias_in)
    operands = (inputs, item_counts, lengths, vectors, weight_in, weight_out, cotangent, seq_table, hid_table)

    choices = sorted({slots // 2, slots})
    choice, low = pl.pallas_call(
        functools.partial(agree_kernel, sizes[0], choices, 2 * rows),
        name="agree",
        out_shape=(shape((1,), jnp.int32), shape((slots, rows, features), BF16)),
        in_specs=[SMEM] * 2 + [ANY],
        out_specs=(SMEM, ANY),
        scratch_shapes=[
            pltpu.VMEM(inputs.shape, F32),
            pltpu.VMEM((slots, rows, features), BF16),
            pltpu.SMEM((slots,), jnp.int32),
            pltpu.SMEM((slots,), jnp.int32),
            pltpu.VMEM((8, LANES), F32),
            pltpu.VMEM((sizes[0], 8, LANES), F32),
            DMA((2,)),
            DMA((sizes[0],)),
            DMA((sizes[0],)),
        ],
        compiler_params=pltpu.CompilerParams(collective_id=1, has_side_effects=True),
    )(item_counts, lengths, inputs)
    branches = [functools.partial(layer, far, index, sizes) for index, far in enumerate(choices)]

    return lax.switch(choice[0], branches, low, *operands)


def solution(mesh):
    placed = (
        P("seq", "dp", None), P("dp"), P("dp"), P(), P(), P(), P(), P(), P(), P(), P(), P("seq", "dp", None),
    )
    wide = P("seq", "dp", None)
    return jax.shard_map(
        per_device,
        mesh=mesh,
        in_specs=placed,
        out_specs=(wide, wide, P(), P(), P(), P(), P(), P(), P(), P()),
        check_vma=False,
    )
```

```python
import functools
import math

import jax
import jax.numpy as jnp
import numpy as np
from jax import lax
from jax.experimental import pallas as pl
from jax.experimental.pallas import tpu as pltpu
from jax.sharding import PartitionSpec as P

EPSILON = 1e-05
MESH = pl.DeviceIdType.MESH
LANES = 128
WIDE = 512
BF16 = jnp.bfloat16
F32 = jnp.float32


def dft_tables(count):
    index = np.arange(count, dtype=np.int64)
    turns = (index[:, None] * index[None, :] % count).astype(np.float32)
    angle = (turns * np.float32(2.0 * math.pi / count)).astype(np.float64)
    return np.cos(angle).astype(np.float32), np.sin(angle).astype(np.float32)


def aligned(value, step):
    return pl.multiple_of(value, step)


def bit_of(value, k):
    return (value // k) % 2


def flipped(value, k):
    return value + k * (1 - 2 * bit_of(value, k))


def axis_bits(axis, size):
    return [(axis, 1 << b) for b in range(size.bit_length() - 1)]


class Cube:
    def __init__(self, sizes, mids):
        dp, seq = sizes
        bits = axis_bits(1, seq) + axis_bits(0, dp)
        first, near, rest = bits[:1], bits[1:4], bits[4:]
        self.orders = [first + [near[i] for i in mid] + rest for mid in mids]
        self.bits = bits
        self.stages = len(bits)
        self.me = (lax.axis_index("dp"), lax.axis_index("seq"))
        self.values = {bit: self.value(bit) for bit in bits}
        self.partners = {bit: self.partner(bit) for bit in bits}

    def value(self, bit):
        return bit_of(self.me[bit[0]], bit[1])

    def partner(self, bit):
        axis, k = bit
        other = flipped(self.me[axis], k)
        return (other, self.me[1]) if axis == 0 else (self.me[0], other)

    def offset(self, order, level, rows):
        total = 0
        for s in range(level):
            total = total + self.values[self.orders[order][s]] * (rows >> (s + 1))
        return total


class Exchange:
    def __init__(self, size, rows, buf, send, recv):
        self.size, self.rows, self.buf, self.send_sem, self.recv_sem = size, rows, buf, send, recv
        self.dp, self.q = lax.axis_index("dp"), lax.axis_index("seq")
        self.order = [1 << b for b in reversed(range(size.bit_length() - 1))]

    def owner(self, pattern):
        index = self.q
        for k in self.order:
            if pattern & k:
                index = flipped(index, k)
        return index

    def copy(self, slot, pattern):
        hop = pattern & -pattern
        place = pl.ds(aligned(self.owner(pattern - hop) * self.rows, self.rows), self.rows)
        ref = self.buf.at[slot, place]
        return pltpu.make_async_remote_copy(
            src_ref=ref,
            dst_ref=ref,
            send_sem=self.send_sem.at[slot, pattern],
            recv_sem=self.recv_sem.at[slot, pattern],
            device_id=(self.dp, flipped(self.q, hop)),
            device_id_type=MESH,
        )

    def patterns(self, far):
        return range(1, self.size) if far else range(1, 2)

    def start_own(self, slot, far):
        for pattern in self.patterns(far):
            if pattern & (pattern - 1) == 0:
                self.copy(slot, pattern).start()

    def forward(self, slot):
        for pattern in self.patterns(True):
            if pattern & 1 == 0:
                self.copy(slot, pattern).wait_recv()
                for k in self.order:
                    if k < (pattern & -pattern):
                        self.copy(slot, pattern | k).start()

    def wait_near(self, slot, far):
        for pattern in self.patterns(far):
            if pattern & 1:
                self.copy(slot, pattern).wait_recv()

    def wait_sends(self, slot, far):
        for pattern in self.patterns(far):
            self.copy(slot, pattern).wait_send()


def greet(partners):
    barrier = pltpu.get_barrier_semaphore()
    for partner in partners:
        pl.semaphore_signal(barrier, inc=1, device_id=partner, device_id_type=MESH)
    return lambda: pl.semaphore_wait(barrier, len(partners))


def rank_slots(count_ref, length_ref, perm_s, slen_s, slots):
    count = count_ref[0]
    live = [jnp.where(i < count, length_ref[i], 0) for i in range(slots)]
    ranks = []
    for i in range(slots):
        rank = 0
        for k in range(slots):
            if k != i:
                ahead = live[k] >= live[i] if k < i else live[k] > live[i]
                rank = rank + jnp.where(ahead, 1, 0)
        ranks.append(rank)
    for j in range(slots):
        perm, length = 0, 0
        for i in range(slots):
            here = ranks[i] == j
            perm = perm + jnp.where(here, i, 0)
            length = length + jnp.where(here, live[i], 0)
        perm_s[j] = perm
        slen_s[j] = length


def live_rows(slen_s, slot, first, rows):
    position = first + lax.broadcasted_iota(jnp.int32, (rows, 1), 0)
    return position < slen_s[slot]


def fold8(values):
    rows, lanes = values.shape
    return values.reshape(rows // 8, 8, lanes).sum(axis=0)


def normalize(values):
    center = values - jnp.mean(values, axis=-1, keepdims=True)
    spread = jnp.mean(center * center, axis=-1, keepdims=True)
    inverse = lax.rsqrt(spread + EPSILON)
    return center * inverse, inverse


def norm_back(grad_hat, normal, inverse):
    first = jnp.mean(grad_hat, axis=-1, keepdims=True)
    second = jnp.mean(grad_hat * normal, axis=-1, keepdims=True)
    return inverse * (grad_hat - first - normal * second)


def mix_slot(slot, far, exchange, tables, buf, uv, place):
    rows = exchange.rows
    if far:
        table, block = tables[...], buf[slot]
    else:
        base = aligned(exchange.q // 2 * (2 * rows), 2 * rows)
        table, block = tables[:, pl.ds(base, 2 * rows)], buf[slot, pl.ds(base, 2 * rows), :]
    both = jnp.dot(table, block, preferred_element_type=F32).astype(BF16)
    width = both.shape[1]
    uv[pl.ds(place, rows), :width] = both[:rows]
    uv[pl.ds(place, rows), width:] = both[rows:]


def group_at(i, near_groups, count):
    if near_groups == 0:
        return count - 1 - i
    return jnp.where(i < near_groups, count - near_groups + i, count - 1 - i)


def forward_kernel(cfg, *refs):
    sizes, far_slots, slots, group = cfg
    vec_refs, refs = refs[2:8], refs[:2] + refs[8:]
    (
        count_ref, length_ref, low_hbm, x_hbm, cot_hbm, wi_hbm, wo_hbm, sc_hbm, hc_hbm,
        act_o, dg_o, nrm_o, sum_o, gs_o, gb_o, lo_o, part_o,
        perm_s, slen_s, x_v, cot_v, wi_v, wo_v, sc_v, hc_v, buf, uv, sum_v, nrm_v, act_v, dg_v, gs_v, gb_v, lo_v, br_v, vec_ref,
        load_sem, out_sem, send_sem, recv_sem,
    ) = refs
    rows, _, features = x_v.shape
    wide = wi_v.shape[1]
    seq_total = rows * sizes[1]
    scale = 1.0 / math.sqrt(features * seq_total)
    exchange = Exchange(sizes[1], rows, buf, send_sem, recv_sem)
    q = exchange.q
    first = q * rows
    gain_one, shift_one, bias_out, gain_two, shift_two = (lambda i=i: vec_ref[i : i + 1, :] for i in range(5))
    loads = [
        pltpu.make_async_copy(low_hbm, buf.at[:, pl.ds(aligned(first, rows), rows), :], load_sem.at[0]),
        pltpu.make_async_copy(sc_hbm.at[q], sc_v, load_sem.at[1]),
        pltpu.make_async_copy(hc_hbm, hc_v, load_sem.at[2]),
        pltpu.make_async_copy(x_hbm, x_v, load_sem.at[6]),
        pltpu.make_async_copy(wi_hbm, wi_v, load_sem.at[3]),
        pltpu.make_async_copy(wo_hbm, wo_v, load_sem.at[4]),
        pltpu.make_async_copy(cot_hbm, cot_v, load_sem.at[5]),
    ]
    loads[0].start()
    met = greet([(exchange.dp, flipped(q, k)) for k in exchange.order])
    row = 0
    for vec in vec_refs:
        for i in range(vec.shape[0] // features):
            vec_ref[row : row + 1, :] = vec[pl.ds(i * features, features)].reshape(1, features)
            row += 1
    rank_slots(count_ref, length_ref, perm_s, slen_s, slots)
    for load in loads[1:3]:
        load.start()
    loads[0].wait()
    for load in loads[3:5]:
        load.start()
    met()

    def prepare(i, _):
        slot = jnp.where(i < far_slots, far_slots - 1 - i, i) if far_slots < slots else slots - 1 - i
        pl.when(i < far_slots)(lambda: exchange.start_own(slot, True))
        if far_slots < slots:
            pl.when(i >= far_slots)(lambda: exchange.start_own(slot, False))
        return 0

    lax.fori_loop(0, slots, prepare, 0)
    part_o[...] = jnp.zeros_like(part_o)
    for load in loads[1:3]:
        load.wait()

    batch = group * rows
    span = features
    count = slots // group
    near_groups = (slots - far_slots) // group

    def outs(base):
        place = pl.ds(base, batch)
        early = [
            pltpu.make_async_copy(nrm_v.at[place], nrm_o.at[place], out_sem.at[0]),
            pltpu.make_async_copy(sum_v.at[place], sum_o.at[place], out_sem.at[1]),
        ]
        for n in range(wide // WIDE):
            cut = pl.ds(n * WIDE, WIDE)
            early.append(pltpu.make_async_copy(act_v.at[place, cut], act_o.at[n, place], out_sem.at[4]))
            early.append(pltpu.make_async_copy(dg_v.at[place, cut], dg_o.at[n, place], out_sem.at[5]))
        late = [
            pltpu.make_async_copy(gs_v.at[place], gs_o.at[place], out_sem.at[2]),
            pltpu.make_async_copy(lo_v.at[place], lo_o.at[place], out_sem.at[3]),
            pltpu.make_async_copy(gb_v.at[place], gb_o.at[place], out_sem.at[6]),
        ]
        return early, late

    def bring(slot0):
        for k in reversed(range(group)):
            exchange.forward(slot0 + k)

    def mixing(slot0, far):
        for k in reversed(range(group)):
            exchange.wait_near(slot0 + k, far)
            mix_slot(slot0 + k, far, exchange, sc_v, buf, uv, k * rows)

    def work(i, _):
        slot0 = group_at(i, near_groups, count) * group
        base = aligned(slot0 * rows, batch)
        place = pl.ds(base, batch)
        if near_groups < count:
            pl.when(i >= near_groups)(lambda: mixing(slot0, True))
        if near_groups > 0:
            pl.when(i < near_groups)(lambda: mixing(slot0, False))
        br_v[...] = jnp.dot(uv[...], hc_v[...], preferred_element_type=F32)
        pl.when(i == 0)(loads[3].wait)

        def norm_one(k, _):
            here = pl.ds(aligned(base + k * rows, rows), rows)
            mixed = (br_v[pl.ds(aligned(k * rows, rows), rows), :] * scale).astype(BF16).astype(F32)
            live = live_rows(slen_s, slot0 + k, first, rows)
            total = jnp.where(live, x_v[:, perm_s[slot0 + k], :], 0.0) + mixed
            sum_v[here, :] = total
            hat, _ = normalize(total)
            nrm_v[here, :] = (hat * gain_one() + shift_one()).astype(BF16)
            return 0

        lax.fori_loop(0, group, norm_one, 0)

        @pl.when(i == 0)
        def _():
            loads[4].wait()
            for load in loads[5:]:
                load.start()

        def expand(n, _):
            cut = pl.ds(aligned(n * span, span), span)
            hidden = jnp.dot(nrm_v[place, :], wi_v[:, cut], preferred_element_type=F32) + vec_ref[pl.ds(5 + n, 1), :]
            gate = 0.5 + 0.5 * lax.erf(hidden * math.sqrt(0.5))
            slope = gate + hidden * (jnp.exp(hidden * hidden * -0.5) * (1.0 / math.sqrt(2.0 * math.pi)))
            act_v[place, cut] = (hidden * gate).astype(BF16)
            dg_v[place, cut] = slope.astype(BF16)
            return 0

        lax.fori_loop(0, wide // span, expand, 0)
        for copy in outs(base)[0]:
            copy.start()
        if near_groups < count:

            @pl.when((i + 1 >= near_groups) & (i + 1 < count))
            def _():
                bring(group_at(i + 1, near_groups, count) * group)

        pl.when(i == 0)(loads[5].wait)
        br_v[...] = jnp.dot(act_v[place, :], wo_v[...], preferred_element_type=F32)

        def norm_two(k, _):
            here = pl.ds(aligned(base + k * rows, rows), rows)
            local = pl.ds(aligned(k * rows, rows), rows)
            slot = slot0 + k
            live = live_rows(slen_s, slot, first, rows)
            hat, inverse = normalize(sum_v[here, :] + (br_v[local, :] + bias_out()))
            grad = jnp.where(live, cot_v[:, perm_s[slot], :], 0.0)
            lo_v[here, :] = jnp.where(live, hat * gain_two() + shift_two(), 0.0).astype(BF16)
            part_o[0:8, :] = part_o[0:8, :] + fold8(grad * hat)
            part_o[8:16, :] = part_o[8:16, :] + fold8(grad)
            second = norm_back(grad * gain_two(), hat, inverse)
            low = second.astype(BF16)
            gs_v[here, :] = second
            gb_v[here, :] = low
            part_o[16:24, :] = part_o[16:24, :] + fold8(low.astype(F32))
            return 0

        pl.when(i == 0)(loads[6].wait)
        lax.fori_loop(0, group, norm_two, 0)
        for copy in outs(base)[1]:
            copy.start()
        return 0

    if near_groups == 0:
        bring((count - 1) * group)
    lax.fori_loop(0, count, work, 0)

    def finish(slot, _):
        pl.when(slot < far_slots)(lambda: exchange.wait_sends(slot, True))
        if far_slots < slots:
            pl.when(slot >= far_slots)(lambda: exchange.wait_sends(slot, False))
        return 0

    lax.fori_loop(0, slots, finish, 0)

    def flush(g, _):
        for copies in outs(aligned(g * batch, batch)):
            for copy in copies:
                copy.wait()
        return 0

    lax.fori_loop(0, count, flush, 0)


def backward_kernel(cfg, *refs):
    sizes, far_slots, slots, group, parts, mids, lags, plan = cfg
    cube = Cube(sizes, mids)
    S = cube.stages
    (
        count_ref, length_ref, gain_ref, part_ref,
        act_hbm, dg_hbm, nrm_hbm, sum_hbm, gs_hbm, gb_hbm, wi_hbm, wo_hbm, sc_hbm, hc_hbm,
        full_o, ig_o, small_o,
        perm_s, slen_s, gs_v, sum_v, nrm_v, gb_v, gh_v, gn_v, act_v, dg_v, wi_v, wo_v, sc_v, hc_v, buf, uv, mix_v, ig_v,
        bin_v, one_v, small_v, gain_v, part_v, full,
    ) = refs[:41]
    landed = refs[41 : 41 + S]
    (
        small_recv, load_sem, sum_sem, stream_sem, out_sem, ig_sem, send_sem, recv_sem,
        rs_s, rs_r, ag_s, ag_r, sm_s, sm_r,
    ) = refs[41 + S :]
    ticks, tick_rows, _ = part_v.shape
    message = tick_rows // parts
    chunks = act_hbm.shape[0]
    per_tick = chunks // ticks
    features = nrm_v.shape[1]
    rows = gs_v.shape[0] // slots
    batch = group * rows
    scale = 1.0 / math.sqrt(features * rows * sizes[1])
    exchange = Exchange(sizes[1], rows, buf, send_sem, recv_sem)
    q = exchange.q
    first = q * rows
    loads = [
        pltpu.make_async_copy(gb_hbm, gb_v, load_sem.at[0]),
        pltpu.make_async_copy(nrm_hbm, nrm_v, load_sem.at[1]),
        pltpu.make_async_copy(gs_hbm, gs_v, load_sem.at[2]),
        pltpu.make_async_copy(sc_hbm.at[q], sc_v, load_sem.at[3]),
        pltpu.make_async_copy(hc_hbm, hc_v, load_sem.at[4]),
    ]

    def turn(i):
        return jnp.where(i < far_slots, far_slots - 1 - i, i) if far_slots < slots else slots - 1 - i

    def sum_copy(i):
        place = pl.ds(aligned(turn(i) * rows, rows), rows)
        return pltpu.make_async_copy(sum_hbm.at[place], sum_v.at[lax.rem(i, 2)], sum_sem.at[lax.rem(i, 2)])

    def streams(n, slot):
        cut = pl.ds(aligned(n * WIDE, WIDE), WIDE)
        return [
            pltpu.make_async_copy(act_hbm.at[n], act_v.at[slot], stream_sem.at[0, slot]),
            pltpu.make_async_copy(wo_hbm.at[cut], wo_v.at[slot], stream_sem.at[1, slot]),
            pltpu.make_async_copy(dg_hbm.at[n], dg_v.at[slot], stream_sem.at[2, slot]),
            pltpu.make_async_copy(wi_hbm.at[:, cut], wi_v.at[slot], stream_sem.at[3, slot]),
        ]

    loads[0].start()
    streams(0, 0)[0].start()
    met = greet([cube.partner(bit) for bit in cube.bits])
    rank_slots(count_ref, length_ref, perm_s, slen_s, slots)

    starts = [[j * message + cube.offset(j, level, message) for level in range(S + 1)] for j in range(parts)]

    def rs(m, t, j, s):
        bit = cube.orders[j][s]
        half = message >> (s + 1)
        off = starts[j][s] + (1 - cube.values[bit]) * half
        return pltpu.make_async_remote_copy(
            src_ref=part_v.at[t, pl.ds(aligned(off, 16), half)],
            dst_ref=landed[s].at[m],
            send_sem=rs_s.at[s],
            recv_sem=rs_r.at[s, m],
            device_id=cube.partners[bit],
            device_id_type=MESH,
        )

    def ag(m, t, j, s):
        bit = cube.orders[j][s]
        half = message >> (s + 1)
        ref = full.at[t, pl.ds(aligned(starts[j][s + 1], 16), half)]
        return pltpu.make_async_remote_copy(
            src_ref=ref,
            dst_ref=ref,
            send_sem=ag_s.at[s],
            recv_sem=ag_r.at[s, m],
            device_id=cube.partners[bit],
            device_id_type=MESH,
        )

    def add(m, t, j, s):
        half = message >> (s + 1)
        place = pl.ds(aligned(starts[j][s + 1], 16), half)
        total = part_v[t, place, :].astype(F32) + landed[s][m].astype(F32)
        target = full if s == S - 1 else part_v
        target[t, place, :] = total.astype(BF16)

    def out(t, j):
        place = pl.ds(j * message, message)
        return pltpu.make_async_copy(full.at[t, place], full_o.at[t, place], out_sem.at[t, j])

    def event(k, m, t, j):
        if k == 0:
            rs(m, t, j, 0).start()
        elif k <= S:
            rs(m, t, j, k - 1).wait_recv()
            add(m, t, j, k - 1)
            (rs(m, t, j, k) if k < S else ag(m, t, j, S - 1)).start()
        elif k < 2 * S:
            s = 2 * S - k
            ag(m, t, j, s).wait_recv()
            ag(m, t, j, s - 1).start()
        else:
            ag(m, t, j, 0).wait_recv()
            out(t, j).start()

    def sends_done():
        for s in range(S):
            for sem in (rs_s.at[s], ag_s.at[s]):
                pltpu.make_async_copy(landed[s], landed[s], sem).wait()

    when = [0 if per_tick == 1 and parts == 4 else parts]
    for lag in lags:
        when.append(when[-1] + lag)

    def events(tick, j):
        for k in reversed(range(2 * S + 1)):
            t = tick + (j - when[k]) // parts
            jj = (j - when[k]) % parts
            pl.when((t >= 0) & (t < ticks))(functools.partial(event, k, t * parts + jj, t, jj))

    bin_v[...] = jnp.zeros_like(bin_v)
    one_v[...] = jnp.zeros_like(one_v)
    gain_v[...] = gain_ref[...].reshape(1, features)
    gn_v[...] = jnp.zeros_like(gn_v)
    small_v[...] = jnp.zeros_like(small_v)
    loads[0].wait()
    for copy in streams(0, 0)[1:]:
        copy.start()
    loads[1].start()
    met()

    def load_rest():
        for load in loads[2:]:
            load.start()
        for i in range(2):
            sum_copy(i).start()


    def contract(left, right, dims):
        return lax.dot_general(left, right, ((dims, dims), ((), ())), preferred_element_type=F32)

    def weigh_out(n, slot, t, base):
        streams(n, slot)[0].wait()
        grad = contract(act_v[slot], gb_v[...], (0,)).astype(BF16)
        for i in range(features // LANES):
            part_v[t, pl.ds(base + i * WIDE, WIDE), :] = grad[:, i * LANES : (i + 1) * LANES]

    def pull(n, slot, t, base):
        streams(n, slot)[1].wait()
        streams(n, slot)[2].wait()
        pulled = contract(gb_v[...], wo_v[slot], (1,)) * dg_v[slot].astype(F32)
        pulled = pulled.astype(BF16)
        gh_v[...] = pulled
        bin_v[n] = fold8(pulled.astype(F32))

    def weigh_in(n, slot, t, base):
        pl.when(n == 0)(loads[1].wait)
        grad = contract(nrm_v[...], gh_v[...], (0,)).astype(BF16)
        for i in range(WIDE // LANES):
            place = pl.ds(base + features // LANES * WIDE + i * features, features)
            part_v[t, place, :] = grad[:, i * LANES : (i + 1) * LANES]

    def spread(n, slot, t, base):
        streams(n, slot)[3].wait()
        for i in range(2):
            here = pl.ds(i * (slots // 2) * rows, slots // 2 * rows)
            gn_v[here, :] = gn_v[here, :] + contract(gh_v[here, :], wi_v[slot], (1,))

    steps = [weigh_out, pull, weigh_in, spread]

    def compute(tick, j):
        if per_tick == 1 and parts == 4:
            slot = lax.rem(tick, 2)
            if j == 0:
                for copy in streams(tick + 1, 1 - slot):
                    pl.when(tick + 1 < chunks)(copy.start)
            steps[j](tick, slot, tick, 0)
        elif j == 0:

            def whole(u, _):
                n = tick * per_tick + u
                slot = lax.rem(n, 2)
                for copy in streams(n + 1, 1 - slot):
                    pl.when(n + 1 < chunks)(copy.start)
                for step in steps:
                    step(n, slot, tick, aligned(u * (tick_rows // per_tick), LANES))
                return 0

            lax.fori_loop(0, per_tick, whole, 0)

    def back(i, _):
        slot = turn(i)
        here = pl.ds(aligned(slot * rows, rows), rows)
        pl.when(i == 0)(loads[2].wait)
        sum_copy(i).wait()
        hat, inverse = normalize(sum_v[lax.rem(i, 2)])
        grad = gn_v[here, :]
        one_v[0:8, :] = one_v[0:8, :] + fold8(grad * hat)
        one_v[8:16, :] = one_v[8:16, :] + fold8(grad)
        grad = gs_v[here, :] + norm_back(grad * gain_v[...], hat, inverse)
        gs_v[here, :] = grad
        buf[slot, pl.ds(aligned(first, rows), rows), :] = grad.astype(BF16)
        pl.when(i < far_slots)(lambda: exchange.start_own(slot, True))
        if far_slots < slots:
            pl.when(i >= far_slots)(lambda: exchange.start_own(slot, False))
        pl.when(i + 2 < slots)(lambda: sum_copy(i + 2).start())
        return 0

    def small_copy(s):
        return pltpu.make_async_remote_copy(
            src_ref=small_v.at[s],
            dst_ref=small_recv.at[s],
            send_sem=sm_s.at[s],
            recv_sem=sm_r.at[s],
            device_id=cube.partners[cube.bits[s]],
            device_id_type=MESH,
        )

    def small_start():
        row = 0
        vectors = [one_v[0:8, :], one_v[8:16, :]] + [bin_v[n] for n in range(chunks)]
        vectors += [part_ref[16:24, :], part_ref[0:8, :], part_ref[8:16, :]]
        for vector in vectors:
            vector = jnp.sum(vector, axis=0, keepdims=True)
            for i in range(vector.shape[1] // LANES):
                small_v[0, row : row + 1, :] = vector[:, i * LANES : (i + 1) * LANES]
                row += 1
        small_copy(0).start()

    def small_step(s):
        small_copy(s).wait()
        if s + 1 < S:
            small_v[s + 1] = small_v[s] + small_recv[s]
            small_copy(s + 1).start()
        else:
            small_o[...] = small_v[s] + small_recv[s]

    count = slots // group
    near_groups = (slots - far_slots) // group

    def grad_copy(i):
        base = aligned(group_at(i, near_groups, count) * batch, batch)
        return pltpu.make_async_copy(ig_v.at[lax.rem(i, 2)], ig_o.at[pl.ds(base, batch)], ig_sem.at[lax.rem(i, 2)])

    def mixing(i, k, far):
        slot = group_at(i, near_groups, count) * group + k
        exchange.wait_near(slot, far)
        mix_slot(slot, far, exchange, sc_v, buf, uv, k * rows)

    def hidden_mix(i):
        pl.when(i >= 2)(lambda: grad_copy(i - 2).wait())
        mix_v[...] = jnp.dot(uv[...], hc_v[...], preferred_element_type=F32)

    def finish(i):
        for k in range(group):
            slot = group_at(i, near_groups, count) * group + k
            here = pl.ds(aligned(slot * rows, rows), rows)
            local = pl.ds(k * rows, rows)
            grad = gs_v[here, :] + mix_v[local, :] * scale
            grad = jnp.where(live_rows(slen_s, slot, first, rows), grad, 0.0)
            ig_v[lax.rem(i, 2), local, :] = grad.astype(BF16)
        grad_copy(i).start()

    def bring(i):
        for k in reversed(range(group)):
            exchange.forward(group_at(i, near_groups, count) * group + k)

    small_at, near_at, far_at, lead = plan

    def drain(tick, j):
        d = tick - ticks

        @pl.when(d == 0)
        def _():
            share = -(-slots // parts)
            lax.fori_loop(min(j * share, slots), min((j + 1) * share, slots), back, 0)

        here = lambda at: pl.when(d * parts + j == at)
        if j == small_at % parts:
            here(small_at)(small_start)
        for s in range(S):
            at = small_at + 3 * (s + 1)
            if j == at % parts:
                here(at)(functools.partial(small_step, s))
        if j == 0:

            @pl.when(d == 1)
            def _():
                for load in loads[3:]:
                    load.wait()

        for far, start, low, high in ((False, near_at, 0, near_groups), (True, far_at, near_groups, count)):
            if low == high:
                continue
            i = d - start + low

            @pl.when((i >= low) & (i < high))
            def _():
                subs = [
                    lambda: mixing(i, 0, far),
                    lambda: [mixing(i, k, far) for k in range(1, group)],
                    lambda: hidden_mix(i),
                    lambda: finish(i),
                ]
                for at, sub in enumerate(subs):
                    if min(at, parts - 1) == j:
                        sub()

            if far and j == parts - 1:
                ahead = i + lead
                pl.when((ahead >= low) & (ahead < high))(lambda: bring(ahead))

    last = ticks + max(
        -(-(when[-1] + 1) // parts),
        (small_at + 3 * S) // parts + 1,
        near_at + near_groups,
        far_at + count - near_groups,
    )

    def body(tick, _):
        pl.when(tick == 1)(load_rest)
        for j in range(parts):
            pl.when(tick < ticks)(lambda: compute(tick, j))
            events(tick, j)
            pl.when(tick >= ticks)(lambda: drain(tick, j))
        return 0

    lax.fori_loop(0, last, body, 0)

    def settle(slot, _):
        pl.when(slot < far_slots)(lambda: exchange.wait_sends(slot, True))
        if far_slots < slots:
            pl.when(slot >= far_slots)(lambda: exchange.wait_sends(slot, False))
        return 0

    lax.fori_loop(0, slots, settle, 0)
    for i in range(max(0, count - 2), count):
        grad_copy(i).wait()

    def finish_out(t, _):
        for j in range(parts):
            out(t, j).wait()
        return 0

    lax.fori_loop(0, ticks, finish_out, 0)
    sends_done()


def output_kernel(slots, cuts, places, count_ref, length_ref, full_ref, lo_ref, ig_ref, small_ref, *refs):
    wi_ref, wo_ref, lo_out, ig_out = refs[:4]
    vector_refs, (perm_s, slen_s) = refs[4:-2], refs[-2:]
    step = pl.program_id(0)
    features = wi_ref.shape[0]
    for u in range(full_ref.shape[0]):
        base = u * WIDE
        for i in range(features // LANES):
            wo_ref[base : base + WIDE, i * LANES : (i + 1) * LANES] = full_ref[u, pl.ds(i * WIDE, WIDE), :].astype(F32)
        for i in range(WIDE // LANES):
            start = features // LANES * WIDE + i * features
            wi_ref[:, base + i * LANES : base + (i + 1) * LANES] = full_ref[u, pl.ds(start, features), :].astype(F32)

    @pl.when(step == 0)
    def _():
        rank_slots(count_ref, length_ref, perm_s, slen_s, slots)
        for ref, start in zip(vector_refs, cuts):
            ref[...] = small_ref[start : start + ref.shape[0], :]

    @pl.when(step < places)
    def _():
        for j in range(slots):
            lo_out[:, perm_s[j], :] = lo_ref[j].astype(F32)
            ig_out[:, perm_s[j], :] = ig_ref[j].astype(F32)


ANY = pl.BlockSpec(memory_space=pl.ANY)
SMEM = pl.BlockSpec(memory_space=pltpu.SMEM)
VMEM = pl.BlockSpec(memory_space=pltpu.VMEM)
DMA = pltpu.SemaphoreType.DMA
LAGS = [3, 5, 4, 3, 3, 3, 3, 4, 6, 3]
PLAN = (4, 1, 4, 1)
FAR_PLAN = (4, 1, 4, 1)
MIDS = ((0, 1, 2), (1, 0, 2), (2, 0, 1), (1, 2, 0))
FAR_MIDS = ((1, 2, 0), (2, 1, 0), (1, 0, 2), (2, 0, 1))


def run_forward(sizes, far_slots, slots, *operands, group=2, name="forward", cid=1):
    rows, _, features = operands[9].shape
    wide = operands[11].shape[1]
    seq_total = rows * sizes[1]
    flat, batch, chunks = rows * slots, group * rows, wide // WIDE
    shape = jax.ShapeDtypeStruct
    return pl.pallas_call(
        functools.partial(forward_kernel, (sizes, far_slots, slots, group)),
        name=name,
        out_shape=(
            shape((chunks, flat, WIDE), BF16),
            shape((chunks, flat, WIDE), BF16),
            shape((flat, features), BF16),
            shape((flat, features), F32),
            shape((flat, features), F32),
            shape((flat, features), BF16),
            shape((flat, features), BF16),
            shape((24, features), F32),
        ),
        in_specs=[SMEM] * 2 + [VMEM] * 6 + [ANY] * 7,
        out_specs=[ANY] * 7 + [VMEM],
        scratch_shapes=[
            pltpu.SMEM((slots,), jnp.int32),
            pltpu.SMEM((slots,), jnp.int32),
            pltpu.VMEM((rows, slots, features), F32),
            pltpu.VMEM((rows, slots, features), F32),
            pltpu.VMEM((features, wide), BF16),
            pltpu.VMEM((wide, features), BF16),
            pltpu.VMEM((2 * rows, seq_total), BF16),
            pltpu.VMEM((2 * features, features), BF16),
            pltpu.VMEM((slots, seq_total, features), BF16),
            pltpu.VMEM((batch, 2 * features), BF16),
            pltpu.VMEM((flat, features), F32),
            pltpu.VMEM((flat, features), BF16),
            pltpu.VMEM((flat, wide), BF16),
            pltpu.VMEM((flat, wide), BF16),
            pltpu.VMEM((flat, features), F32),
            pltpu.VMEM((flat, features), BF16),
            pltpu.VMEM((flat, features), BF16),
            pltpu.VMEM((batch, features), F32),
            pltpu.VMEM((5 + wide // features, features), F32),
            DMA((7,)),
            DMA((7,)),
            DMA((slots, sizes[1])),
            DMA((slots, sizes[1])),
        ],
        compiler_params=pltpu.CompilerParams(collective_id=cid, has_side_effects=True, vmem_limit_bytes=62 << 20),
    )(*operands)


def run_backward(sizes, far_slots, slots, ticks, tick_rows, parts, *operands, group=2, mids=None, lags=None, plan=None, name="backward", cid=2):
    devices = sizes[0] * sizes[1]
    chunks, flat, _ = operands[4].shape
    features, wide = operands[10].shape
    rows = flat // slots
    seq_total = rows * sizes[1]
    batch = group * rows
    message = tick_rows // parts
    shape = jax.ShapeDtypeStruct
    mostly_far = far_slots > slots * 5 // 8
    mids = mids or (FAR_MIDS if mostly_far else MIDS)
    plan = plan or (FAR_PLAN if mostly_far else PLAN)
    lags = lags or LAGS
    stages = devices.bit_length() - 1
    lags = (lags[:stages] + [2] * stages)[:stages] + ([2] * stages + lags[-stages:])[-stages:]
    return pl.pallas_call(
        functools.partial(backward_kernel, (sizes, far_slots, slots, group, parts, mids, lags, plan)),
        name=name,
        out_shape=(
            shape((ticks, tick_rows, LANES), BF16),
            shape((flat, features), BF16),
            shape((64, LANES), F32),
        ),
        in_specs=[SMEM] * 2 + [VMEM] * 2 + [ANY] * 10,
        out_specs=[ANY] * 2 + [VMEM],
        scratch_shapes=[
            pltpu.SMEM((slots,), jnp.int32),
            pltpu.SMEM((slots,), jnp.int32),
            pltpu.VMEM((flat, features), F32),
            pltpu.VMEM((2, rows, features), F32),
            pltpu.VMEM((flat, features), BF16),
            pltpu.VMEM((flat, features), BF16),
            pltpu.VMEM((flat, WIDE), BF16),
            pltpu.VMEM((flat, features), F32),
            pltpu.VMEM((2, flat, WIDE), BF16),
            pltpu.VMEM((2, flat, WIDE), BF16),
            pltpu.VMEM((2, features, WIDE), BF16),
            pltpu.VMEM((2, WIDE, features), BF16),
            pltpu.VMEM((2 * rows, seq_total), BF16),
            pltpu.VMEM((2 * features, features), BF16),
            pltpu.VMEM((slots, seq_total, features), BF16),
            pltpu.VMEM((batch, 2 * features), BF16),
            pltpu.VMEM((batch, features), F32),
            pltpu.VMEM((2, batch, features), BF16),
            pltpu.VMEM((chunks, 8, WIDE), F32),
            pltpu.VMEM((16, features), F32),
            pltpu.VMEM((stages, 64, LANES), F32),
            pltpu.VMEM((1, features), F32),
            pltpu.VMEM((ticks, tick_rows, LANES), BF16),
            pltpu.VMEM((ticks, tick_rows, LANES), BF16),
        ]
        + [pltpu.VMEM((ticks * parts, message >> (s + 1), LANES), BF16) for s in range(stages)]
        + [
            pltpu.VMEM((stages, 64, LANES), F32),
            DMA((5,)),
            DMA((2,)),
            DMA((4, 2)),
            DMA((ticks, parts)),
            DMA((2,)),
            DMA((slots, sizes[1])),
            DMA((slots, sizes[1])),
            DMA((stages,)),
            DMA((stages, ticks * parts)),
            DMA((stages,)),
            DMA((stages, ticks * parts)),
            DMA((stages,)),
            DMA((stages,)),
        ],
        compiler_params=pltpu.CompilerParams(collective_id=cid, has_side_effects=True, vmem_limit_bytes=62 << 20),
    )(*operands)


def agree_kernel(
    groups, choices, span, count_ref, length_ref, x_hbm, choice_o, low_o, x_v, low_v, perm_s, slen_s, mine, theirs, load_sem, send_sem, recv_sem
):
    dp, q = lax.axis_index("dp"), lax.axis_index("seq")
    rows, slots, _ = x_v.shape
    load = pltpu.make_async_copy(x_hbm, x_v, load_sem.at[0])
    load.start()

    def peer(i):
        return lax.rem(dp + i, groups)

    def copy(i):
        return pltpu.make_async_remote_copy(
            src_ref=mine,
            dst_ref=theirs.at[i],
            send_sem=send_sem.at[i],
            recv_sem=recv_sem.at[i],
            device_id=(peer(i), q),
            device_id_type=MESH,
        )

    met = greet([(peer(i), q) for i in range(1, groups)])
    far = 0
    for i in range(length_ref.shape[0]):
        far = far + jnp.where((i < count_ref[0]) & (length_ref[i] > span), 1, 0)
    need = jnp.full(mine.shape, far, jnp.int32)
    mine[...] = need.astype(F32)
    theirs[0] = need.astype(F32)
    met()
    for i in range(1, groups):
        copy(i).start()
    rank_slots(count_ref, length_ref, perm_s, slen_s, slots)
    load.wait()
    store = pltpu.make_async_copy(low_v, low_o, load_sem.at[1])

    def prepare(slot, _):
        live = live_rows(slen_s, slot, q * rows, rows)
        low_v[slot] = jnp.where(live, x_v[:, perm_s[slot], :], 0.0).astype(BF16)
        return 0

    lax.fori_loop(0, slots, prepare, 0)
    store.start()
    for i in range(1, groups):
        copy(i).wait()
    most = jnp.max(theirs[...])
    place = 0
    for far in choices[:-1]:
        place = place + jnp.where(most > far, 1, 0)
    choice_o[0] = place
    store.wait()


def cut_messages(devices, chunks, chunk_rows):
    per_tick, parts = min(
        (count, -cut)
        for count in range(1, chunks + 1)
        for cut in range(1, 5)
        if chunks % count == 0 and chunk_rows * count % (devices * 16 * cut) == 0
    )
    return per_tick, -parts


def layer(far_slots, index, sizes, low_input, inputs, item_counts, lengths, vectors, weight_in, weight_out, cotangent, seq_table, hid_table):
    rows, slots, features = inputs.shape
    wide = weight_in.shape[1]
    chunks = wide // WIDE
    chunk_rows = 2 * features * WIDE // LANES
    per_tick, parts = cut_messages(sizes[0] * sizes[1], chunks, chunk_rows)
    act, dg, nrm, summed, second, low, lo, part = run_forward(
        sizes, far_slots, slots,
        item_counts, lengths, *vectors, low_input, inputs, cotangent, weight_in, weight_out, seq_table, hid_table,
        cid=2 * index + 2,
    )
    full, grad, small = run_backward(
        sizes, far_slots, slots, chunks // per_tick, chunk_rows * per_tick, parts,
        item_counts, lengths, vectors[0], part, act, dg, nrm, summed, second, low, weight_in, weight_out, seq_table, hid_table,
        cid=2 * index + 3,
    )
    shape = jax.ShapeDtypeStruct
    side = 2 if chunks % 2 == 0 else 1
    places = 1 << min((chunks // side).bit_length() - 1, 3)
    step = rows // places
    lo, grad = lo.reshape(slots, rows, features), grad.reshape(slots, rows, features)
    heights = [size // LANES for size in (features, features, wide, features, features, features)]
    cuts = [sum(heights[:i]) for i in range(len(heights))]
    slot_first = pl.BlockSpec((slots, step, features), lambda n: (0, jnp.minimum(n, places - 1), 0))
    place_first = pl.BlockSpec((step, slots, features), lambda n: (jnp.minimum(n, places - 1), 0, 0))
    wi_grad, wo_grad, layer_out, input_grad, *vectors = pl.pallas_call(
        functools.partial(output_kernel, slots, cuts, places),
        name="output",
        grid=(chunks // side,),
        out_shape=(
            shape((features, wide), F32),
            shape((wide, features), F32),
            shape(inputs.shape, F32),
            shape(inputs.shape, F32),
            *(shape((height, LANES), F32) for height in heights),
        ),
        in_specs=[SMEM] * 2 + [pl.BlockSpec((side, chunk_rows, LANES), lambda n: (n, 0, 0))] + [slot_first] * 2 + [VMEM],
        out_specs=(
            pl.BlockSpec((features, side * WIDE), lambda n: (0, n)),
            pl.BlockSpec((side * WIDE, features), lambda n: (n, 0)),
            place_first,
            place_first,
            *([VMEM] * len(heights)),
        ),
        scratch_shapes=[pltpu.SMEM((slots,), jnp.int32), pltpu.SMEM((slots,), jnp.int32)],
        compiler_params=pltpu.CompilerParams(vmem_limit_bytes=60 << 20),
    )(item_counts, lengths, full.reshape(chunks, chunk_rows, LANES), lo, grad, small)
    gain_one_grad, shift_one_grad, bias_in_grad, bias_out_grad, gain_two_grad, shift_two_grad = [v.reshape(-1) for v in vectors]
    return (
        layer_out, input_grad, gain_one_grad, shift_one_grad, wi_grad, bias_in_grad, wo_grad, bias_out_grad, gain_two_grad, shift_two_grad,
    )


def per_device(
    inputs, item_counts, lengths, gain_one, shift_one, weight_in, bias_in, weight_out, bias_out, gain_two, shift_two, cotangent
):
    rows, slots, features = inputs.shape
    wide = weight_in.shape[1]
    sizes = (lax.axis_size("dp"), lax.axis_size("seq"))
    seq_total = rows * sizes[1]
    chunks = wide // WIDE
    chunk_rows = 2 * features * WIDE // LANES
    shape = jax.ShapeDtypeStruct

    seq_cos, seq_sin = dft_tables(seq_total)
    hid_cos, hid_sin = dft_tables(features)
    seq_table = [table.reshape(sizes[1], rows, seq_total) for table in (seq_cos, seq_sin)]
    seq_table = jnp.asarray(np.concatenate(seq_table, axis=1).astype(jnp.bfloat16))
    hid_table = jnp.asarray(np.concatenate([hid_cos, -hid_sin], axis=0).astype(jnp.bfloat16))
    vectors = (gain_one, shift_one, bias_out, gain_two, shift_two, bias_in)
    operands = (inputs, item_counts, lengths, vectors, weight_in, weight_out, cotangent, seq_table, hid_table)

    choices = sorted({slots // 2, slots})
    choice, low = pl.pallas_call(
        functools.partial(agree_kernel, sizes[0], choices, 2 * rows),
        name="agree",
        out_shape=(shape((1,), jnp.int32), shape((slots, rows, features), BF16)),
        in_specs=[SMEM] * 2 + [ANY],
        out_specs=(SMEM, ANY),
        scratch_shapes=[
            pltpu.VMEM(inputs.shape, F32),
            pltpu.VMEM((slots, rows, features), BF16),
            pltpu.SMEM((slots,), jnp.int32),
            pltpu.SMEM((slots,), jnp.int32),
            pltpu.VMEM((8, LANES), F32),
            pltpu.VMEM((sizes[0], 8, LANES), F32),
            DMA((2,)),
            DMA((sizes[0],)),
            DMA((sizes[0],)),
        ],
        compiler_params=pltpu.CompilerParams(collective_id=1, has_side_effects=True),
    )(item_counts, lengths, inputs)
    branches = [functools.partial(layer, far, index, sizes) for index, far in enumerate(choices)]

    return lax.switch(choice[0], branches, low, *operands)


def solution(mesh):
    placed = (
        P("seq", "dp", None), P("dp"), P("dp"), P(), P(), P(), P(), P(), P(), P(), P(), P("seq", "dp", None),
    )
    wide = P("seq", "dp", None)
    return jax.shard_map(
        per_device,
        mesh=mesh,
        in_specs=placed,
        out_specs=(wide, wide, P(), P(), P(), P(), P(), P(), P(), P()),
        check_vma=False,
    )
```

```python
import functools
import math

import jax
import jax.numpy as jnp
import numpy as np
from jax import lax
from jax.experimental import pallas as pl
from jax.experimental.pallas import tpu as pltpu
from jax.sharding import PartitionSpec as P

EPSILON = 1e-05
MESH = pl.DeviceIdType.MESH
LANES = 128
WIDE = 512
BF16 = jnp.bfloat16
F32 = jnp.float32


def dft_tables(count):
    index = np.arange(count, dtype=np.int64)
    turns = (index[:, None] * index[None, :] % count).astype(np.float32)
    angle = (turns * np.float32(2.0 * math.pi / count)).astype(np.float64)
    return np.cos(angle).astype(np.float32), np.sin(angle).astype(np.float32)


def aligned(value, step):
    return pl.multiple_of(value, step)


def bit_of(value, k):
    return (value // k) % 2


def flipped(value, k):
    return value + k * (1 - 2 * bit_of(value, k))


def axis_bits(axis, size):
    return [(axis, 1 << b) for b in range(size.bit_length() - 1)]


class Cube:
    def __init__(self, sizes, mids):
        dp, seq = sizes
        bits = axis_bits(1, seq) + axis_bits(0, dp)
        first, near, rest = bits[:1], bits[1:4], bits[4:]
        self.orders = [first + [near[i] for i in mid] + rest for mid in mids]
        self.bits = bits
        self.stages = len(bits)
        self.me = (lax.axis_index("dp"), lax.axis_index("seq"))
        self.values = {bit: self.value(bit) for bit in bits}
        self.partners = {bit: self.partner(bit) for bit in bits}

    def value(self, bit):
        return bit_of(self.me[bit[0]], bit[1])

    def partner(self, bit):
        axis, k = bit
        other = flipped(self.me[axis], k)
        return (other, self.me[1]) if axis == 0 else (self.me[0], other)

    def offset(self, order, level, rows):
        total = 0
        for s in range(level):
            total = total + self.values[self.orders[order][s]] * (rows >> (s + 1))
        return total


class Exchange:
    def __init__(self, size, rows, buf, send, recv):
        self.size, self.rows, self.buf, self.send_sem, self.recv_sem = size, rows, buf, send, recv
        self.dp, self.q = lax.axis_index("dp"), lax.axis_index("seq")
        self.order = [1 << b for b in reversed(range(size.bit_length() - 1))]

    def owner(self, pattern):
        index = self.q
        for k in self.order:
            if pattern & k:
                index = flipped(index, k)
        return index

    def copy(self, slot, pattern):
        hop = pattern & -pattern
        place = pl.ds(aligned(self.owner(pattern - hop) * self.rows, self.rows), self.rows)
        ref = self.buf.at[slot, place]
        return pltpu.make_async_remote_copy(
            src_ref=ref,
            dst_ref=ref,
            send_sem=self.send_sem.at[slot, pattern],
            recv_sem=self.recv_sem.at[slot, pattern],
            device_id=(self.dp, flipped(self.q, hop)),
            device_id_type=MESH,
        )

    def patterns(self, far):
        return range(1, self.size) if far else range(1, 2)

    def start_own(self, slot, far):
        for pattern in self.patterns(far):
            if pattern & (pattern - 1) == 0:
                self.copy(slot, pattern).start()

    def forward(self, slot):
        for pattern in self.patterns(True):
            if pattern & 1 == 0:
                self.copy(slot, pattern).wait_recv()
                for k in self.order:
                    if k < (pattern & -pattern):
                        self.copy(slot, pattern | k).start()

    def wait_near(self, slot, far):
        for pattern in self.patterns(far):
            if pattern & 1:
                self.copy(slot, pattern).wait_recv()

    def wait_sends(self, slot, far):
        for pattern in self.patterns(far):
            self.copy(slot, pattern).wait_send()


def greet(partners):
    barrier = pltpu.get_barrier_semaphore()
    for partner in partners:
        pl.semaphore_signal(barrier, inc=1, device_id=partner, device_id_type=MESH)
    return lambda: pl.semaphore_wait(barrier, len(partners))


def rank_slots(count_ref, length_ref, perm_s, slen_s, slots):
    count = count_ref[0]
    live = [jnp.where(i < count, length_ref[i], 0) for i in range(slots)]
    ranks = []
    for i in range(slots):
        rank = 0
        for k in range(slots):
            if k != i:
                ahead = live[k] >= live[i] if k < i else live[k] > live[i]
                rank = rank + jnp.where(ahead, 1, 0)
        ranks.append(rank)
    for j in range(slots):
        perm, length = 0, 0
        for i in range(slots):
            here = ranks[i] == j
            perm = perm + jnp.where(here, i, 0)
            length = length + jnp.where(here, live[i], 0)
        perm_s[j] = perm
        slen_s[j] = length


def live_rows(slen_s, slot, first, rows):
    position = first + lax.broadcasted_iota(jnp.int32, (rows, 1), 0)
    return position < slen_s[slot]


def fold8(values):
    rows, lanes = values.shape
    return values.reshape(rows // 8, 8, lanes).sum(axis=0)


def normalize(values):
    center = values - jnp.mean(values, axis=-1, keepdims=True)
    spread = jnp.mean(center * center, axis=-1, keepdims=True)
    inverse = lax.rsqrt(spread + EPSILON)
    return center * inverse, inverse


def norm_back(grad_hat, normal, inverse):
    first = jnp.mean(grad_hat, axis=-1, keepdims=True)
    second = jnp.mean(grad_hat * normal, axis=-1, keepdims=True)
    return inverse * (grad_hat - first - normal * second)


def mix_slot(slot, far, exchange, tables, buf, uv, place):
    rows = exchange.rows
    if far:
        table, block = tables[...], buf[slot]
    else:
        base = aligned(exchange.q // 2 * (2 * rows), 2 * rows)
        table, block = tables[:, pl.ds(base, 2 * rows)], buf[slot, pl.ds(base, 2 * rows), :]
    both = jnp.dot(table, block, preferred_element_type=F32).astype(BF16)
    width = both.shape[1]
    uv[pl.ds(place, rows), :width] = both[:rows]
    uv[pl.ds(place, rows), width:] = both[rows:]


def group_at(i, near_groups, count):
    if near_groups == 0:
        return count - 1 - i
    return jnp.where(i < near_groups, count - near_groups + i, count - 1 - i)


def forward_kernel(cfg, *refs):
    sizes, far_slots, slots, group, agrees = cfg
    if agrees:
        choice_o, (mine, theirs, say_sem, hear_sem) = refs[agrees], refs[-4:]
        refs = refs[:agrees] + refs[agrees + 1 : -4]
    vec_refs, refs = refs[2:8], refs[:2] + refs[8:]
    (
        count_ref, length_ref, x_hbm, cot_hbm, wi_hbm, wo_hbm, sc_hbm, hc_hbm,
        act_o, dg_o, nrm_o, sum_o, gs_o, gb_o, lo_o, part_o,
        perm_s, slen_s, x_v, cot_v, wi_v, wo_v, sc_v, hc_v, buf, uv, sum_v, nrm_v, act_v, dg_v, gs_v, gb_v, lo_v, br_v, vec_ref,
        load_sem, out_sem, send_sem, recv_sem,
    ) = refs
    rows, _, features = x_v.shape
    wide = wi_v.shape[1]
    seq_total = rows * sizes[1]
    scale = 1.0 / math.sqrt(features * seq_total)
    exchange = Exchange(sizes[1], rows, buf, send_sem, recv_sem)
    q = exchange.q
    first = q * rows
    gain_one, shift_one, bias_out, gain_two, shift_two = (lambda i=i: vec_ref[i : i + 1, :] for i in range(5))
    loads = [
        pltpu.make_async_copy(x_hbm, x_v, load_sem.at[0]),
        pltpu.make_async_copy(sc_hbm.at[q], sc_v, load_sem.at[1]),
        pltpu.make_async_copy(hc_hbm, hc_v, load_sem.at[2]),
        pltpu.make_async_copy(wi_hbm, wi_v, load_sem.at[3]),
        pltpu.make_async_copy(wo_hbm, wo_v, load_sem.at[4]),
        pltpu.make_async_copy(cot_hbm, cot_v, load_sem.at[5]),
    ]
    loads[0].start()
    partners = [(exchange.dp, flipped(q, k)) for k in exchange.order]
    peers = [(lax.rem(exchange.dp + i, sizes[0]), q) for i in range(1, sizes[0])] if agrees else []
    met = greet(partners + peers)
    row = 0
    for vec in vec_refs:
        for i in range(vec.shape[0] // features):
            vec_ref[row : row + 1, :] = vec[pl.ds(i * features, features)].reshape(1, features)
            row += 1
    rank_slots(count_ref, length_ref, perm_s, slen_s, slots)
    for load in loads[1:3]:
        load.start()
    loads[0].wait()
    loads[3].start()
    met()

    def word(i):
        return pltpu.make_async_remote_copy(
            src_ref=mine,
            dst_ref=theirs.at[i],
            send_sem=say_sem.at[i],
            recv_sem=hear_sem.at[i],
            device_id=peers[i - 1],
            device_id_type=MESH,
        )

    if agrees:
        long = 0
        for i in range(slots):
            long = long + jnp.where((i < count_ref[0]) & (length_ref[i] > 2 * rows), 1, 0)
        mine[...] = jnp.full(mine.shape, long, jnp.int32).astype(F32)
        theirs[0] = mine[...]
        for i in range(1, sizes[0]):
            word(i).start()

    def prepare(i, _):
        slot = jnp.where(i < slots - far_slots, far_slots + i, slots - 1 - i)
        value = jnp.where(live_rows(slen_s, slot, first, rows), x_v[:, perm_s[slot], :], 0.0)
        buf[slot, pl.ds(aligned(first, rows), rows), :] = value.astype(BF16)
        pl.when(slot < far_slots)(lambda: exchange.start_own(slot, True))
        if far_slots < slots:
            pl.when(slot >= far_slots)(lambda: exchange.start_own(slot, False))
        return 0

    lax.fori_loop(0, slots, prepare, 0)
    part_o[...] = jnp.zeros_like(part_o)
    for load in loads[1:3]:
        load.wait()

    batch = group * rows
    span = features
    count = slots // group
    near_groups = (slots - far_slots) // group

    def outs(base):
        place = pl.ds(base, batch)
        early = [
            pltpu.make_async_copy(nrm_v.at[place], nrm_o.at[place], out_sem.at[0]),
            pltpu.make_async_copy(sum_v.at[place], sum_o.at[place], out_sem.at[1]),
        ]
        for n in range(wide // WIDE):
            cut = pl.ds(n * WIDE, WIDE)
            early.append(pltpu.make_async_copy(act_v.at[place, cut], act_o.at[n, place], out_sem.at[4]))
            early.append(pltpu.make_async_copy(dg_v.at[place, cut], dg_o.at[n, place], out_sem.at[5]))
        late = [
            pltpu.make_async_copy(gs_v.at[place], gs_o.at[place], out_sem.at[2]),
            pltpu.make_async_copy(lo_v.at[place], lo_o.at[place], out_sem.at[3]),
            pltpu.make_async_copy(gb_v.at[place], gb_o.at[place], out_sem.at[6]),
        ]
        return early, late

    def bring(slot0):
        for k in reversed(range(group)):
            exchange.forward(slot0 + k)

    def mixing(slot0, far):
        for k in reversed(range(group)):
            exchange.wait_near(slot0 + k, far)
            mix_slot(slot0 + k, far, exchange, sc_v, buf, uv, k * rows)

    def work(i, _):
        slot0 = group_at(i, near_groups, count) * group
        base = aligned(slot0 * rows, batch)
        place = pl.ds(base, batch)
        if near_groups < count:
            pl.when(i >= near_groups)(lambda: mixing(slot0, True))
        if near_groups > 0:
            pl.when(i < near_groups)(lambda: mixing(slot0, False))
        br_v[...] = jnp.dot(uv[...], hc_v[...], preferred_element_type=F32)

        def norm_one(k, _):
            here = pl.ds(aligned(base + k * rows, rows), rows)
            mixed = (br_v[pl.ds(aligned(k * rows, rows), rows), :] * scale).astype(BF16).astype(F32)
            live = live_rows(slen_s, slot0 + k, first, rows)
            total = jnp.where(live, x_v[:, perm_s[slot0 + k], :], 0.0) + mixed
            sum_v[here, :] = total
            hat, _ = normalize(total)
            nrm_v[here, :] = (hat * gain_one() + shift_one()).astype(BF16)
            return 0

        lax.fori_loop(0, group, norm_one, 0)

        @pl.when(i == 0)
        def _():
            loads[3].wait()
            for load in loads[4:]:
                load.start()

        def expand(n, _):
            cut = pl.ds(aligned(n * span, span), span)
            hidden = jnp.dot(nrm_v[place, :], wi_v[:, cut], preferred_element_type=F32) + vec_ref[pl.ds(5 + n, 1), :]
            gate = 0.5 + 0.5 * lax.erf(hidden * math.sqrt(0.5))
            slope = gate + hidden * (jnp.exp(hidden * hidden * -0.5) * (1.0 / math.sqrt(2.0 * math.pi)))
            act_v[place, cut] = (hidden * gate).astype(BF16)
            dg_v[place, cut] = slope.astype(BF16)
            return 0

        lax.fori_loop(0, wide // span, expand, 0)
        for copy in outs(base)[0]:
            copy.start()
        if near_groups < count:

            @pl.when((i + 1 >= near_groups) & (i + 1 < count))
            def _():
                bring(group_at(i + 1, near_groups, count) * group)

        pl.when(i == 0)(loads[4].wait)
        br_v[...] = jnp.dot(act_v[place, :], wo_v[...], preferred_element_type=F32)

        def norm_two(k, _):
            here = pl.ds(aligned(base + k * rows, rows), rows)
            local = pl.ds(aligned(k * rows, rows), rows)
            slot = slot0 + k
            live = live_rows(slen_s, slot, first, rows)
            hat, inverse = normalize(sum_v[here, :] + (br_v[local, :] + bias_out()))
            grad = jnp.where(live, cot_v[:, perm_s[slot], :], 0.0)
            lo_v[here, :] = jnp.where(live, hat * gain_two() + shift_two(), 0.0).astype(BF16)
            part_o[0:8, :] = part_o[0:8, :] + fold8(grad * hat)
            part_o[8:16, :] = part_o[8:16, :] + fold8(grad)
            second = norm_back(grad * gain_two(), hat, inverse)
            low = second.astype(BF16)
            gs_v[here, :] = second
            gb_v[here, :] = low
            part_o[16:24, :] = part_o[16:24, :] + fold8(low.astype(F32))
            return 0

        pl.when(i == 0)(loads[5].wait)
        lax.fori_loop(0, group, norm_two, 0)
        for copy in outs(base)[1]:
            copy.start()
        return 0

    if near_groups == 0:
        bring((count - 1) * group)
    lax.fori_loop(0, count, work, 0)

    def finish(slot, _):
        pl.when(slot < far_slots)(lambda: exchange.wait_sends(slot, True))
        if far_slots < slots:
            pl.when(slot >= far_slots)(lambda: exchange.wait_sends(slot, False))
        return 0

    lax.fori_loop(0, slots, finish, 0)

    if agrees:
        for i in range(1, sizes[0]):
            word(i).wait()
        choice_o[0] = jnp.where(jnp.max(theirs[...]) > far_slots, 1, 0)

    def flush(g, _):
        for copies in outs(aligned(g * batch, batch)):
            for copy in copies:
                copy.wait()
        return 0

    lax.fori_loop(0, count, flush, 0)


def backward_kernel(cfg, *refs):
    sizes, far_slots, slots, group, parts, mids, lags, plan = cfg
    cube = Cube(sizes, mids)
    S = cube.stages
    (
        count_ref, length_ref, gain_ref, part_ref,
        act_hbm, dg_hbm, nrm_hbm, sum_hbm, gs_hbm, gb_hbm, wi_hbm, wo_hbm, sc_hbm, hc_hbm,
        full_o, ig_o, small_o,
        perm_s, slen_s, gs_v, sum_v, nrm_v, gb_v, gh_v, gn_v, act_v, dg_v, wi_v, wo_v, sc_v, hc_v, buf, uv, mix_v, ig_v,
        bin_v, one_v, small_v, gain_v, part_v, full,
    ) = refs[:41]
    landed = refs[41 : 41 + S]
    (
        small_recv, load_sem, sum_sem, stream_sem, out_sem, ig_sem, send_sem, recv_sem,
        rs_s, rs_r, ag_s, ag_r, sm_s, sm_r,
    ) = refs[41 + S :]
    ticks, tick_rows, _ = part_v.shape
    message = tick_rows // parts
    chunks = act_hbm.shape[0]
    per_tick = chunks // ticks
    features = nrm_v.shape[1]
    rows = gs_v.shape[0] // slots
    batch = group * rows
    scale = 1.0 / math.sqrt(features * rows * sizes[1])
    exchange = Exchange(sizes[1], rows, buf, send_sem, recv_sem)
    q = exchange.q
    first = q * rows
    loads = [
        pltpu.make_async_copy(gb_hbm, gb_v, load_sem.at[0]),
        pltpu.make_async_copy(nrm_hbm, nrm_v, load_sem.at[1]),
        pltpu.make_async_copy(gs_hbm, gs_v, load_sem.at[2]),
        pltpu.make_async_copy(sc_hbm.at[q], sc_v, load_sem.at[3]),
        pltpu.make_async_copy(hc_hbm, hc_v, load_sem.at[4]),
    ]

    def turn(i):
        return jnp.where(i < far_slots, far_slots - 1 - i, i) if far_slots < slots else slots - 1 - i

    def sum_copy(i):
        place = pl.ds(aligned(turn(i) * rows, rows), rows)
        return pltpu.make_async_copy(sum_hbm.at[place], sum_v.at[lax.rem(i, 2)], sum_sem.at[lax.rem(i, 2)])

    def streams(n, slot):
        cut = pl.ds(aligned(n * WIDE, WIDE), WIDE)
        return [
            pltpu.make_async_copy(act_hbm.at[n], act_v.at[slot], stream_sem.at[0, slot]),
            pltpu.make_async_copy(wo_hbm.at[cut], wo_v.at[slot], stream_sem.at[1, slot]),
            pltpu.make_async_copy(dg_hbm.at[n], dg_v.at[slot], stream_sem.at[2, slot]),
            pltpu.make_async_copy(wi_hbm.at[:, cut], wi_v.at[slot], stream_sem.at[3, slot]),
        ]

    loads[0].start()
    streams(0, 0)[0].start()
    met = greet([cube.partner(bit) for bit in cube.bits])
    rank_slots(count_ref, length_ref, perm_s, slen_s, slots)

    starts = [[j * message + cube.offset(j, level, message) for level in range(S + 1)] for j in range(parts)]

    def rs(m, t, j, s):
        bit = cube.orders[j][s]
        half = message >> (s + 1)
        off = starts[j][s] + (1 - cube.values[bit]) * half
        return pltpu.make_async_remote_copy(
            src_ref=part_v.at[t, pl.ds(aligned(off, 16), half)],
            dst_ref=landed[s].at[m],
            send_sem=rs_s.at[s],
            recv_sem=rs_r.at[s, m],
            device_id=cube.partners[bit],
            device_id_type=MESH,
        )

    def ag(m, t, j, s):
        bit = cube.orders[j][s]
        half = message >> (s + 1)
        ref = full.at[t, pl.ds(aligned(starts[j][s + 1], 16), half)]
        return pltpu.make_async_remote_copy(
            src_ref=ref,
            dst_ref=ref,
            send_sem=ag_s.at[s],
            recv_sem=ag_r.at[s, m],
            device_id=cube.partners[bit],
            device_id_type=MESH,
        )

    def add(m, t, j, s):
        half = message >> (s + 1)
        place = pl.ds(aligned(starts[j][s + 1], 16), half)
        total = part_v[t, place, :].astype(F32) + landed[s][m].astype(F32)
        target = full if s == S - 1 else part_v
        target[t, place, :] = total.astype(BF16)

    def out(t, j):
        place = pl.ds(j * message, message)
        return pltpu.make_async_copy(full.at[t, place], full_o.at[t, place], out_sem.at[t, j])

    def event(k, m, t, j):
        if k == 0:
            rs(m, t, j, 0).start()
        elif k <= S:
            rs(m, t, j, k - 1).wait_recv()
            add(m, t, j, k - 1)
            (rs(m, t, j, k) if k < S else ag(m, t, j, S - 1)).start()
        elif k < 2 * S:
            s = 2 * S - k
            ag(m, t, j, s).wait_recv()
            ag(m, t, j, s - 1).start()
        else:
            ag(m, t, j, 0).wait_recv()
            out(t, j).start()

    def sends_done():
        for s in range(S):
            for sem in (rs_s.at[s], ag_s.at[s]):
                pltpu.make_async_copy(landed[s], landed[s], sem).wait()

    when = [0 if per_tick == 1 and parts == 4 else parts]
    for lag in lags:
        when.append(when[-1] + lag)

    def events(tick, j):
        for k in reversed(range(2 * S + 1)):
            t = tick + (j - when[k]) // parts
            jj = (j - when[k]) % parts
            pl.when((t >= 0) & (t < ticks))(functools.partial(event, k, t * parts + jj, t, jj))

    bin_v[...] = jnp.zeros_like(bin_v)
    one_v[...] = jnp.zeros_like(one_v)
    gain_v[...] = gain_ref[...].reshape(1, features)
    gn_v[...] = jnp.zeros_like(gn_v)
    small_v[...] = jnp.zeros_like(small_v)
    loads[0].wait()
    for copy in streams(0, 0)[1:]:
        copy.start()
    loads[1].start()
    met()

    def load_rest():
        for load in loads[2:]:
            load.start()
        for i in range(2):
            sum_copy(i).start()


    def contract(left, right, dims):
        return lax.dot_general(left, right, ((dims, dims), ((), ())), preferred_element_type=F32)

    def weigh_out(n, slot, t, base):
        streams(n, slot)[0].wait()
        grad = contract(act_v[slot], gb_v[...], (0,)).astype(BF16)
        for i in range(features // LANES):
            part_v[t, pl.ds(base + i * WIDE, WIDE), :] = grad[:, i * LANES : (i + 1) * LANES]

    def pull(n, slot, t, base):
        streams(n, slot)[1].wait()
        streams(n, slot)[2].wait()
        pulled = contract(gb_v[...], wo_v[slot], (1,)) * dg_v[slot].astype(F32)
        pulled = pulled.astype(BF16)
        gh_v[...] = pulled
        bin_v[n] = fold8(pulled.astype(F32))

    def weigh_in(n, slot, t, base):
        pl.when(n == 0)(loads[1].wait)
        grad = contract(nrm_v[...], gh_v[...], (0,)).astype(BF16)
        for i in range(WIDE // LANES):
            place = pl.ds(base + features // LANES * WIDE + i * features, features)
            part_v[t, place, :] = grad[:, i * LANES : (i + 1) * LANES]

    def spread(n, slot, t, base):
        streams(n, slot)[3].wait()
        for i in range(2):
            here = pl.ds(i * (slots // 2) * rows, slots // 2 * rows)
            gn_v[here, :] = gn_v[here, :] + contract(gh_v[here, :], wi_v[slot], (1,))

    steps = [weigh_out, pull, weigh_in, spread]

    def compute(tick, j):
        if per_tick == 1 and parts == 4:
            slot = lax.rem(tick, 2)
            if j == 0:
                for copy in streams(tick + 1, 1 - slot):
                    pl.when(tick + 1 < chunks)(copy.start)
            steps[j](tick, slot, tick, 0)
        elif j == 0:

            def whole(u, _):
                n = tick * per_tick + u
                slot = lax.rem(n, 2)
                for copy in streams(n + 1, 1 - slot):
                    pl.when(n + 1 < chunks)(copy.start)
                for step in steps:
                    step(n, slot, tick, aligned(u * (tick_rows // per_tick), LANES))
                return 0

            lax.fori_loop(0, per_tick, whole, 0)

    def back(i, _):
        slot = turn(i)
        here = pl.ds(aligned(slot * rows, rows), rows)
        pl.when(i == 0)(loads[2].wait)
        sum_copy(i).wait()
        hat, inverse = normalize(sum_v[lax.rem(i, 2)])
        grad = gn_v[here, :]
        one_v[0:8, :] = one_v[0:8, :] + fold8(grad * hat)
        one_v[8:16, :] = one_v[8:16, :] + fold8(grad)
        grad = gs_v[here, :] + norm_back(grad * gain_v[...], hat, inverse)
        gs_v[here, :] = grad
        buf[slot, pl.ds(aligned(first, rows), rows), :] = grad.astype(BF16)
        pl.when(i < far_slots)(lambda: exchange.start_own(slot, True))
        if far_slots < slots:
            pl.when(i >= far_slots)(lambda: exchange.start_own(slot, False))
        pl.when(i + 2 < slots)(lambda: sum_copy(i + 2).start())
        return 0

    def small_copy(s):
        return pltpu.make_async_remote_copy(
            src_ref=small_v.at[s],
            dst_ref=small_recv.at[s],
            send_sem=sm_s.at[s],
            recv_sem=sm_r.at[s],
            device_id=cube.partners[cube.bits[s]],
            device_id_type=MESH,
        )

    def small_start():
        row = 0
        vectors = [one_v[0:8, :], one_v[8:16, :]] + [bin_v[n] for n in range(chunks)]
        vectors += [part_ref[16:24, :], part_ref[0:8, :], part_ref[8:16, :]]
        for vector in vectors:
            vector = jnp.sum(vector, axis=0, keepdims=True)
            for i in range(vector.shape[1] // LANES):
                small_v[0, row : row + 1, :] = vector[:, i * LANES : (i + 1) * LANES]
                row += 1
        small_copy(0).start()

    def small_step(s):
        small_copy(s).wait()
        if s + 1 < S:
            small_v[s + 1] = small_v[s] + small_recv[s]
            small_copy(s + 1).start()
        else:
            small_o[...] = small_v[s] + small_recv[s]

    count = slots // group
    near_groups = (slots - far_slots) // group

    def grad_copy(i):
        base = aligned(group_at(i, near_groups, count) * batch, batch)
        return pltpu.make_async_copy(ig_v.at[lax.rem(i, 2)], ig_o.at[pl.ds(base, batch)], ig_sem.at[lax.rem(i, 2)])

    def mixing(i, k, far):
        slot = group_at(i, near_groups, count) * group + k
        exchange.wait_near(slot, far)
        mix_slot(slot, far, exchange, sc_v, buf, uv, k * rows)

    def hidden_mix(i):
        pl.when(i >= 2)(lambda: grad_copy(i - 2).wait())
        mix_v[...] = jnp.dot(uv[...], hc_v[...], preferred_element_type=F32)

    def finish(i):
        for k in range(group):
            slot = group_at(i, near_groups, count) * group + k
            here = pl.ds(aligned(slot * rows, rows), rows)
            local = pl.ds(k * rows, rows)
            grad = gs_v[here, :] + mix_v[local, :] * scale
            grad = jnp.where(live_rows(slen_s, slot, first, rows), grad, 0.0)
            ig_v[lax.rem(i, 2), local, :] = grad.astype(BF16)
        grad_copy(i).start()

    def bring(i):
        for k in reversed(range(group)):
            exchange.forward(group_at(i, near_groups, count) * group + k)

    small_at, near_at, far_at, lead = plan

    def drain(tick, j):
        d = tick - ticks

        @pl.when(d == 0)
        def _():
            share = -(-slots // parts)
            lax.fori_loop(min(j * share, slots), min((j + 1) * share, slots), back, 0)

        here = lambda at: pl.when(d * parts + j == at)
        if j == small_at % parts:
            here(small_at)(small_start)
        for s in range(S):
            at = small_at + 3 * (s + 1)
            if j == at % parts:
                here(at)(functools.partial(small_step, s))
        if j == 0:

            @pl.when(d == 1)
            def _():
                for load in loads[3:]:
                    load.wait()

        for far, start, low, high in ((False, near_at, 0, near_groups), (True, far_at, near_groups, count)):
            if low == high:
                continue
            i = d - start + low

            @pl.when((i >= low) & (i < high))
            def _():
                subs = [
                    lambda: mixing(i, 0, far),
                    lambda: [mixing(i, k, far) for k in range(1, group)],
                    lambda: hidden_mix(i),
                    lambda: finish(i),
                ]
                for at, sub in enumerate(subs):
                    if min(at, parts - 1) == j:
                        sub()

            if far and j == parts - 1:
                ahead = i + lead
                pl.when((ahead >= low) & (ahead < high))(lambda: bring(ahead))

    last = ticks + max(
        -(-(when[-1] + 1) // parts),
        (small_at + 3 * S) // parts + 1,
        near_at + near_groups,
        far_at + count - near_groups,
    )

    def body(tick, _):
        pl.when(tick == 1)(load_rest)
        for j in range(parts):
            pl.when(tick < ticks)(lambda: compute(tick, j))
            events(tick, j)
            pl.when(tick >= ticks)(lambda: drain(tick, j))
        return 0

    lax.fori_loop(0, last, body, 0)

    def settle(slot, _):
        pl.when(slot < far_slots)(lambda: exchange.wait_sends(slot, True))
        if far_slots < slots:
            pl.when(slot >= far_slots)(lambda: exchange.wait_sends(slot, False))
        return 0

    lax.fori_loop(0, slots, settle, 0)
    for i in range(max(0, count - 2), count):
        grad_copy(i).wait()

    def finish_out(t, _):
        for j in range(parts):
            out(t, j).wait()
        return 0

    lax.fori_loop(0, ticks, finish_out, 0)
    sends_done()


def output_kernel(slots, cuts, places, count_ref, length_ref, full_ref, lo_ref, ig_ref, small_ref, *refs):
    wi_ref, wo_ref, lo_out, ig_out = refs[:4]
    vector_refs, (perm_s, slen_s) = refs[4:-2], refs[-2:]
    step = pl.program_id(0)
    features = wi_ref.shape[0]
    for u in range(full_ref.shape[0]):
        base = u * WIDE
        for i in range(features // LANES):
            wo_ref[base : base + WIDE, i * LANES : (i + 1) * LANES] = full_ref[u, pl.ds(i * WIDE, WIDE), :].astype(F32)
        for i in range(WIDE // LANES):
            start = features // LANES * WIDE + i * features
            wi_ref[:, base + i * LANES : base + (i + 1) * LANES] = full_ref[u, pl.ds(start, features), :].astype(F32)

    @pl.when(step == 0)
    def _():
        rank_slots(count_ref, length_ref, perm_s, slen_s, slots)
        for ref, start in zip(vector_refs, cuts):
            ref[...] = small_ref[start : start + ref.shape[0], :]

    @pl.when(step < places)
    def _():
        for j in range(slots):
            lo_out[:, perm_s[j], :] = lo_ref[j].astype(F32)
            ig_out[:, perm_s[j], :] = ig_ref[j].astype(F32)


ANY = pl.BlockSpec(memory_space=pl.ANY)
SMEM = pl.BlockSpec(memory_space=pltpu.SMEM)
VMEM = pl.BlockSpec(memory_space=pltpu.VMEM)
DMA = pltpu.SemaphoreType.DMA
LAGS = [3, 5, 4, 3, 3, 3, 3, 4, 6, 3]
PLAN = (4, 1, 4, 1)
FAR_PLAN = (4, 1, 4, 1)
MIDS = ((0, 1, 2), (1, 0, 2), (2, 0, 1), (1, 2, 0))
FAR_MIDS = ((1, 2, 0), (2, 1, 0), (1, 0, 2), (2, 0, 1))


def run_forward(sizes, far_slots, slots, *operands, agrees=False, group=2, name="forward", cid=1):
    rows, _, features = operands[8].shape
    wide = operands[10].shape[1]
    seq_total = rows * sizes[1]
    flat, batch, chunks = rows * slots, group * rows, wide // WIDE
    shape = jax.ShapeDtypeStruct
    return pl.pallas_call(
        functools.partial(forward_kernel, (sizes, far_slots, slots, group, len(operands) + 8 if agrees else 0)),
        name=name,
        out_shape=(
            shape((chunks, flat, WIDE), BF16),
            shape((chunks, flat, WIDE), BF16),
            shape((flat, features), BF16),
            shape((flat, features), F32),
            shape((flat, features), F32),
            shape((flat, features), BF16),
            shape((flat, features), BF16),
            shape((24, features), F32),
        )
        + ((shape((1,), jnp.int32),) if agrees else ()),
        in_specs=[SMEM] * 2 + [VMEM] * 6 + [ANY] * 6,
        out_specs=[ANY] * 7 + [VMEM] + [SMEM] * agrees,
        scratch_shapes=[
            pltpu.SMEM((slots,), jnp.int32),
            pltpu.SMEM((slots,), jnp.int32),
            pltpu.VMEM((rows, slots, features), F32),
            pltpu.VMEM((rows, slots, features), F32),
            pltpu.VMEM((features, wide), BF16),
            pltpu.VMEM((wide, features), BF16),
            pltpu.VMEM((2 * rows, seq_total), BF16),
            pltpu.VMEM((2 * features, features), BF16),
            pltpu.VMEM((slots, seq_total, features), BF16),
            pltpu.VMEM((batch, 2 * features), BF16),
            pltpu.VMEM((flat, features), F32),
            pltpu.VMEM((flat, features), BF16),
            pltpu.VMEM((flat, wide), BF16),
            pltpu.VMEM((flat, wide), BF16),
            pltpu.VMEM((flat, features), F32),
            pltpu.VMEM((flat, features), BF16),
            pltpu.VMEM((flat, features), BF16),
            pltpu.VMEM((batch, features), F32),
            pltpu.VMEM((5 + wide // features, features), F32),
            DMA((6,)),
            DMA((7,)),
            DMA((slots, sizes[1])),
            DMA((slots, sizes[1])),
        ]
        + agrees * [pltpu.VMEM((8, LANES), F32), pltpu.VMEM((sizes[0], 8, LANES), F32), DMA((sizes[0],)), DMA((sizes[0],))],
        compiler_params=pltpu.CompilerParams(collective_id=cid, has_side_effects=True, vmem_limit_bytes=62 << 20),
    )(*operands)


def run_backward(sizes, far_slots, slots, ticks, tick_rows, parts, *operands, group=2, mids=None, lags=None, plan=None, name="backward", cid=2):
    devices = sizes[0] * sizes[1]
    chunks, flat, _ = operands[4].shape
    features, wide = operands[10].shape
    rows = flat // slots
    seq_total = rows * sizes[1]
    batch = group * rows
    message = tick_rows // parts
    shape = jax.ShapeDtypeStruct
    mostly_far = far_slots > slots * 5 // 8
    mids = mids or (FAR_MIDS if mostly_far else MIDS)
    plan = plan or (FAR_PLAN if mostly_far else PLAN)
    lags = lags or LAGS
    stages = devices.bit_length() - 1
    lags = (lags[:stages] + [2] * stages)[:stages] + ([2] * stages + lags[-stages:])[-stages:]
    return pl.pallas_call(
        functools.partial(backward_kernel, (sizes, far_slots, slots, group, parts, mids, lags, plan)),
        name=name,
        out_shape=(
            shape((ticks, tick_rows, LANES), BF16),
            shape((flat, features), BF16),
            shape((64, LANES), F32),
        ),
        in_specs=[SMEM] * 2 + [VMEM] * 2 + [ANY] * 10,
        out_specs=[ANY] * 2 + [VMEM],
        scratch_shapes=[
            pltpu.SMEM((slots,), jnp.int32),
            pltpu.SMEM((slots,), jnp.int32),
            pltpu.VMEM((flat, features), F32),
            pltpu.VMEM((2, rows, features), F32),
            pltpu.VMEM((flat, features), BF16),
            pltpu.VMEM((flat, features), BF16),
            pltpu.VMEM((flat, WIDE), BF16),
            pltpu.VMEM((flat, features), F32),
            pltpu.VMEM((2, flat, WIDE), BF16),
            pltpu.VMEM((2, flat, WIDE), BF16),
            pltpu.VMEM((2, features, WIDE), BF16),
            pltpu.VMEM((2, WIDE, features), BF16),
            pltpu.VMEM((2 * rows, seq_total), BF16),
            pltpu.VMEM((2 * features, features), BF16),
            pltpu.VMEM((slots, seq_total, features), BF16),
            pltpu.VMEM((batch, 2 * features), BF16),
            pltpu.VMEM((batch, features), F32),
            pltpu.VMEM((2, batch, features), BF16),
            pltpu.VMEM((chunks, 8, WIDE), F32),
            pltpu.VMEM((16, features), F32),
            pltpu.VMEM((stages, 64, LANES), F32),
            pltpu.VMEM((1, features), F32),
            pltpu.VMEM((ticks, tick_rows, LANES), BF16),
            pltpu.VMEM((ticks, tick_rows, LANES), BF16),
        ]
        + [pltpu.VMEM((ticks * parts, message >> (s + 1), LANES), BF16) for s in range(stages)]
        + [
            pltpu.VMEM((stages, 64, LANES), F32),
            DMA((5,)),
            DMA((2,)),
            DMA((4, 2)),
            DMA((ticks, parts)),
            DMA((2,)),
            DMA((slots, sizes[1])),
            DMA((slots, sizes[1])),
            DMA((stages,)),
            DMA((stages, ticks * parts)),
            DMA((stages,)),
            DMA((stages, ticks * parts)),
            DMA((stages,)),
            DMA((stages,)),
        ],
        compiler_params=pltpu.CompilerParams(collective_id=cid, has_side_effects=True, vmem_limit_bytes=62 << 20),
    )(*operands)


def cut_messages(devices, chunks, chunk_rows):
    per_tick, parts = min(
        (count, -cut)
        for count in range(1, chunks + 1)
        for cut in range(1, 5)
        if chunks % count == 0 and chunk_rows * count % (devices * 16 * cut) == 0
    )
    return per_tick, -parts


def rest_of_layer(far_slots, sizes, cid, known, inputs, item_counts, lengths, vectors, weight_in, weight_out, cotangent, seq_table, hid_table):
    rows, slots, features = inputs.shape
    wide = weight_in.shape[1]
    chunks = wide // WIDE
    chunk_rows = 2 * features * WIDE // LANES
    shape = jax.ShapeDtypeStruct
    per_tick, parts = cut_messages(sizes[0] * sizes[1], chunks, chunk_rows)
    act, dg, nrm, summed, second, low, lo, part = known or run_forward(
        sizes, far_slots, slots,
        item_counts, lengths, *vectors, inputs, cotangent, weight_in, weight_out, seq_table, hid_table,
        cid=cid,
    )
    full, grad, small = run_backward(
        sizes, far_slots, slots, chunks // per_tick, chunk_rows * per_tick, parts,
        item_counts, lengths, vectors[0], part, act, dg, nrm, summed, second, low, weight_in, weight_out, seq_table, hid_table,
        cid=cid + 1,
    )
    side = 2 if chunks % 2 == 0 else 1
    places = 1 << min((chunks // side).bit_length() - 1, 3)
    step = rows // places
    lo, grad = lo.reshape(slots, rows, features), grad.reshape(slots, rows, features)
    heights = [size // LANES for size in (features, features, wide, features, features, features)]
    cuts = [sum(heights[:i]) for i in range(len(heights))]
    slot_first = pl.BlockSpec((slots, step, features), lambda n: (0, jnp.minimum(n, places - 1), 0))
    place_first = pl.BlockSpec((step, slots, features), lambda n: (jnp.minimum(n, places - 1), 0, 0))
    wi_grad, wo_grad, layer_out, input_grad, *vectors = pl.pallas_call(
        functools.partial(output_kernel, slots, cuts, places),
        name="output",
        grid=(chunks // side,),
        out_shape=(
            shape((features, wide), F32),
            shape((wide, features), F32),
            shape(inputs.shape, F32),
            shape(inputs.shape, F32),
            *(shape((height, LANES), F32) for height in heights),
        ),
        in_specs=[SMEM] * 2 + [pl.BlockSpec((side, chunk_rows, LANES), lambda n: (n, 0, 0))] + [slot_first] * 2 + [VMEM],
        out_specs=(
            pl.BlockSpec((features, side * WIDE), lambda n: (0, n)),
            pl.BlockSpec((side * WIDE, features), lambda n: (n, 0)),
            place_first,
            place_first,
            *([VMEM] * len(heights)),
        ),
        scratch_shapes=[pltpu.SMEM((slots,), jnp.int32), pltpu.SMEM((slots,), jnp.int32)],
        compiler_params=pltpu.CompilerParams(vmem_limit_bytes=60 << 20),
    )(item_counts, lengths, full.reshape(chunks, chunk_rows, LANES), lo, grad, small)
    gain_one_grad, shift_one_grad, bias_in_grad, bias_out_grad, gain_two_grad, shift_two_grad = [v.reshape(-1) for v in vectors]
    return (
        layer_out, input_grad, gain_one_grad, shift_one_grad, wi_grad, bias_in_grad, wo_grad, bias_out_grad, gain_two_grad, shift_two_grad,
    )


def per_device(
    inputs, item_counts, lengths, gain_one, shift_one, weight_in, bias_in, weight_out, bias_out, gain_two, shift_two, cotangent
):
    rows, slots, features = inputs.shape
    wide = weight_in.shape[1]
    sizes = (lax.axis_size("dp"), lax.axis_size("seq"))
    seq_total = rows * sizes[1]
    chunks = wide // WIDE
    chunk_rows = 2 * features * WIDE // LANES
    shape = jax.ShapeDtypeStruct

    seq_cos, seq_sin = dft_tables(seq_total)
    hid_cos, hid_sin = dft_tables(features)
    seq_table = [table.reshape(sizes[1], rows, seq_total) for table in (seq_cos, seq_sin)]
    seq_table = jnp.asarray(np.concatenate(seq_table, axis=1).astype(jnp.bfloat16))
    hid_table = jnp.asarray(np.concatenate([hid_cos, -hid_sin], axis=0).astype(jnp.bfloat16))
    vectors = (gain_one, shift_one, bias_out, gain_two, shift_two, bias_in)
    operands = (inputs, item_counts, lengths, vectors, weight_in, weight_out, cotangent, seq_table, hid_table)

    few = slots // 2
    *known, choice = run_forward(
        sizes, few, slots,
        item_counts, lengths, *vectors, inputs, cotangent, weight_in, weight_out, seq_table, hid_table,
        agrees=True, cid=1,
    )
    return lax.cond(
        choice[0] == 0,
        lambda known, *given: rest_of_layer(few, sizes, 2, known, *given),
        lambda known, *given: rest_of_layer(slots, sizes, 4, None, *given),
        tuple(known), *operands,
    )


def solution(mesh):
    placed = (
        P("seq", "dp", None), P("dp"), P("dp"), P(), P(), P(), P(), P(), P(), P(), P(), P("seq", "dp", None),
    )
    wide = P("seq", "dp", None)
    return jax.shard_map(
        per_device,
        mesh=mesh,
        in_specs=placed,
        out_specs=(wide, wide, P(), P(), P(), P(), P(), P(), P(), P()),
        check_vma=False,
    )
```

```python
import functools
import math

import jax
import jax.numpy as jnp
import numpy as np
from jax import lax
from jax.experimental import pallas as pl
from jax.experimental.pallas import tpu as pltpu
from jax.sharding import PartitionSpec as P

EPSILON = 1e-05
MESH = pl.DeviceIdType.MESH
LANES = 128
WIDE = 512
BF16 = jnp.bfloat16
F32 = jnp.float32


def dft_tables(count):
    index = np.arange(count, dtype=np.int64)
    turns = (index[:, None] * index[None, :] % count).astype(np.float32)
    angle = (turns * np.float32(2.0 * math.pi / count)).astype(np.float64)
    return np.cos(angle).astype(np.float32), np.sin(angle).astype(np.float32)


def aligned(value, step):
    return pl.multiple_of(value, step)


def bit_of(value, k):
    return (value // k) % 2


def flipped(value, k):
    return value + k * (1 - 2 * bit_of(value, k))


def axis_bits(axis, size):
    return [(axis, 1 << b) for b in range(size.bit_length() - 1)]


class Cube:
    def __init__(self, sizes, mids):
        dp, seq = sizes
        bits = axis_bits(1, seq) + axis_bits(0, dp)
        first, near, rest = bits[:1], bits[1:4], bits[4:]
        self.orders = [first + [near[i] for i in mid] + rest for mid in mids]
        self.bits = bits
        self.stages = len(bits)
        self.me = (lax.axis_index("dp"), lax.axis_index("seq"))
        self.values = {bit: self.value(bit) for bit in bits}
        self.partners = {bit: self.partner(bit) for bit in bits}

    def value(self, bit):
        return bit_of(self.me[bit[0]], bit[1])

    def partner(self, bit):
        axis, k = bit
        other = flipped(self.me[axis], k)
        return (other, self.me[1]) if axis == 0 else (self.me[0], other)

    def offset(self, order, level, rows):
        total = 0
        for s in range(level):
            total = total + self.values[self.orders[order][s]] * (rows >> (s + 1))
        return total


class Exchange:
    def __init__(self, size, rows, buf, send, recv):
        self.size, self.rows, self.buf, self.send_sem, self.recv_sem = size, rows, buf, send, recv
        self.dp, self.q = lax.axis_index("dp"), lax.axis_index("seq")
        self.order = [1 << b for b in reversed(range(size.bit_length() - 1))]

    def owner(self, pattern):
        index = self.q
        for k in self.order:
            if pattern & k:
                index = flipped(index, k)
        return index

    def copy(self, slot, pattern):
        hop = pattern & -pattern
        place = pl.ds(aligned(self.owner(pattern - hop) * self.rows, self.rows), self.rows)
        ref = self.buf.at[slot, place]
        return pltpu.make_async_remote_copy(
            src_ref=ref,
            dst_ref=ref,
            send_sem=self.send_sem.at[slot, pattern],
            recv_sem=self.recv_sem.at[slot, pattern],
            device_id=(self.dp, flipped(self.q, hop)),
            device_id_type=MESH,
        )

    def patterns(self, far):
        return range(1, self.size) if far else range(1, 2)

    def start_own(self, slot, far):
        for pattern in self.patterns(far):
            if pattern & (pattern - 1) == 0:
                self.copy(slot, pattern).start()

    def forward(self, slot):
        for pattern in self.patterns(True):
            if pattern & 1 == 0:
                self.copy(slot, pattern).wait_recv()
                for k in self.order:
                    if k < (pattern & -pattern):
                        self.copy(slot, pattern | k).start()

    def wait_near(self, slot, far):
        for pattern in self.patterns(far):
            if pattern & 1:
                self.copy(slot, pattern).wait_recv()

    def wait_sends(self, slot, far):
        for pattern in self.patterns(far):
            self.copy(slot, pattern).wait_send()


def greet(partners):
    barrier = pltpu.get_barrier_semaphore()
    for partner in partners:
        pl.semaphore_signal(barrier, inc=1, device_id=partner, device_id_type=MESH)
    return lambda: pl.semaphore_wait(barrier, len(partners))


def rank_slots(count_ref, length_ref, perm_s, slen_s, slots):
    count = count_ref[0]
    live = [jnp.where(i < count, length_ref[i], 0) for i in range(slots)]
    ranks = []
    for i in range(slots):
        rank = 0
        for k in range(slots):
            if k != i:
                ahead = live[k] >= live[i] if k < i else live[k] > live[i]
                rank = rank + jnp.where(ahead, 1, 0)
        ranks.append(rank)
    for j in range(slots):
        perm, length = 0, 0
        for i in range(slots):
            here = ranks[i] == j
            perm = perm + jnp.where(here, i, 0)
            length = length + jnp.where(here, live[i], 0)
        perm_s[j] = perm
        slen_s[j] = length


def live_rows(slen_s, slot, first, rows):
    position = first + lax.broadcasted_iota(jnp.int32, (rows, 1), 0)
    return position < slen_s[slot]


def fold8(values):
    rows, lanes = values.shape
    return values.reshape(rows // 8, 8, lanes).sum(axis=0)


def normalize(values):
    center = values - jnp.mean(values, axis=-1, keepdims=True)
    spread = jnp.mean(center * center, axis=-1, keepdims=True)
    inverse = lax.rsqrt(spread + EPSILON)
    return center * inverse, inverse


def norm_back(grad_hat, normal, inverse):
    first = jnp.mean(grad_hat, axis=-1, keepdims=True)
    second = jnp.mean(grad_hat * normal, axis=-1, keepdims=True)
    return inverse * (grad_hat - first - normal * second)


def mix_slot(slot, far, exchange, tables, buf, uv, place):
    rows = exchange.rows
    if far:
        table, block = tables[...], buf[slot]
    else:
        base = aligned(exchange.q // 2 * (2 * rows), 2 * rows)
        table, block = tables[:, pl.ds(base, 2 * rows)], buf[slot, pl.ds(base, 2 * rows), :]
    both = jnp.dot(table, block, preferred_element_type=F32).astype(BF16)
    width = both.shape[1]
    uv[pl.ds(place, rows), :width] = both[:rows]
    uv[pl.ds(place, rows), width:] = both[rows:]


def group_at(i, near_groups, count):
    if near_groups == 0:
        return count - 1 - i
    return jnp.where(i < near_groups, count - near_groups + i, count - 1 - i)


def forward_kernel(cfg, *refs):
    sizes, far_slots, slots, group, agrees = cfg
    if agrees:
        choice_o, (mine, theirs, say_sem, hear_sem) = refs[agrees], refs[-4:]
        refs = refs[:agrees] + refs[agrees + 1 : -4]
    vec_refs, refs = refs[2:8], refs[:2] + refs[8:]
    (
        count_ref, length_ref, x_hbm, cot_hbm, wi_hbm, wo_hbm, sc_hbm, hc_hbm,
        act_o, dg_o, nrm_o, sum_o, gs_o, gb_o, lo_o, part_o,
        perm_s, slen_s, x_v, cot_v, wi_v, wo_v, sc_v, hc_v, buf, uv, sum_v, nrm_v, act_v, dg_v, gs_v, gb_v, lo_v, br_v, vec_ref,
        load_sem, out_sem, send_sem, recv_sem,
    ) = refs
    rows, _, features = x_v.shape
    wide = wi_v.shape[1]
    seq_total = rows * sizes[1]
    scale = 1.0 / math.sqrt(features * seq_total)
    exchange = Exchange(sizes[1], rows, buf, send_sem, recv_sem)
    q = exchange.q
    first = q * rows
    gain_one, shift_one, bias_out, gain_two, shift_two = (lambda i=i: vec_ref[i : i + 1, :] for i in range(5))
    loads = [
        pltpu.make_async_copy(x_hbm, x_v, load_sem.at[0]),
        pltpu.make_async_copy(sc_hbm.at[q], sc_v, load_sem.at[1]),
        pltpu.make_async_copy(hc_hbm, hc_v, load_sem.at[2]),
        pltpu.make_async_copy(wi_hbm, wi_v, load_sem.at[3]),
        pltpu.make_async_copy(wo_hbm, wo_v, load_sem.at[4]),
        pltpu.make_async_copy(cot_hbm, cot_v, load_sem.at[5]),
    ]
    loads[0].start()
    partners = [(exchange.dp, flipped(q, k)) for k in exchange.order]
    peers = [(lax.rem(exchange.dp + i, sizes[0]), q) for i in range(1, sizes[0])] if agrees else []
    met = greet(partners + peers)
    row = 0
    for vec in vec_refs:
        for i in range(vec.shape[0] // features):
            vec_ref[row : row + 1, :] = vec[pl.ds(i * features, features)].reshape(1, features)
            row += 1
    rank_slots(count_ref, length_ref, perm_s, slen_s, slots)
    for load in loads[1:3]:
        load.start()
    loads[0].wait()
    loads[3].start()
    met()

    def word(i):
        return pltpu.make_async_remote_copy(
            src_ref=mine,
            dst_ref=theirs.at[i],
            send_sem=say_sem.at[i],
            recv_sem=hear_sem.at[i],
            device_id=peers[i - 1],
            device_id_type=MESH,
        )

    if agrees:
        long = 0
        for i in range(slots):
            long = long + jnp.where((i < count_ref[0]) & (length_ref[i] > 2 * rows), 1, 0)
        mine[...] = jnp.full(mine.shape, long, jnp.int32).astype(F32)
        theirs[0] = mine[...]
        for i in range(1, sizes[0]):
            word(i).start()

    def prepare(i, _):
        slot = jnp.where(i < slots - far_slots, far_slots + i, slots - 1 - i)
        value = jnp.where(live_rows(slen_s, slot, first, rows), x_v[:, perm_s[slot], :], 0.0)
        buf[slot, pl.ds(aligned(first, rows), rows), :] = value.astype(BF16)
        pl.when(slot < far_slots)(lambda: exchange.start_own(slot, True))
        if far_slots < slots:
            pl.when(slot >= far_slots)(lambda: exchange.start_own(slot, False))
        return 0

    lax.fori_loop(0, slots, prepare, 0)
    part_o[...] = jnp.zeros_like(part_o)
    for load in loads[1:3]:
        load.wait()

    batch = group * rows
    folds = 2 if wide % (2 * features) == 0 else 1
    span = folds * features
    count = slots // group
    near_groups = (slots - far_slots) // group

    def outs(base):
        place = pl.ds(base, batch)
        early = [
            pltpu.make_async_copy(nrm_v.at[place], nrm_o.at[place], out_sem.at[0]),
            pltpu.make_async_copy(sum_v.at[place], sum_o.at[place], out_sem.at[1]),
        ]
        for n in range(wide // WIDE):
            cut = pl.ds(n * WIDE, WIDE)
            early.append(pltpu.make_async_copy(act_v.at[place, cut], act_o.at[n, place], out_sem.at[4]))
            early.append(pltpu.make_async_copy(dg_v.at[place, cut], dg_o.at[n, place], out_sem.at[5]))
        late = [
            pltpu.make_async_copy(gs_v.at[place], gs_o.at[place], out_sem.at[2]),
            pltpu.make_async_copy(lo_v.at[place], lo_o.at[place], out_sem.at[3]),
            pltpu.make_async_copy(gb_v.at[place], gb_o.at[place], out_sem.at[6]),
        ]
        return early, late

    def bring(slot0):
        for k in reversed(range(group)):
            exchange.forward(slot0 + k)

    def mixing(slot0, far):
        for k in reversed(range(group)):
            exchange.wait_near(slot0 + k, far)
            mix_slot(slot0 + k, far, exchange, sc_v, buf, uv, k * rows)

    def work(i, _):
        slot0 = group_at(i, near_groups, count) * group
        base = aligned(slot0 * rows, batch)
        place = pl.ds(base, batch)
        if near_groups < count:
            pl.when(i >= near_groups)(lambda: mixing(slot0, True))
        if near_groups > 0:
            pl.when(i < near_groups)(lambda: mixing(slot0, False))
        br_v[...] = jnp.dot(uv[...], hc_v[...], preferred_element_type=F32)

        for k in range(group):
            here = pl.ds(aligned(base + k * rows, rows), rows)
            mixed = (br_v[k * rows : (k + 1) * rows, :] * scale).astype(BF16).astype(F32)
            live = live_rows(slen_s, slot0 + k, first, rows)
            total = jnp.where(live, x_v[:, perm_s[slot0 + k], :], 0.0) + mixed
            sum_v[here, :] = total
            hat, _ = normalize(total)
            nrm_v[here, :] = (hat * gain_one() + shift_one()).astype(BF16)

        @pl.when(i == 0)
        def _():
            loads[3].wait()
            for load in loads[4:]:
                load.start()

        def expand(n, _):
            cut = pl.ds(aligned(n * span, span), span)
            bias = [vec_ref[pl.ds(5 + folds * n + i, 1), :] for i in range(folds)]
            hidden = jnp.dot(nrm_v[place, :], wi_v[:, cut], preferred_element_type=F32) + jnp.concatenate(bias, axis=1)
            gate = 0.5 + 0.5 * lax.erf(hidden * math.sqrt(0.5))
            slope = gate + hidden * (jnp.exp(hidden * hidden * -0.5) * (1.0 / math.sqrt(2.0 * math.pi)))
            act_v[place, cut] = (hidden * gate).astype(BF16)
            dg_v[place, cut] = slope.astype(BF16)
            return 0

        lax.fori_loop(0, wide // span, expand, 0)
        for copy in outs(base)[0]:
            copy.start()
        if near_groups < count:

            @pl.when((i + 1 >= near_groups) & (i + 1 < count))
            def _():
                bring(group_at(i + 1, near_groups, count) * group)

        pl.when(i == 0)(loads[4].wait)
        br_v[...] = jnp.dot(act_v[place, :], wo_v[...], preferred_element_type=F32)

        def norm_two(k, _):
            here = pl.ds(aligned(base + k * rows, rows), rows)
            local = pl.ds(aligned(k * rows, rows), rows)
            slot = slot0 + k
            live = live_rows(slen_s, slot, first, rows)
            hat, inverse = normalize(sum_v[here, :] + (br_v[local, :] + bias_out()))
            grad = jnp.where(live, cot_v[:, perm_s[slot], :], 0.0)
            lo_v[here, :] = jnp.where(live, hat * gain_two() + shift_two(), 0.0).astype(BF16)
            part_o[0:8, :] = part_o[0:8, :] + fold8(grad * hat)
            part_o[8:16, :] = part_o[8:16, :] + fold8(grad)
            second = norm_back(grad * gain_two(), hat, inverse)
            low = second.astype(BF16)
            gs_v[here, :] = second
            gb_v[here, :] = low
            part_o[16:24, :] = part_o[16:24, :] + fold8(low.astype(F32))
            return 0

        pl.when(i == 0)(loads[5].wait)
        lax.fori_loop(0, group, norm_two, 0)
        for copy in outs(base)[1]:
            copy.start()
        return 0

    if near_groups == 0:
        bring((count - 1) * group)
    lax.fori_loop(0, count, work, 0)

    def finish(slot, _):
        pl.when(slot < far_slots)(lambda: exchange.wait_sends(slot, True))
        if far_slots < slots:
            pl.when(slot >= far_slots)(lambda: exchange.wait_sends(slot, False))
        return 0

    lax.fori_loop(0, slots, finish, 0)

    if agrees:
        for i in range(1, sizes[0]):
            word(i).wait()
        choice_o[0] = jnp.where(jnp.max(theirs[...]) > far_slots, 1, 0)

    def flush(g, _):
        for copies in outs(aligned(g * batch, batch)):
            for copy in copies:
                copy.wait()
        return 0

    lax.fori_loop(0, count, flush, 0)


def backward_kernel(cfg, *refs):
    sizes, far_slots, slots, group, parts, mids, lags, plan = cfg
    cube = Cube(sizes, mids)
    S = cube.stages
    (
        count_ref, length_ref, gain_ref, part_ref,
        act_hbm, dg_hbm, nrm_hbm, sum_hbm, gs_hbm, gb_hbm, wi_hbm, wo_hbm, sc_hbm, hc_hbm,
        full_o, ig_o, small_o,
        perm_s, slen_s, gs_v, sum_v, nrm_v, gb_v, gh_v, gn_v, act_v, dg_v, wi_v, wo_v, sc_v, hc_v, buf, uv, mix_v, ig_v,
        bin_v, one_v, small_v, gain_v, part_v, full,
    ) = refs[:41]
    landed = refs[41 : 41 + S]
    (
        small_recv, load_sem, sum_sem, stream_sem, out_sem, ig_sem, send_sem, recv_sem,
        rs_s, rs_r, ag_s, ag_r, sm_s, sm_r,
    ) = refs[41 + S :]
    ticks, tick_rows, _ = part_v.shape
    message = tick_rows // parts
    chunks = act_hbm.shape[0]
    per_tick = chunks // ticks
    features = nrm_v.shape[1]
    rows = gs_v.shape[0] // slots
    batch = group * rows
    scale = 1.0 / math.sqrt(features * rows * sizes[1])
    exchange = Exchange(sizes[1], rows, buf, send_sem, recv_sem)
    q = exchange.q
    first = q * rows
    loads = [
        pltpu.make_async_copy(gb_hbm, gb_v, load_sem.at[0]),
        pltpu.make_async_copy(nrm_hbm, nrm_v, load_sem.at[1]),
        pltpu.make_async_copy(gs_hbm, gs_v, load_sem.at[2]),
        pltpu.make_async_copy(sc_hbm.at[q], sc_v, load_sem.at[3]),
        pltpu.make_async_copy(hc_hbm, hc_v, load_sem.at[4]),
    ]

    def turn(i):
        return jnp.where(i < far_slots, far_slots - 1 - i, i) if far_slots < slots else slots - 1 - i

    def sum_copy(i):
        place = pl.ds(aligned(turn(i) * rows, rows), rows)
        return pltpu.make_async_copy(sum_hbm.at[place], sum_v.at[lax.rem(i, 2)], sum_sem.at[lax.rem(i, 2)])

    def streams(n, slot):
        cut = pl.ds(aligned(n * WIDE, WIDE), WIDE)
        return [
            pltpu.make_async_copy(act_hbm.at[n], act_v.at[slot], stream_sem.at[0, slot]),
            pltpu.make_async_copy(wo_hbm.at[cut], wo_v.at[slot], stream_sem.at[1, slot]),
            pltpu.make_async_copy(dg_hbm.at[n], dg_v.at[slot], stream_sem.at[2, slot]),
            pltpu.make_async_copy(wi_hbm.at[:, cut], wi_v.at[slot], stream_sem.at[3, slot]),
        ]

    loads[0].start()
    streams(0, 0)[0].start()
    met = greet([cube.partner(bit) for bit in cube.bits])
    rank_slots(count_ref, length_ref, perm_s, slen_s, slots)

    starts = [[j * message + cube.offset(j, level, message) for level in range(S + 1)] for j in range(parts)]

    def rs(m, t, j, s):
        bit = cube.orders[j][s]
        half = message >> (s + 1)
        off = starts[j][s] + (1 - cube.values[bit]) * half
        return pltpu.make_async_remote_copy(
            src_ref=part_v.at[t, pl.ds(aligned(off, 16), half)],
            dst_ref=landed[s].at[m],
            send_sem=rs_s.at[s],
            recv_sem=rs_r.at[s, m],
            device_id=cube.partners[bit],
            device_id_type=MESH,
        )

    def ag(m, t, j, s):
        bit = cube.orders[j][s]
        half = message >> (s + 1)
        ref = full.at[t, pl.ds(aligned(starts[j][s + 1], 16), half)]
        return pltpu.make_async_remote_copy(
            src_ref=ref,
            dst_ref=ref,
            send_sem=ag_s.at[s],
            recv_sem=ag_r.at[s, m],
            device_id=cube.partners[bit],
            device_id_type=MESH,
        )

    def add(m, t, j, s):
        half = message >> (s + 1)
        place = pl.ds(aligned(starts[j][s + 1], 16), half)
        total = part_v[t, place, :].astype(F32) + landed[s][m].astype(F32)
        target = full if s == S - 1 else part_v
        target[t, place, :] = total.astype(BF16)

    def out(t, j):
        place = pl.ds(j * message, message)
        return pltpu.make_async_copy(full.at[t, place], full_o.at[t, place], out_sem.at[t, j])

    def event(k, m, t, j):
        if k == 0:
            rs(m, t, j, 0).start()
        elif k <= S:
            rs(m, t, j, k - 1).wait_recv()
            add(m, t, j, k - 1)
            (rs(m, t, j, k) if k < S else ag(m, t, j, S - 1)).start()
        elif k < 2 * S:
            s = 2 * S - k
            ag(m, t, j, s).wait_recv()
            ag(m, t, j, s - 1).start()
        else:
            ag(m, t, j, 0).wait_recv()
            out(t, j).start()

    def sends_done():
        for s in range(S):
            for sem in (rs_s.at[s], ag_s.at[s]):
                pltpu.make_async_copy(landed[s], landed[s], sem).wait()

    when = [0 if per_tick == 1 and parts == 4 else parts]
    for lag in lags:
        when.append(when[-1] + lag)

    def events(tick, j):
        for k in reversed(range(2 * S + 1)):
            t = tick + (j - when[k]) // parts
            jj = (j - when[k]) % parts
            pl.when((t >= 0) & (t < ticks))(functools.partial(event, k, t * parts + jj, t, jj))

    bin_v[...] = jnp.zeros_like(bin_v)
    one_v[...] = jnp.zeros_like(one_v)
    gain_v[...] = gain_ref[...].reshape(1, features)
    gn_v[...] = jnp.zeros_like(gn_v)
    small_v[...] = jnp.zeros_like(small_v)
    loads[0].wait()
    for copy in streams(0, 0)[1:]:
        copy.start()
    loads[1].start()
    met()

    def load_rest():
        for load in loads[2:]:
            load.start()
        for i in range(2):
            sum_copy(i).start()


    def contract(left, right, dims):
        return lax.dot_general(left, right, ((dims, dims), ((), ())), preferred_element_type=F32)

    def weigh_out(n, slot, t, base):
        streams(n, slot)[0].wait()
        grad = contract(act_v[slot], gb_v[...], (0,)).astype(BF16)
        for i in range(features // LANES):
            part_v[t, pl.ds(base + i * WIDE, WIDE), :] = grad[:, i * LANES : (i + 1) * LANES]

    def pull(n, slot, t, base):
        streams(n, slot)[1].wait()
        streams(n, slot)[2].wait()
        pulled = contract(gb_v[...], wo_v[slot], (1,)) * dg_v[slot].astype(F32)
        pulled = pulled.astype(BF16)
        gh_v[...] = pulled
        bin_v[n] = fold8(pulled.astype(F32))

    def weigh_in(n, slot, t, base):
        pl.when(n == 0)(loads[1].wait)
        grad = contract(nrm_v[...], gh_v[...], (0,)).astype(BF16)
        for i in range(WIDE // LANES):
            place = pl.ds(base + features // LANES * WIDE + i * features, features)
            part_v[t, place, :] = grad[:, i * LANES : (i + 1) * LANES]

    def spread(n, slot, t, base):
        streams(n, slot)[3].wait()
        for i in range(2):
            here = pl.ds(i * (slots // 2) * rows, slots // 2 * rows)
            gn_v[here, :] = gn_v[here, :] + contract(gh_v[here, :], wi_v[slot], (1,))

    steps = [weigh_out, pull, weigh_in, spread]

    def compute(tick, j):
        if per_tick == 1 and parts == 4:
            slot = lax.rem(tick, 2)
            if j == 0:
                for copy in streams(tick + 1, 1 - slot):
                    pl.when(tick + 1 < chunks)(copy.start)
            steps[j](tick, slot, tick, 0)
        elif j == 0:

            def whole(u, _):
                n = tick * per_tick + u
                slot = lax.rem(n, 2)
                for copy in streams(n + 1, 1 - slot):
                    pl.when(n + 1 < chunks)(copy.start)
                for step in steps:
                    step(n, slot, tick, aligned(u * (tick_rows // per_tick), LANES))
                return 0

            lax.fori_loop(0, per_tick, whole, 0)

    def back(i, _):
        slot = turn(i)
        here = pl.ds(aligned(slot * rows, rows), rows)
        pl.when(i == 0)(loads[2].wait)
        sum_copy(i).wait()
        hat, inverse = normalize(sum_v[lax.rem(i, 2)])
        grad = gn_v[here, :]
        one_v[0:8, :] = one_v[0:8, :] + fold8(grad * hat)
        one_v[8:16, :] = one_v[8:16, :] + fold8(grad)
        grad = gs_v[here, :] + norm_back(grad * gain_v[...], hat, inverse)
        gs_v[here, :] = grad
        buf[slot, pl.ds(aligned(first, rows), rows), :] = grad.astype(BF16)
        pl.when(i < far_slots)(lambda: exchange.start_own(slot, True))
        if far_slots < slots:
            pl.when(i >= far_slots)(lambda: exchange.start_own(slot, False))
        pl.when(i + 2 < slots)(lambda: sum_copy(i + 2).start())
        return 0

    def small_copy(s):
        return pltpu.make_async_remote_copy(
            src_ref=small_v.at[s],
            dst_ref=small_recv.at[s],
            send_sem=sm_s.at[s],
            recv_sem=sm_r.at[s],
            device_id=cube.partners[cube.bits[s]],
            device_id_type=MESH,
        )

    def small_start():
        row = 0
        vectors = [one_v[0:8, :], one_v[8:16, :]] + [bin_v[n] for n in range(chunks)]
        vectors += [part_ref[16:24, :], part_ref[0:8, :], part_ref[8:16, :]]
        for vector in vectors:
            vector = jnp.sum(vector, axis=0, keepdims=True)
            for i in range(vector.shape[1] // LANES):
                small_v[0, row : row + 1, :] = vector[:, i * LANES : (i + 1) * LANES]
                row += 1
        small_copy(0).start()

    def small_step(s):
        small_copy(s).wait()
        if s + 1 < S:
            small_v[s + 1] = small_v[s] + small_recv[s]
            small_copy(s + 1).start()
        else:
            small_o[...] = small_v[s] + small_recv[s]

    count = slots // group
    near_groups = (slots - far_slots) // group

    def grad_copy(i):
        base = aligned(group_at(i, near_groups, count) * batch, batch)
        return pltpu.make_async_copy(ig_v.at[lax.rem(i, 2)], ig_o.at[pl.ds(base, batch)], ig_sem.at[lax.rem(i, 2)])

    def mixing(i, k, far):
        slot = group_at(i, near_groups, count) * group + k
        exchange.wait_near(slot, far)
        mix_slot(slot, far, exchange, sc_v, buf, uv, k * rows)

    def hidden_mix(i):
        pl.when(i >= 2)(lambda: grad_copy(i - 2).wait())
        mix_v[...] = jnp.dot(uv[...], hc_v[...], preferred_element_type=F32)

    def finish(i):
        for k in range(group):
            slot = group_at(i, near_groups, count) * group + k
            here = pl.ds(aligned(slot * rows, rows), rows)
            local = pl.ds(k * rows, rows)
            grad = gs_v[here, :] + mix_v[local, :] * scale
            grad = jnp.where(live_rows(slen_s, slot, first, rows), grad, 0.0)
            ig_v[lax.rem(i, 2), local, :] = grad.astype(BF16)
        grad_copy(i).start()

    def bring(i):
        for k in reversed(range(group)):
            exchange.forward(group_at(i, near_groups, count) * group + k)

    small_at, near_at, far_at, lead = plan

    def drain(tick, j):
        d = tick - ticks

        @pl.when(d == 0)
        def _():
            share = -(-slots // parts)
            lax.fori_loop(min(j * share, slots), min((j + 1) * share, slots), back, 0)

        here = lambda at: pl.when(d * parts + j == at)
        if j == small_at % parts:
            here(small_at)(small_start)
        for s in range(S):
            at = small_at + 3 * (s + 1)
            if j == at % parts:
                here(at)(functools.partial(small_step, s))
        if j == 0:

            @pl.when(d == 1)
            def _():
                for load in loads[3:]:
                    load.wait()

        for far, start, low, high in ((False, near_at, 0, near_groups), (True, far_at, near_groups, count)):
            if low == high:
                continue
            i = d - start + low

            @pl.when((i >= low) & (i < high))
            def _():
                subs = [
                    lambda: mixing(i, 0, far),
                    lambda: [mixing(i, k, far) for k in range(1, group)],
                    lambda: hidden_mix(i),
                    lambda: finish(i),
                ]
                for at, sub in enumerate(subs):
                    if min(at, parts - 1) == j:
                        sub()

            if far and j == parts - 1:
                ahead = i + lead
                pl.when((ahead >= low) & (ahead < high))(lambda: bring(ahead))

    last = ticks + max(
        -(-(when[-1] + 1) // parts),
        (small_at + 3 * S) // parts + 1,
        near_at + near_groups,
        far_at + count - near_groups,
    )

    def body(tick, _):
        pl.when(tick == 1)(load_rest)
        for j in range(parts):
            pl.when(tick < ticks)(lambda: compute(tick, j))
            events(tick, j)
            pl.when(tick >= ticks)(lambda: drain(tick, j))
        return 0

    lax.fori_loop(0, last, body, 0)

    def settle(slot, _):
        pl.when(slot < far_slots)(lambda: exchange.wait_sends(slot, True))
        if far_slots < slots:
            pl.when(slot >= far_slots)(lambda: exchange.wait_sends(slot, False))
        return 0

    lax.fori_loop(0, slots, settle, 0)
    for i in range(max(0, count - 2), count):
        grad_copy(i).wait()

    def finish_out(t, _):
        for j in range(parts):
            out(t, j).wait()
        return 0

    lax.fori_loop(0, ticks, finish_out, 0)
    sends_done()


def output_kernel(slots, cuts, places, count_ref, length_ref, full_ref, lo_ref, ig_ref, small_ref, *refs):
    wi_ref, wo_ref, lo_out, ig_out = refs[:4]
    vector_refs, (perm_s, slen_s) = refs[4:-2], refs[-2:]
    step = pl.program_id(0)
    features = wi_ref.shape[0]
    for u in range(full_ref.shape[0]):
        base = u * WIDE
        for i in range(features // LANES):
            wo_ref[base : base + WIDE, i * LANES : (i + 1) * LANES] = full_ref[u, pl.ds(i * WIDE, WIDE), :].astype(F32)
        for i in range(WIDE // LANES):
            start = features // LANES * WIDE + i * features
            wi_ref[:, base + i * LANES : base + (i + 1) * LANES] = full_ref[u, pl.ds(start, features), :].astype(F32)

    @pl.when(step == 0)
    def _():
        rank_slots(count_ref, length_ref, perm_s, slen_s, slots)
        for ref, start in zip(vector_refs, cuts):
            ref[...] = small_ref[start : start + ref.shape[0], :]

    @pl.when(step < places)
    def _():
        for j in range(slots):
            lo_out[:, perm_s[j], :] = lo_ref[j].astype(F32)
            ig_out[:, perm_s[j], :] = ig_ref[j].astype(F32)


ANY = pl.BlockSpec(memory_space=pl.ANY)
SMEM = pl.BlockSpec(memory_space=pltpu.SMEM)
VMEM = pl.BlockSpec(memory_space=pltpu.VMEM)
DMA = pltpu.SemaphoreType.DMA
LAGS = [3, 5, 4, 3, 3, 3, 3, 4, 6, 3]
PLAN = (4, 1, 4, 1)
FAR_PLAN = (4, 1, 4, 1)
MIDS = ((0, 1, 2), (1, 0, 2), (2, 0, 1), (1, 2, 0))
FAR_MIDS = ((1, 2, 0), (2, 1, 0), (1, 0, 2), (2, 0, 1))


def run_forward(sizes, far_slots, slots, *operands, agrees=False, group=2, name="forward", cid=1):
    rows, _, features = operands[8].shape
    wide = operands[10].shape[1]
    seq_total = rows * sizes[1]
    flat, batch, chunks = rows * slots, group * rows, wide // WIDE
    shape = jax.ShapeDtypeStruct
    return pl.pallas_call(
        functools.partial(forward_kernel, (sizes, far_slots, slots, group, len(operands) + 8 if agrees else 0)),
        name=name,
        out_shape=(
            shape((chunks, flat, WIDE), BF16),
            shape((chunks, flat, WIDE), BF16),
            shape((flat, features), BF16),
            shape((flat, features), F32),
            shape((flat, features), F32),
            shape((flat, features), BF16),
            shape((flat, features), BF16),
            shape((24, features), F32),
        )
        + ((shape((1,), jnp.int32),) if agrees else ()),
        in_specs=[SMEM] * 2 + [VMEM] * 6 + [ANY] * 6,
        out_specs=[ANY] * 7 + [VMEM] + [SMEM] * agrees,
        scratch_shapes=[
            pltpu.SMEM((slots,), jnp.int32),
            pltpu.SMEM((slots,), jnp.int32),
            pltpu.VMEM((rows, slots, features), F32),
            pltpu.VMEM((rows, slots, features), F32),
            pltpu.VMEM((features, wide), BF16),
            pltpu.VMEM((wide, features), BF16),
            pltpu.VMEM((2 * rows, seq_total), BF16),
            pltpu.VMEM((2 * features, features), BF16),
            pltpu.VMEM((slots, seq_total, features), BF16),
            pltpu.VMEM((batch, 2 * features), BF16),
            pltpu.VMEM((flat, features), F32),
            pltpu.VMEM((flat, features), BF16),
            pltpu.VMEM((flat, wide), BF16),
            pltpu.VMEM((flat, wide), BF16),
            pltpu.VMEM((flat, features), F32),
            pltpu.VMEM((flat, features), BF16),
            pltpu.VMEM((flat, features), BF16),
            pltpu.VMEM((batch, features), F32),
            pltpu.VMEM((5 + wide // features, features), F32),
            DMA((6,)),
            DMA((7,)),
            DMA((slots, sizes[1])),
            DMA((slots, sizes[1])),
        ]
        + agrees * [pltpu.VMEM((8, LANES), F32), pltpu.VMEM((sizes[0], 8, LANES), F32), DMA((sizes[0],)), DMA((sizes[0],))],
        compiler_params=pltpu.CompilerParams(collective_id=cid, has_side_effects=True, vmem_limit_bytes=62 << 20),
    )(*operands)


def run_backward(sizes, far_slots, slots, ticks, tick_rows, parts, *operands, group=2, mids=None, lags=None, plan=None, name="backward", cid=2):
    devices = sizes[0] * sizes[1]
    chunks, flat, _ = operands[4].shape
    features, wide = operands[10].shape
    rows = flat // slots
    seq_total = rows * sizes[1]
    batch = group * rows
    message = tick_rows // parts
    shape = jax.ShapeDtypeStruct
    mostly_far = far_slots > slots * 5 // 8
    mids = mids or (FAR_MIDS if mostly_far else MIDS)
    plan = plan or (FAR_PLAN if mostly_far else PLAN)
    lags = lags or LAGS
    stages = devices.bit_length() - 1
    lags = (lags[:stages] + [2] * stages)[:stages] + ([2] * stages + lags[-stages:])[-stages:]
    return pl.pallas_call(
        functools.partial(backward_kernel, (sizes, far_slots, slots, group, parts, mids, lags, plan)),
        name=name,
        out_shape=(
            shape((ticks, tick_rows, LANES), BF16),
            shape((flat, features), BF16),
            shape((64, LANES), F32),
        ),
        in_specs=[SMEM] * 2 + [VMEM] * 2 + [ANY] * 10,
        out_specs=[ANY] * 2 + [VMEM],
        scratch_shapes=[
            pltpu.SMEM((slots,), jnp.int32),
            pltpu.SMEM((slots,), jnp.int32),
            pltpu.VMEM((flat, features), F32),
            pltpu.VMEM((2, rows, features), F32),
            pltpu.VMEM((flat, features), BF16),
            pltpu.VMEM((flat, features), BF16),
            pltpu.VMEM((flat, WIDE), BF16),
            pltpu.VMEM((flat, features), F32),
            pltpu.VMEM((2, flat, WIDE), BF16),
            pltpu.VMEM((2, flat, WIDE), BF16),
            pltpu.VMEM((2, features, WIDE), BF16),
            pltpu.VMEM((2, WIDE, features), BF16),
            pltpu.VMEM((2 * rows, seq_total), BF16),
            pltpu.VMEM((2 * features, features), BF16),
            pltpu.VMEM((slots, seq_total, features), BF16),
            pltpu.VMEM((batch, 2 * features), BF16),
            pltpu.VMEM((batch, features), F32),
            pltpu.VMEM((2, batch, features), BF16),
            pltpu.VMEM((chunks, 8, WIDE), F32),
            pltpu.VMEM((16, features), F32),
            pltpu.VMEM((stages, 64, LANES), F32),
            pltpu.VMEM((1, features), F32),
            pltpu.VMEM((ticks, tick_rows, LANES), BF16),
            pltpu.VMEM((ticks, tick_rows, LANES), BF16),
        ]
        + [pltpu.VMEM((ticks * parts, message >> (s + 1), LANES), BF16) for s in range(stages)]
        + [
            pltpu.VMEM((stages, 64, LANES), F32),
            DMA((5,)),
            DMA((2,)),
            DMA((4, 2)),
            DMA((ticks, parts)),
            DMA((2,)),
            DMA((slots, sizes[1])),
            DMA((slots, sizes[1])),
            DMA((stages,)),
            DMA((stages, ticks * parts)),
            DMA((stages,)),
            DMA((stages, ticks * parts)),
            DMA((stages,)),
            DMA((stages,)),
        ],
        compiler_params=pltpu.CompilerParams(collective_id=cid, has_side_effects=True, vmem_limit_bytes=62 << 20),
    )(*operands)


def cut_messages(devices, chunks, chunk_rows):
    per_tick, parts = min(
        (count, -cut)
        for count in range(1, chunks + 1)
        for cut in range(1, 5)
        if chunks % count == 0 and chunk_rows * count % (devices * 16 * cut) == 0
    )
    return per_tick, -parts


def rest_of_layer(far_slots, sizes, cid, known, inputs, item_counts, lengths, vectors, weight_in, weight_out, cotangent, seq_table, hid_table):
    rows, slots, features = inputs.shape
    wide = weight_in.shape[1]
    chunks = wide // WIDE
    chunk_rows = 2 * features * WIDE // LANES
    shape = jax.ShapeDtypeStruct
    per_tick, parts = cut_messages(sizes[0] * sizes[1], chunks, chunk_rows)
    act, dg, nrm, summed, second, low, lo, part = known or run_forward(
        sizes, far_slots, slots,
        item_counts, lengths, *vectors, inputs, cotangent, weight_in, weight_out, seq_table, hid_table,
        cid=cid,
    )
    full, grad, small = run_backward(
        sizes, far_slots, slots, chunks // per_tick, chunk_rows * per_tick, parts,
        item_counts, lengths, vectors[0], part, act, dg, nrm, summed, second, low, weight_in, weight_out, seq_table, hid_table,
        cid=cid + 1,
    )
    side = 2 if chunks % 2 == 0 else 1
    places = 1 << min((chunks // side).bit_length() - 1, 3)
    step = rows // places
    lo, grad = lo.reshape(slots, rows, features), grad.reshape(slots, rows, features)
    heights = [size // LANES for size in (features, features, wide, features, features, features)]
    cuts = [sum(heights[:i]) for i in range(len(heights))]
    slot_first = pl.BlockSpec((slots, step, features), lambda n: (0, jnp.minimum(n, places - 1), 0))
    place_first = pl.BlockSpec((step, slots, features), lambda n: (jnp.minimum(n, places - 1), 0, 0))
    wi_grad, wo_grad, layer_out, input_grad, *vectors = pl.pallas_call(
        functools.partial(output_kernel, slots, cuts, places),
        name="output",
        grid=(chunks // side,),
        out_shape=(
            shape((features, wide), F32),
            shape((wide, features), F32),
            shape(inputs.shape, F32),
            shape(inputs.shape, F32),
            *(shape((height, LANES), F32) for height in heights),
        ),
        in_specs=[SMEM] * 2 + [pl.BlockSpec((side, chunk_rows, LANES), lambda n: (n, 0, 0))] + [slot_first] * 2 + [VMEM],
        out_specs=(
            pl.BlockSpec((features, side * WIDE), lambda n: (0, n)),
            pl.BlockSpec((side * WIDE, features), lambda n: (n, 0)),
            place_first,
            place_first,
            *([VMEM] * len(heights)),
        ),
        scratch_shapes=[pltpu.SMEM((slots,), jnp.int32), pltpu.SMEM((slots,), jnp.int32)],
        compiler_params=pltpu.CompilerParams(vmem_limit_bytes=60 << 20),
    )(item_counts, lengths, full.reshape(chunks, chunk_rows, LANES), lo, grad, small)
    gain_one_grad, shift_one_grad, bias_in_grad, bias_out_grad, gain_two_grad, shift_two_grad = [v.reshape(-1) for v in vectors]
    return (
        layer_out, input_grad, gain_one_grad, shift_one_grad, wi_grad, bias_in_grad, wo_grad, bias_out_grad, gain_two_grad, shift_two_grad,
    )


def per_device(
    inputs, item_counts, lengths, gain_one, shift_one, weight_in, bias_in, weight_out, bias_out, gain_two, shift_two, cotangent
):
    rows, slots, features = inputs.shape
    wide = weight_in.shape[1]
    sizes = (lax.axis_size("dp"), lax.axis_size("seq"))
    seq_total = rows * sizes[1]
    chunks = wide // WIDE
    chunk_rows = 2 * features * WIDE // LANES
    shape = jax.ShapeDtypeStruct

    seq_cos, seq_sin = dft_tables(seq_total)
    hid_cos, hid_sin = dft_tables(features)
    seq_table = [table.reshape(sizes[1], rows, seq_total) for table in (seq_cos, seq_sin)]
    seq_table = jnp.asarray(np.concatenate(seq_table, axis=1).astype(jnp.bfloat16))
    hid_table = jnp.asarray(np.concatenate([hid_cos, -hid_sin], axis=0).astype(jnp.bfloat16))
    vectors = (gain_one, shift_one, bias_out, gain_two, shift_two, bias_in)
    operands = (inputs, item_counts, lengths, vectors, weight_in, weight_out, cotangent, seq_table, hid_table)

    few = slots // 2
    *known, choice = run_forward(
        sizes, few, slots,
        item_counts, lengths, *vectors, inputs, cotangent, weight_in, weight_out, seq_table, hid_table,
        agrees=True, cid=1,
    )
    return lax.cond(
        choice[0] == 0,
        lambda known, *given: rest_of_layer(few, sizes, 2, known, *given),
        lambda known, *given: rest_of_layer(slots, sizes, 4, None, *given),
        tuple(known), *operands,
    )


def solution(mesh):
    placed = (
        P("seq", "dp", None), P("dp"), P("dp"), P(), P(), P(), P(), P(), P(), P(), P(), P("seq", "dp", None),
    )
    wide = P("seq", "dp", None)
    return jax.shard_map(
        per_device,
        mesh=mesh,
        in_specs=placed,
        out_specs=(wide, wide, P(), P(), P(), P(), P(), P(), P(), P()),
        check_vma=False,
    )
```

```python
import functools
import math

import jax
import jax.numpy as jnp
import numpy as np
from jax import lax
from jax.experimental import pallas as pl
from jax.experimental.pallas import tpu as pltpu
from jax.sharding import PartitionSpec as P

EPSILON = 1e-05
MESH = pl.DeviceIdType.MESH
LANES = 128
WIDE = 512
BF16 = jnp.bfloat16
F32 = jnp.float32


def dft_tables(count):
    index = np.arange(count, dtype=np.int64)
    turns = (index[:, None] * index[None, :] % count).astype(np.float32)
    angle = (turns * np.float32(2.0 * math.pi / count)).astype(np.float64)
    return np.cos(angle).astype(np.float32), np.sin(angle).astype(np.float32)


def aligned(value, step):
    return pl.multiple_of(value, step)


def bit_of(value, k):
    return (value // k) % 2


def flipped(value, k):
    return value + k * (1 - 2 * bit_of(value, k))


def axis_bits(axis, size):
    return [(axis, 1 << b) for b in range(size.bit_length() - 1)]


class Cube:
    def __init__(self, sizes, mids):
        dp, seq = sizes
        bits = axis_bits(1, seq) + axis_bits(0, dp)
        first, near, rest = bits[:1], bits[1:4], bits[4:]
        self.orders = [first + [near[i] for i in mid] + rest for mid in mids]
        self.bits = bits
        self.stages = len(bits)
        self.me = (lax.axis_index("dp"), lax.axis_index("seq"))
        self.values = {bit: self.value(bit) for bit in bits}
        self.partners = {bit: self.partner(bit) for bit in bits}

    def value(self, bit):
        return bit_of(self.me[bit[0]], bit[1])

    def partner(self, bit):
        axis, k = bit
        other = flipped(self.me[axis], k)
        return (other, self.me[1]) if axis == 0 else (self.me[0], other)

    def offset(self, order, level, rows):
        total = 0
        for s in range(level):
            total = total + self.values[self.orders[order][s]] * (rows >> (s + 1))
        return total


class Exchange:
    def __init__(self, size, rows, buf, send, recv):
        self.size, self.rows, self.buf, self.send_sem, self.recv_sem = size, rows, buf, send, recv
        self.dp, self.q = lax.axis_index("dp"), lax.axis_index("seq")
        self.order = [1 << b for b in reversed(range(size.bit_length() - 1))]

    def owner(self, pattern):
        index = self.q
        for k in self.order:
            if pattern & k:
                index = flipped(index, k)
        return index

    def copy(self, slot, pattern):
        hop = pattern & -pattern
        place = pl.ds(aligned(self.owner(pattern - hop) * self.rows, self.rows), self.rows)
        ref = self.buf.at[slot, place]
        return pltpu.make_async_remote_copy(
            src_ref=ref,
            dst_ref=ref,
            send_sem=self.send_sem.at[slot, pattern],
            recv_sem=self.recv_sem.at[slot, pattern],
            device_id=(self.dp, flipped(self.q, hop)),
            device_id_type=MESH,
        )

    def patterns(self, far):
        return range(1, self.size) if far else range(1, 2)

    def start_own(self, slot, far):
        for pattern in self.patterns(far):
            if pattern & (pattern - 1) == 0:
                self.copy(slot, pattern).start()

    def forward(self, slot):
        for pattern in self.patterns(True):
            if pattern & 1 == 0:
                self.copy(slot, pattern).wait_recv()
                for k in self.order:
                    if k < (pattern & -pattern):
                        self.copy(slot, pattern | k).start()

    def wait_near(self, slot, far):
        for pattern in self.patterns(far):
            if pattern & 1:
                self.copy(slot, pattern).wait_recv()

    def wait_sends(self, slot, far):
        for pattern in self.patterns(far):
            self.copy(slot, pattern).wait_send()


def greet(partners):
    barrier = pltpu.get_barrier_semaphore()
    for partner in partners:
        pl.semaphore_signal(barrier, inc=1, device_id=partner, device_id_type=MESH)
    return lambda: pl.semaphore_wait(barrier, len(partners))


def rank_slots(count_ref, length_ref, perm_s, slen_s, slots):
    count = count_ref[0]
    live = [jnp.where(i < count, length_ref[i], 0) for i in range(slots)]
    ranks = []
    for i in range(slots):
        rank = 0
        for k in range(slots):
            if k != i:
                ahead = live[k] >= live[i] if k < i else live[k] > live[i]
                rank = rank + jnp.where(ahead, 1, 0)
        ranks.append(rank)
    for j in range(slots):
        perm, length = 0, 0
        for i in range(slots):
            here = ranks[i] == j
            perm = perm + jnp.where(here, i, 0)
            length = length + jnp.where(here, live[i], 0)
        perm_s[j] = perm
        slen_s[j] = length


def live_rows(slen_s, slot, first, rows):
    position = first + lax.broadcasted_iota(jnp.int32, (rows, 1), 0)
    return position < slen_s[slot]


def fold8(values):
    rows, lanes = values.shape
    return values.reshape(rows // 8, 8, lanes).sum(axis=0)


def normalize(values):
    center = values - jnp.mean(values, axis=-1, keepdims=True)
    spread = jnp.mean(center * center, axis=-1, keepdims=True)
    inverse = lax.rsqrt(spread + EPSILON)
    return center * inverse, inverse


def norm_back(grad_hat, normal, inverse):
    first = jnp.mean(grad_hat, axis=-1, keepdims=True)
    second = jnp.mean(grad_hat * normal, axis=-1, keepdims=True)
    return inverse * (grad_hat - first - normal * second)


def mix_slot(slot, far, exchange, tables, buf, uv, place):
    rows = exchange.rows
    if far:
        table, block = tables[...], buf[slot]
    else:
        base = aligned(exchange.q // 2 * (2 * rows), 2 * rows)
        table, block = tables[:, pl.ds(base, 2 * rows)], buf[slot, pl.ds(base, 2 * rows), :]
    both = jnp.dot(table, block, preferred_element_type=F32).astype(BF16)
    width = both.shape[1]
    uv[pl.ds(place, rows), :width] = both[:rows]
    uv[pl.ds(place, rows), width:] = both[rows:]


def group_at(i, near_groups, count):
    if near_groups == 0:
        return count - 1 - i
    return jnp.where(i < near_groups, count - near_groups + i, count - 1 - i)


def forward_kernel(cfg, *refs):
    sizes, far_slots, slots, group, agrees = cfg
    if agrees:
        choice_o, (mine, theirs, say_sem, hear_sem) = refs[agrees], refs[-4:]
        refs = refs[:agrees] + refs[agrees + 1 : -4]
    vec_refs, refs = refs[2:8], refs[:2] + refs[8:]
    (
        count_ref, length_ref, x_hbm, cot_hbm, wi_hbm, wo_hbm, sc_hbm, hc_hbm,
        act_o, dg_o, nrm_o, sum_o, gs_o, gb_o, lo_o, part_o,
        perm_s, slen_s, x_v, cot_v, wi_v, wo_v, sc_v, hc_v, buf, uv, sum_v, nrm_v, act_v, dg_v, gs_v, gb_v, lo_v, br_v, vec_ref,
        load_sem, out_sem, send_sem, recv_sem,
    ) = refs
    rows, _, features = x_v.shape
    wide = wi_v.shape[1]
    seq_total = rows * sizes[1]
    scale = 1.0 / math.sqrt(features * seq_total)
    exchange = Exchange(sizes[1], rows, buf, send_sem, recv_sem)
    q = exchange.q
    first = q * rows
    gain_one, shift_one, bias_out, gain_two, shift_two = (lambda i=i: vec_ref[i : i + 1, :] for i in range(5))
    loads = [
        pltpu.make_async_copy(x_hbm, x_v, load_sem.at[0]),
        pltpu.make_async_copy(sc_hbm.at[q], sc_v, load_sem.at[1]),
        pltpu.make_async_copy(hc_hbm, hc_v, load_sem.at[2]),
        pltpu.make_async_copy(wi_hbm, wi_v, load_sem.at[3]),
        pltpu.make_async_copy(wo_hbm, wo_v, load_sem.at[4]),
        pltpu.make_async_copy(cot_hbm, cot_v, load_sem.at[5]),
    ]
    loads[0].start()
    partners = [(exchange.dp, flipped(q, k)) for k in exchange.order]
    peers = [(lax.rem(exchange.dp + i, sizes[0]), q) for i in range(1, sizes[0])] if agrees else []
    met = greet(partners + peers)
    row = 0
    for vec in vec_refs:
        for i in range(vec.shape[0] // features):
            vec_ref[row : row + 1, :] = vec[pl.ds(i * features, features)].reshape(1, features)
            row += 1
    rank_slots(count_ref, length_ref, perm_s, slen_s, slots)
    for load in loads[1:3]:
        load.start()
    loads[0].wait()
    loads[3].start()
    met()

    def word(i):
        return pltpu.make_async_remote_copy(
            src_ref=mine,
            dst_ref=theirs.at[i],
            send_sem=say_sem.at[i],
            recv_sem=hear_sem.at[i],
            device_id=peers[i - 1],
            device_id_type=MESH,
        )

    if agrees:
        long = 0
        for i in range(slots):
            long = long + jnp.where((i < count_ref[0]) & (length_ref[i] > 2 * rows), 1, 0)
        mine[...] = jnp.full(mine.shape, long, jnp.int32).astype(F32)
        theirs[0] = mine[...]
        for i in range(1, sizes[0]):
            word(i).start()

    def prepare(i, _):
        slot = jnp.where(i < slots - far_slots, far_slots + i, slots - 1 - i)
        value = jnp.where(live_rows(slen_s, slot, first, rows), x_v[:, perm_s[slot], :], 0.0)
        buf[slot, pl.ds(aligned(first, rows), rows), :] = value.astype(BF16)
        pl.when(slot < far_slots)(lambda: exchange.start_own(slot, True))
        if far_slots < slots:
            pl.when(slot >= far_slots)(lambda: exchange.start_own(slot, False))
        return 0

    lax.fori_loop(0, slots, prepare, 0)
    part_o[...] = jnp.zeros_like(part_o)
    for load in loads[1:3]:
        load.wait()

    batch = group * rows
    folds = 2 if wide % (2 * features) == 0 else 1
    span = folds * features
    count = slots // group
    near_groups = (slots - far_slots) // group

    def outs(base):
        place = pl.ds(base, batch)
        early = [
            pltpu.make_async_copy(nrm_v.at[place], nrm_o.at[place], out_sem.at[0]),
            pltpu.make_async_copy(sum_v.at[place], sum_o.at[place], out_sem.at[1]),
        ]
        for n in range(wide // WIDE):
            cut = pl.ds(n * WIDE, WIDE)
            early.append(pltpu.make_async_copy(act_v.at[place, cut], act_o.at[n, place], out_sem.at[4]))
            early.append(pltpu.make_async_copy(dg_v.at[place, cut], dg_o.at[n, place], out_sem.at[5]))
        late = [
            pltpu.make_async_copy(gs_v.at[place], gs_o.at[place], out_sem.at[2]),
            pltpu.make_async_copy(lo_v.at[place], lo_o.at[place], out_sem.at[3]),
            pltpu.make_async_copy(gb_v.at[place], gb_o.at[place], out_sem.at[6]),
        ]
        return early, late

    def bring(slot0):
        for k in reversed(range(group)):
            exchange.forward(slot0 + k)

    def mixing(slot0, far):
        for k in reversed(range(group)):
            exchange.wait_near(slot0 + k, far)
            mix_slot(slot0 + k, far, exchange, sc_v, buf, uv, k * rows)

    def work(i, _):
        slot0 = group_at(i, near_groups, count) * group
        base = aligned(slot0 * rows, batch)
        place = pl.ds(base, batch)
        if near_groups < count:
            pl.when(i >= near_groups)(lambda: mixing(slot0, True))
        if near_groups > 0:
            pl.when(i < near_groups)(lambda: mixing(slot0, False))
        br_v[...] = jnp.dot(uv[...], hc_v[...], preferred_element_type=F32)

        for k in range(group):
            here = pl.ds(aligned(base + k * rows, rows), rows)
            mixed = (br_v[k * rows : (k + 1) * rows, :] * scale).astype(BF16).astype(F32)
            live = live_rows(slen_s, slot0 + k, first, rows)
            total = jnp.where(live, x_v[:, perm_s[slot0 + k], :], 0.0) + mixed
            sum_v[here, :] = total
            hat, _ = normalize(total)
            nrm_v[here, :] = (hat * gain_one() + shift_one()).astype(BF16)

        @pl.when(i == 0)
        def _():
            loads[3].wait()
            for load in loads[4:]:
                load.start()

        def expand(n, _):
            cut = pl.ds(aligned(n * span, span), span)
            bias = [vec_ref[pl.ds(5 + folds * n + i, 1), :] for i in range(folds)]
            hidden = jnp.dot(nrm_v[place, :], wi_v[:, cut], preferred_element_type=F32) + jnp.concatenate(bias, axis=1)
            gate = 0.5 + 0.5 * lax.erf(hidden * math.sqrt(0.5))
            slope = gate + hidden * (jnp.exp(hidden * hidden * -0.5) * (1.0 / math.sqrt(2.0 * math.pi)))
            act_v[place, cut] = (hidden * gate).astype(BF16)
            dg_v[place, cut] = slope.astype(BF16)
            return 0

        lax.fori_loop(0, wide // span, expand, 0)
        for copy in outs(base)[0]:
            copy.start()
        if near_groups < count:

            @pl.when((i + 1 >= near_groups) & (i + 1 < count))
            def _():
                bring(group_at(i + 1, near_groups, count) * group)

        pl.when(i == 0)(loads[4].wait)
        br_v[...] = jnp.dot(act_v[place, :], wo_v[...], preferred_element_type=F32)

        def norm_two(k, _):
            here = pl.ds(aligned(base + k * rows, rows), rows)
            local = pl.ds(aligned(k * rows, rows), rows)
            slot = slot0 + k
            live = live_rows(slen_s, slot, first, rows)
            hat, inverse = normalize(sum_v[here, :] + (br_v[local, :] + bias_out()))
            grad = jnp.where(live, cot_v[:, perm_s[slot], :], 0.0)
            lo_v[here, :] = jnp.where(live, hat * gain_two() + shift_two(), 0.0).astype(BF16)
            part_o[0:8, :] = part_o[0:8, :] + fold8(grad * hat)
            part_o[8:16, :] = part_o[8:16, :] + fold8(grad)
            second = norm_back(grad * gain_two(), hat, inverse)
            low = second.astype(BF16)
            gs_v[here, :] = second
            gb_v[here, :] = low
            part_o[16:24, :] = part_o[16:24, :] + fold8(low.astype(F32))
            return 0

        pl.when(i == 0)(loads[5].wait)
        lax.fori_loop(0, group, norm_two, 0)
        for copy in outs(base)[1]:
            copy.start()
        return 0

    if near_groups == 0:
        bring((count - 1) * group)
    lax.fori_loop(0, count, work, 0)

    def finish(slot, _):
        pl.when(slot < far_slots)(lambda: exchange.wait_sends(slot, True))
        if far_slots < slots:
            pl.when(slot >= far_slots)(lambda: exchange.wait_sends(slot, False))
        return 0

    lax.fori_loop(0, slots, finish, 0)

    if agrees:
        for i in range(1, sizes[0]):
            word(i).wait()
        choice_o[0] = jnp.where(jnp.max(theirs[...]) > far_slots, 1, 0)

    def flush(g, _):
        for copies in outs(aligned(g * batch, batch)):
            for copy in copies:
                copy.wait()
        return 0

    lax.fori_loop(0, count, flush, 0)


def backward_kernel(cfg, *refs):
    sizes, far_slots, slots, group, parts, mids, lags, plan = cfg
    cube = Cube(sizes, mids)
    S = cube.stages
    (
        count_ref, length_ref, gain_ref, part_ref,
        act_hbm, dg_hbm, nrm_hbm, sum_hbm, gs_hbm, gb_hbm, wi_hbm, wo_hbm, sc_hbm, hc_hbm,
        full_o, ig_o, small_o,
        perm_s, slen_s, gs_v, sum_v, nrm_v, gb_v, gh_v, gn_v, act_v, dg_v, wi_v, wo_v, sc_v, hc_v, buf, uv, mix_v, ig_v,
        bin_v, one_v, small_v, gain_v, part_v, full,
    ) = refs[:41]
    landed = refs[41 : 41 + S]
    (
        small_recv, load_sem, sum_sem, stream_sem, out_sem, ig_sem, send_sem, recv_sem,
        rs_s, rs_r, ag_s, ag_r, sm_s, sm_r,
    ) = refs[41 + S :]
    ticks, tick_rows, _ = part_v.shape
    message = tick_rows // parts
    chunks = act_hbm.shape[0]
    per_tick = chunks // ticks
    features = nrm_v.shape[1]
    rows = gs_v.shape[0] // slots
    batch = group * rows
    scale = 1.0 / math.sqrt(features * rows * sizes[1])
    exchange = Exchange(sizes[1], rows, buf, send_sem, recv_sem)
    q = exchange.q
    first = q * rows
    loads = [
        pltpu.make_async_copy(gb_hbm, gb_v, load_sem.at[0]),
        pltpu.make_async_copy(nrm_hbm, nrm_v, load_sem.at[1]),
        pltpu.make_async_copy(gs_hbm, gs_v, load_sem.at[2]),
        pltpu.make_async_copy(sc_hbm.at[q], sc_v, load_sem.at[3]),
        pltpu.make_async_copy(hc_hbm, hc_v, load_sem.at[4]),
    ]

    def turn(i):
        return jnp.where(i < far_slots, far_slots - 1 - i, i) if far_slots < slots else slots - 1 - i

    def sum_copy(i):
        place = pl.ds(aligned(turn(i) * rows, rows), rows)
        return pltpu.make_async_copy(sum_hbm.at[place], sum_v.at[lax.rem(i, 2)], sum_sem.at[lax.rem(i, 2)])

    def streams(n, slot):
        cut = pl.ds(aligned(n * WIDE, WIDE), WIDE)
        return [
            pltpu.make_async_copy(act_hbm.at[n], act_v.at[slot], stream_sem.at[0, slot]),
            pltpu.make_async_copy(wo_hbm.at[cut], wo_v.at[slot], stream_sem.at[1, slot]),
            pltpu.make_async_copy(dg_hbm.at[n], dg_v.at[slot], stream_sem.at[2, slot]),
            pltpu.make_async_copy(wi_hbm.at[:, cut], wi_v.at[slot], stream_sem.at[3, slot]),
        ]

    loads[0].start()
    streams(0, 0)[0].start()
    met = greet([cube.partner(bit) for bit in cube.bits])
    rank_slots(count_ref, length_ref, perm_s, slen_s, slots)

    side = cube.values[cube.bits[0]]
    starts, hops = [], []
    for j in range(parts):
        twin = len(cube.orders) // 2 + j
        here, there = cube.orders[j], cube.orders[twin]
        blend = lambda a, b: a + side * (b - a)
        offsets = [blend(cube.offset(j, n, message), cube.offset(twin, n, message)) for n in range(S + 1)]
        starts.append([j * message + off for off in offsets])
        hops.append(
            [
                (
                    blend(cube.values[a], cube.values[b]),
                    tuple(blend(x, y) for x, y in zip(cube.partners[a], cube.partners[b])),
                )
                for a, b in zip(here, there)
            ]
        )

    def rs(m, t, j, s):
        value, partner = hops[j][s]
        half = message >> (s + 1)
        off = starts[j][s] + (1 - value) * half
        return pltpu.make_async_remote_copy(
            src_ref=part_v.at[t, pl.ds(aligned(off, 16), half)],
            dst_ref=landed[s].at[m],
            send_sem=rs_s.at[s],
            recv_sem=rs_r.at[s, m],
            device_id=partner,
            device_id_type=MESH,
        )

    def ag(m, t, j, s):
        _, partner = hops[j][s]
        half = message >> (s + 1)
        ref = full.at[t, pl.ds(aligned(starts[j][s + 1], 16), half)]
        return pltpu.make_async_remote_copy(
            src_ref=ref,
            dst_ref=ref,
            send_sem=ag_s.at[s],
            recv_sem=ag_r.at[s, m],
            device_id=partner,
            device_id_type=MESH,
        )

    def add(m, t, j, s):
        half = message >> (s + 1)
        place = pl.ds(aligned(starts[j][s + 1], 16), half)
        total = part_v[t, place, :].astype(F32) + landed[s][m].astype(F32)
        target = full if s == S - 1 else part_v
        target[t, place, :] = total.astype(BF16)

    def out(t, j):
        place = pl.ds(j * message, message)
        return pltpu.make_async_copy(full.at[t, place], full_o.at[t, place], out_sem.at[t, j])

    def event(k, m, t, j):
        if k == 0:
            rs(m, t, j, 0).start()
        elif k <= S:
            rs(m, t, j, k - 1).wait_recv()
            add(m, t, j, k - 1)
            (rs(m, t, j, k) if k < S else ag(m, t, j, S - 1)).start()
        elif k < 2 * S:
            s = 2 * S - k
            ag(m, t, j, s).wait_recv()
            ag(m, t, j, s - 1).start()
        else:
            ag(m, t, j, 0).wait_recv()
            out(t, j).start()

    def sends_done():
        for s in range(S):
            for sem in (rs_s.at[s], ag_s.at[s]):
                pltpu.make_async_copy(landed[s], landed[s], sem).wait()

    when = [0 if per_tick == 1 and parts == 4 else parts]
    for lag in lags:
        when.append(when[-1] + lag)

    def events(tick, j):
        for k in reversed(range(2 * S + 1)):
            t = tick + (j - when[k]) // parts
            jj = (j - when[k]) % parts
            pl.when((t >= 0) & (t < ticks))(functools.partial(event, k, t * parts + jj, t, jj))

    bin_v[...] = jnp.zeros_like(bin_v)
    one_v[...] = jnp.zeros_like(one_v)
    gain_v[...] = gain_ref[...].reshape(1, features)
    gn_v[...] = jnp.zeros_like(gn_v)
    small_v[...] = jnp.zeros_like(small_v)
    loads[0].wait()
    for copy in streams(0, 0)[1:]:
        copy.start()
    loads[1].start()
    met()

    def load_rest():
        for load in loads[2:]:
            load.start()
        for i in range(2):
            sum_copy(i).start()


    def contract(left, right, dims):
        return lax.dot_general(left, right, ((dims, dims), ((), ())), preferred_element_type=F32)

    def weigh_out(n, slot, t, base):
        streams(n, slot)[0].wait()
        grad = contract(act_v[slot], gb_v[...], (0,)).astype(BF16)
        for i in range(features // LANES):
            part_v[t, pl.ds(base + i * WIDE, WIDE), :] = grad[:, i * LANES : (i + 1) * LANES]

    def pull(n, slot, t, base):
        streams(n, slot)[1].wait()
        streams(n, slot)[2].wait()
        pulled = contract(gb_v[...], wo_v[slot], (1,)) * dg_v[slot].astype(F32)
        pulled = pulled.astype(BF16)
        gh_v[...] = pulled
        bin_v[n] = fold8(pulled.astype(F32))

    def weigh_in(n, slot, t, base):
        pl.when(n == 0)(loads[1].wait)
        grad = contract(nrm_v[...], gh_v[...], (0,)).astype(BF16)
        for i in range(WIDE // LANES):
            place = pl.ds(base + features // LANES * WIDE + i * features, features)
            part_v[t, place, :] = grad[:, i * LANES : (i + 1) * LANES]

    def spread(n, slot, t, base):
        streams(n, slot)[3].wait()
        for i in range(2):
            here = pl.ds(i * (slots // 2) * rows, slots // 2 * rows)
            gn_v[here, :] = gn_v[here, :] + contract(gh_v[here, :], wi_v[slot], (1,))

    steps = [weigh_out, pull, weigh_in, spread]

    def compute(tick, j):
        if per_tick == 1 and parts == 4:
            slot = lax.rem(tick, 2)
            if j == 0:
                for copy in streams(tick + 1, 1 - slot):
                    pl.when(tick + 1 < chunks)(copy.start)
            steps[j](tick, slot, tick, 0)
        elif j == 0:

            def whole(u, _):
                n = tick * per_tick + u
                slot = lax.rem(n, 2)
                for copy in streams(n + 1, 1 - slot):
                    pl.when(n + 1 < chunks)(copy.start)
                for step in steps:
                    step(n, slot, tick, aligned(u * (tick_rows // per_tick), LANES))
                return 0

            lax.fori_loop(0, per_tick, whole, 0)

    def back(i, _):
        slot = turn(i)
        here = pl.ds(aligned(slot * rows, rows), rows)
        pl.when(i == 0)(loads[2].wait)
        sum_copy(i).wait()
        hat, inverse = normalize(sum_v[lax.rem(i, 2)])
        grad = gn_v[here, :]
        one_v[0:8, :] = one_v[0:8, :] + fold8(grad * hat)
        one_v[8:16, :] = one_v[8:16, :] + fold8(grad)
        grad = gs_v[here, :] + norm_back(grad * gain_v[...], hat, inverse)
        gs_v[here, :] = grad
        buf[slot, pl.ds(aligned(first, rows), rows), :] = grad.astype(BF16)
        pl.when(i < far_slots)(lambda: exchange.start_own(slot, True))
        if far_slots < slots:
            pl.when(i >= far_slots)(lambda: exchange.start_own(slot, False))
        pl.when(i + 2 < slots)(lambda: sum_copy(i + 2).start())
        return 0

    def small_copy(s):
        return pltpu.make_async_remote_copy(
            src_ref=small_v.at[s],
            dst_ref=small_recv.at[s],
            send_sem=sm_s.at[s],
            recv_sem=sm_r.at[s],
            device_id=cube.partners[cube.bits[s]],
            device_id_type=MESH,
        )

    def small_start():
        row = 0
        vectors = [one_v[0:8, :], one_v[8:16, :]] + [bin_v[n] for n in range(chunks)]
        vectors += [part_ref[16:24, :], part_ref[0:8, :], part_ref[8:16, :]]
        for vector in vectors:
            vector = jnp.sum(vector, axis=0, keepdims=True)
            for i in range(vector.shape[1] // LANES):
                small_v[0, row : row + 1, :] = vector[:, i * LANES : (i + 1) * LANES]
                row += 1
        small_copy(0).start()

    def small_step(s):
        small_copy(s).wait()
        if s + 1 < S:
            small_v[s + 1] = small_v[s] + small_recv[s]
            small_copy(s + 1).start()
        else:
            small_o[...] = small_v[s] + small_recv[s]

    count = slots // group
    near_groups = (slots - far_slots) // group

    def grad_copy(i):
        base = aligned(group_at(i, near_groups, count) * batch, batch)
        return pltpu.make_async_copy(ig_v.at[lax.rem(i, 2)], ig_o.at[pl.ds(base, batch)], ig_sem.at[lax.rem(i, 2)])

    def mixing(i, k, far):
        slot = group_at(i, near_groups, count) * group + k
        exchange.wait_near(slot, far)
        mix_slot(slot, far, exchange, sc_v, buf, uv, k * rows)

    def hidden_mix(i):
        pl.when(i >= 2)(lambda: grad_copy(i - 2).wait())
        mix_v[...] = jnp.dot(uv[...], hc_v[...], preferred_element_type=F32)

    def finish(i):
        for k in range(group):
            slot = group_at(i, near_groups, count) * group + k
            here = pl.ds(aligned(slot * rows, rows), rows)
            local = pl.ds(k * rows, rows)
            grad = gs_v[here, :] + mix_v[local, :] * scale
            grad = jnp.where(live_rows(slen_s, slot, first, rows), grad, 0.0)
            ig_v[lax.rem(i, 2), local, :] = grad.astype(BF16)
        grad_copy(i).start()

    def bring(i):
        for k in reversed(range(group)):
            exchange.forward(group_at(i, near_groups, count) * group + k)

    small_at, near_at, far_at, lead = plan

    def drain(tick, j):
        d = tick - ticks

        @pl.when(d == 0)
        def _():
            share = -(-slots // parts)
            lax.fori_loop(min(j * share, slots), min((j + 1) * share, slots), back, 0)

        here = lambda at: pl.when(d * parts + j == at)
        if j == small_at % parts:
            here(small_at)(small_start)
        for s in range(S):
            at = small_at + 5 * (s + 1)
            if j == at % parts:
                here(at)(functools.partial(small_step, s))
        if j == 0:

            @pl.when(d == 1)
            def _():
                for load in loads[3:]:
                    load.wait()

        for far, start, low, high in ((False, near_at, 0, near_groups), (True, far_at, near_groups, count)):
            if low == high:
                continue
            i = d - start + low

            @pl.when((i >= low) & (i < high))
            def _():
                subs = [
                    lambda: mixing(i, 0, far),
                    lambda: [mixing(i, k, far) for k in range(1, group)],
                    lambda: hidden_mix(i),
                    lambda: finish(i),
                ]
                for at, sub in enumerate(subs):
                    if min(at, parts - 1) == j:
                        sub()

            if far and j == parts - 1:
                ahead = i + lead
                pl.when((ahead >= low) & (ahead < high))(lambda: bring(ahead))

    last = ticks + max(
        -(-(when[-1] + 1) // parts),
        (small_at + 5 * S) // parts + 1,
        near_at + near_groups,
        far_at + count - near_groups,
    )

    def body(tick, _):
        pl.when(tick == 1)(load_rest)
        for j in range(parts):
            pl.when(tick < ticks)(lambda: compute(tick, j))
            events(tick, j)
            pl.when(tick >= ticks)(lambda: drain(tick, j))
        return 0

    lax.fori_loop(0, last, body, 0)

    def settle(slot, _):
        pl.when(slot < far_slots)(lambda: exchange.wait_sends(slot, True))
        if far_slots < slots:
            pl.when(slot >= far_slots)(lambda: exchange.wait_sends(slot, False))
        return 0

    lax.fori_loop(0, slots, settle, 0)
    for i in range(max(0, count - 2), count):
        grad_copy(i).wait()

    def finish_out(t, _):
        for j in range(parts):
            out(t, j).wait()
        return 0

    lax.fori_loop(0, ticks, finish_out, 0)
    sends_done()


def output_kernel(slots, cuts, places, count_ref, length_ref, full_ref, lo_ref, ig_ref, small_ref, *refs):
    wi_ref, wo_ref, lo_out, ig_out = refs[:4]
    vector_refs, (perm_s, slen_s) = refs[4:-2], refs[-2:]
    step = pl.program_id(0)
    features = wi_ref.shape[0]
    for u in range(full_ref.shape[0]):
        base = u * WIDE
        for i in range(features // LANES):
            wo_ref[base : base + WIDE, i * LANES : (i + 1) * LANES] = full_ref[u, pl.ds(i * WIDE, WIDE), :].astype(F32)
        for i in range(WIDE // LANES):
            start = features // LANES * WIDE + i * features
            wi_ref[:, base + i * LANES : base + (i + 1) * LANES] = full_ref[u, pl.ds(start, features), :].astype(F32)

    @pl.when(step == 0)
    def _():
        rank_slots(count_ref, length_ref, perm_s, slen_s, slots)
        for ref, start in zip(vector_refs, cuts):
            ref[...] = small_ref[start : start + ref.shape[0], :]

    @pl.when(step < places)
    def _():
        for j in range(slots):
            lo_out[:, perm_s[j], :] = lo_ref[j].astype(F32)
            ig_out[:, perm_s[j], :] = ig_ref[j].astype(F32)


ANY = pl.BlockSpec(memory_space=pl.ANY)
SMEM = pl.BlockSpec(memory_space=pltpu.SMEM)
VMEM = pl.BlockSpec(memory_space=pltpu.VMEM)
DMA = pltpu.SemaphoreType.DMA
LAGS = [3, 5, 4, 3, 3, 3, 3, 4, 6, 3]
PLAN = (4, 1, 4, 1)
FAR_PLAN = (4, 1, 4, 1)
XYZ, YXZ, ZXY, YZX, ZYX = (0, 1, 2), (1, 0, 2), (2, 0, 1), (1, 2, 0), (2, 1, 0)
MIDS = (XYZ, YXZ, ZXY, YZX, YXZ, ZXY, YZX, XYZ)
FAR_MIDS = (YZX, ZYX, YXZ, ZXY, ZXY, YZX, XYZ, YXZ)


def run_forward(sizes, far_slots, slots, *operands, agrees=False, group=2, name="forward", cid=1):
    rows, _, features = operands[8].shape
    wide = operands[10].shape[1]
    seq_total = rows * sizes[1]
    flat, batch, chunks = rows * slots, group * rows, wide // WIDE
    shape = jax.ShapeDtypeStruct
    return pl.pallas_call(
        functools.partial(forward_kernel, (sizes, far_slots, slots, group, len(operands) + 8 if agrees else 0)),
        name=name,
        out_shape=(
            shape((chunks, flat, WIDE), BF16),
            shape((chunks, flat, WIDE), BF16),
            shape((flat, features), BF16),
            shape((flat, features), F32),
            shape((flat, features), F32),
            shape((flat, features), BF16),
            shape((flat, features), BF16),
            shape((24, features), F32),
        )
        + ((shape((1,), jnp.int32),) if agrees else ()),
        in_specs=[SMEM] * 2 + [VMEM] * 6 + [ANY] * 6,
        out_specs=[ANY] * 7 + [VMEM] + [SMEM] * agrees,
        scratch_shapes=[
            pltpu.SMEM((slots,), jnp.int32),
            pltpu.SMEM((slots,), jnp.int32),
            pltpu.VMEM((rows, slots, features), F32),
            pltpu.VMEM((rows, slots, features), F32),
            pltpu.VMEM((features, wide), BF16),
            pltpu.VMEM((wide, features), BF16),
            pltpu.VMEM((2 * rows, seq_total), BF16),
            pltpu.VMEM((2 * features, features), BF16),
            pltpu.VMEM((slots, seq_total, features), BF16),
            pltpu.VMEM((batch, 2 * features), BF16),
            pltpu.VMEM((flat, features), F32),
            pltpu.VMEM((flat, features), BF16),
            pltpu.VMEM((flat, wide), BF16),
            pltpu.VMEM((flat, wide), BF16),
            pltpu.VMEM((flat, features), F32),
            pltpu.VMEM((flat, features), BF16),
            pltpu.VMEM((flat, features), BF16),
            pltpu.VMEM((batch, features), F32),
            pltpu.VMEM((5 + wide // features, features), F32),
            DMA((6,)),
            DMA((7,)),
            DMA((slots, sizes[1])),
            DMA((slots, sizes[1])),
        ]
        + agrees * [pltpu.VMEM((8, LANES), F32), pltpu.VMEM((sizes[0], 8, LANES), F32), DMA((sizes[0],)), DMA((sizes[0],))],
        compiler_params=pltpu.CompilerParams(collective_id=cid, has_side_effects=True, vmem_limit_bytes=62 << 20),
    )(*operands)


def run_backward(sizes, far_slots, slots, ticks, tick_rows, parts, *operands, group=2, mids=None, lags=None, plan=None, name="backward", cid=2):
    devices = sizes[0] * sizes[1]
    chunks, flat, _ = operands[4].shape
    features, wide = operands[10].shape
    rows = flat // slots
    seq_total = rows * sizes[1]
    batch = group * rows
    message = tick_rows // parts
    shape = jax.ShapeDtypeStruct
    mostly_far = far_slots > slots * 5 // 8
    mids = mids or (FAR_MIDS if mostly_far else MIDS)
    plan = plan or (FAR_PLAN if mostly_far else PLAN)
    lags = lags or LAGS
    stages = devices.bit_length() - 1
    lags = (lags[:stages] + [2] * stages)[:stages] + ([2] * stages + lags[-stages:])[-stages:]
    return pl.pallas_call(
        functools.partial(backward_kernel, (sizes, far_slots, slots, group, parts, mids, lags, plan)),
        name=name,
        out_shape=(
            shape((ticks, tick_rows, LANES), BF16),
            shape((flat, features), BF16),
            shape((64, LANES), F32),
        ),
        in_specs=[SMEM] * 2 + [VMEM] * 2 + [ANY] * 10,
        out_specs=[ANY] * 2 + [VMEM],
        scratch_shapes=[
            pltpu.SMEM((slots,), jnp.int32),
            pltpu.SMEM((slots,), jnp.int32),
            pltpu.VMEM((flat, features), F32),
            pltpu.VMEM((2, rows, features), F32),
            pltpu.VMEM((flat, features), BF16),
            pltpu.VMEM((flat, features), BF16),
            pltpu.VMEM((flat, WIDE), BF16),
            pltpu.VMEM((flat, features), F32),
            pltpu.VMEM((2, flat, WIDE), BF16),
            pltpu.VMEM((2, flat, WIDE), BF16),
            pltpu.VMEM((2, features, WIDE), BF16),
            pltpu.VMEM((2, WIDE, features), BF16),
            pltpu.VMEM((2 * rows, seq_total), BF16),
            pltpu.VMEM((2 * features, features), BF16),
            pltpu.VMEM((slots, seq_total, features), BF16),
            pltpu.VMEM((batch, 2 * features), BF16),
            pltpu.VMEM((batch, features), F32),
            pltpu.VMEM((2, batch, features), BF16),
            pltpu.VMEM((chunks, 8, WIDE), F32),
            pltpu.VMEM((16, features), F32),
            pltpu.VMEM((stages, 64, LANES), F32),
            pltpu.VMEM((1, features), F32),
            pltpu.VMEM((ticks, tick_rows, LANES), BF16),
            pltpu.VMEM((ticks, tick_rows, LANES), BF16),
        ]
        + [pltpu.VMEM((ticks * parts, message >> (s + 1), LANES), BF16) for s in range(stages)]
        + [
            pltpu.VMEM((stages, 64, LANES), F32),
            DMA((5,)),
            DMA((2,)),
            DMA((4, 2)),
            DMA((ticks, parts)),
            DMA((2,)),
            DMA((slots, sizes[1])),
            DMA((slots, sizes[1])),
            DMA((stages,)),
            DMA((stages, ticks * parts)),
            DMA((stages,)),
            DMA((stages, ticks * parts)),
            DMA((stages,)),
            DMA((stages,)),
        ],
        compiler_params=pltpu.CompilerParams(collective_id=cid, has_side_effects=True, vmem_limit_bytes=62 << 20),
    )(*operands)


def cut_messages(devices, chunks, chunk_rows):
    per_tick, parts = min(
        (count, -cut)
        for count in range(1, chunks + 1)
        for cut in range(1, 5)
        if chunks % count == 0 and chunk_rows * count % (devices * 16 * cut) == 0
    )
    return per_tick, -parts


def rest_of_layer(far_slots, sizes, cid, known, inputs, item_counts, lengths, vectors, weight_in, weight_out, cotangent, seq_table, hid_table):
    rows, slots, features = inputs.shape
    wide = weight_in.shape[1]
    chunks = wide // WIDE
    chunk_rows = 2 * features * WIDE // LANES
    shape = jax.ShapeDtypeStruct
    per_tick, parts = cut_messages(sizes[0] * sizes[1], chunks, chunk_rows)
    act, dg, nrm, summed, second, low, lo, part = known or run_forward(
        sizes, far_slots, slots,
        item_counts, lengths, *vectors, inputs, cotangent, weight_in, weight_out, seq_table, hid_table,
        cid=cid,
    )
    full, grad, small = run_backward(
        sizes, far_slots, slots, chunks // per_tick, chunk_rows * per_tick, parts,
        item_counts, lengths, vectors[0], part, act, dg, nrm, summed, second, low, weight_in, weight_out, seq_table, hid_table,
        cid=cid + 1,
    )
    side = 2 if chunks % 2 == 0 else 1
    places = 1 << min((chunks // side).bit_length() - 1, 3)
    step = rows // places
    lo, grad = lo.reshape(slots, rows, features), grad.reshape(slots, rows, features)
    heights = [size // LANES for size in (features, features, wide, features, features, features)]
    cuts = [sum(heights[:i]) for i in range(len(heights))]
    slot_first = pl.BlockSpec((slots, step, features), lambda n: (0, jnp.minimum(n, places - 1), 0))
    place_first = pl.BlockSpec((step, slots, features), lambda n: (jnp.minimum(n, places - 1), 0, 0))
    wi_grad, wo_grad, layer_out, input_grad, *vectors = pl.pallas_call(
        functools.partial(output_kernel, slots, cuts, places),
        name="output",
        grid=(chunks // side,),
        out_shape=(
            shape((features, wide), F32),
            shape((wide, features), F32),
            shape(inputs.shape, F32),
            shape(inputs.shape, F32),
            *(shape((height, LANES), F32) for height in heights),
        ),
        in_specs=[SMEM] * 2 + [pl.BlockSpec((side, chunk_rows, LANES), lambda n: (n, 0, 0))] + [slot_first] * 2 + [VMEM],
        out_specs=(
            pl.BlockSpec((features, side * WIDE), lambda n: (0, n)),
            pl.BlockSpec((side * WIDE, features), lambda n: (n, 0)),
            place_first,
            place_first,
            *([VMEM] * len(heights)),
        ),
        scratch_shapes=[pltpu.SMEM((slots,), jnp.int32), pltpu.SMEM((slots,), jnp.int32)],
        compiler_params=pltpu.CompilerParams(vmem_limit_bytes=60 << 20),
    )(item_counts, lengths, full.reshape(chunks, chunk_rows, LANES), lo, grad, small)
    gain_one_grad, shift_one_grad, bias_in_grad, bias_out_grad, gain_two_grad, shift_two_grad = [v.reshape(-1) for v in vectors]
    return (
        layer_out, input_grad, gain_one_grad, shift_one_grad, wi_grad, bias_in_grad, wo_grad, bias_out_grad, gain_two_grad, shift_two_grad,
    )


def per_device(
    inputs, item_counts, lengths, gain_one, shift_one, weight_in, bias_in, weight_out, bias_out, gain_two, shift_two, cotangent
):
    rows, slots, features = inputs.shape
    wide = weight_in.shape[1]
    sizes = (lax.axis_size("dp"), lax.axis_size("seq"))
    seq_total = rows * sizes[1]
    chunks = wide // WIDE
    chunk_rows = 2 * features * WIDE // LANES
    shape = jax.ShapeDtypeStruct

    seq_cos, seq_sin = dft_tables(seq_total)
    hid_cos, hid_sin = dft_tables(features)
    seq_table = [table.reshape(sizes[1], rows, seq_total) for table in (seq_cos, seq_sin)]
    seq_table = jnp.asarray(np.concatenate(seq_table, axis=1).astype(jnp.bfloat16))
    hid_table = jnp.asarray(np.concatenate([hid_cos, -hid_sin], axis=0).astype(jnp.bfloat16))
    vectors = (gain_one, shift_one, bias_out, gain_two, shift_two, bias_in)
    operands = (inputs, item_counts, lengths, vectors, weight_in, weight_out, cotangent, seq_table, hid_table)

    few = slots // 2
    *known, choice = run_forward(
        sizes, few, slots,
        item_counts, lengths, *vectors, inputs, cotangent, weight_in, weight_out, seq_table, hid_table,
        agrees=True, cid=1,
    )
    return lax.cond(
        choice[0] == 0,
        lambda known, *given: rest_of_layer(few, sizes, 2, known, *given),
        lambda known, *given: rest_of_layer(slots, sizes, 4, None, *given),
        tuple(known), *operands,
    )


def solution(mesh):
    placed = (
        P("seq", "dp", None), P("dp"), P("dp"), P(), P(), P(), P(), P(), P(), P(), P(), P("seq", "dp", None),
    )
    wide = P("seq", "dp", None)
    return jax.shard_map(
        per_device,
        mesh=mesh,
        in_specs=placed,
        out_specs=(wide, wide, P(), P(), P(), P(), P(), P(), P(), P()),
        check_vma=False,
    )
```

```python
import functools
import math

import jax
import jax.numpy as jnp
import numpy as np
from jax import lax
from jax.experimental import pallas as pl
from jax.experimental.pallas import tpu as pltpu
from jax.sharding import PartitionSpec as P

EPSILON = 1e-05
MESH = pl.DeviceIdType.MESH
LANES = 128
WIDE = 512
BF16 = jnp.bfloat16
F32 = jnp.float32


def dft_tables(count):
    index = np.arange(count, dtype=np.int64)
    turns = (index[:, None] * index[None, :] % count).astype(np.float32)
    angle = (turns * np.float32(2.0 * math.pi / count)).astype(np.float64)
    return np.cos(angle).astype(np.float32), np.sin(angle).astype(np.float32)


def aligned(value, step):
    return pl.multiple_of(value, step)


def bit_of(value, k):
    return (value // k) % 2


def flipped(value, k):
    return value + k * (1 - 2 * bit_of(value, k))


def axis_bits(axis, size):
    return [(axis, 1 << b) for b in range(size.bit_length() - 1)]


class Cube:
    def __init__(self, sizes, mids):
        dp, seq = sizes
        bits = axis_bits(1, seq) + axis_bits(0, dp)
        first, near, rest = bits[:1], bits[1:4], bits[4:]
        self.orders = [first + [near[i] for i in mid] + rest for mid in mids]
        self.bits = bits
        self.stages = len(bits)
        self.me = (lax.axis_index("dp"), lax.axis_index("seq"))
        self.values = {bit: self.value(bit) for bit in bits}
        self.partners = {bit: self.partner(bit) for bit in bits}

    def value(self, bit):
        return bit_of(self.me[bit[0]], bit[1])

    def partner(self, bit):
        axis, k = bit
        other = flipped(self.me[axis], k)
        return (other, self.me[1]) if axis == 0 else (self.me[0], other)

    def offset(self, order, level, rows):
        total = 0
        for s in range(level):
            total = total + self.values[self.orders[order][s]] * (rows >> (s + 1))
        return total


class Exchange:
    def __init__(self, size, rows, buf, send, recv):
        self.size, self.rows, self.buf, self.send_sem, self.recv_sem = size, rows, buf, send, recv
        self.dp, self.q = lax.axis_index("dp"), lax.axis_index("seq")
        self.order = [1 << b for b in reversed(range(size.bit_length() - 1))]

    def owner(self, pattern):
        index = self.q
        for k in self.order:
            if pattern & k:
                index = flipped(index, k)
        return index

    def copy(self, slot, pattern):
        hop = pattern & -pattern
        place = pl.ds(aligned(self.owner(pattern - hop) * self.rows, self.rows), self.rows)
        ref = self.buf.at[slot, place]
        return pltpu.make_async_remote_copy(
            src_ref=ref,
            dst_ref=ref,
            send_sem=self.send_sem.at[slot, pattern],
            recv_sem=self.recv_sem.at[slot, pattern],
            device_id=(self.dp, flipped(self.q, hop)),
            device_id_type=MESH,
        )

    def patterns(self, far):
        return range(1, self.size) if far else range(1, 2)

    def start_own(self, slot, far):
        for pattern in self.patterns(far):
            if pattern & (pattern - 1) == 0:
                self.copy(slot, pattern).start()

    def forward(self, slot):
        for pattern in self.patterns(True):
            if pattern & 1 == 0:
                self.copy(slot, pattern).wait_recv()
                for k in self.order:
                    if k < (pattern & -pattern):
                        self.copy(slot, pattern | k).start()

    def wait_near(self, slot, far):
        for pattern in self.patterns(far):
            if pattern & 1:
                self.copy(slot, pattern).wait_recv()

    def wait_sends(self, slot, far):
        for pattern in self.patterns(far):
            self.copy(slot, pattern).wait_send()


def greet(partners):
    barrier = pltpu.get_barrier_semaphore()
    for partner in partners:
        pl.semaphore_signal(barrier, inc=1, device_id=partner, device_id_type=MESH)
    return lambda: pl.semaphore_wait(barrier, len(partners))


def rank_slots(count_ref, length_ref, perm_s, slen_s, slots):
    count = count_ref[0]
    live = [jnp.where(i < count, length_ref[i], 0) for i in range(slots)]
    ranks = []
    for i in range(slots):
        rank = 0
        for k in range(slots):
            if k != i:
                ahead = live[k] >= live[i] if k < i else live[k] > live[i]
                rank = rank + jnp.where(ahead, 1, 0)
        ranks.append(rank)
    for j in range(slots):
        perm, length = 0, 0
        for i in range(slots):
            here = ranks[i] == j
            perm = perm + jnp.where(here, i, 0)
            length = length + jnp.where(here, live[i], 0)
        perm_s[j] = perm
        slen_s[j] = length


def live_rows(slen_s, slot, first, rows):
    position = first + lax.broadcasted_iota(jnp.int32, (rows, 1), 0)
    return position < slen_s[slot]


def fold8(values):
    rows, lanes = values.shape
    return values.reshape(rows // 8, 8, lanes).sum(axis=0)


def normalize(values):
    center = values - jnp.mean(values, axis=-1, keepdims=True)
    spread = jnp.mean(center * center, axis=-1, keepdims=True)
    inverse = lax.rsqrt(spread + EPSILON)
    return center * inverse, inverse


def norm_back(grad_hat, normal, inverse):
    first = jnp.mean(grad_hat, axis=-1, keepdims=True)
    second = jnp.mean(grad_hat * normal, axis=-1, keepdims=True)
    return inverse * (grad_hat - first - normal * second)


def mix_slot(slot, far, exchange, tables, buf, uv, place):
    rows = exchange.rows
    if far:
        table, block = tables[...], buf[slot]
    else:
        base = aligned(exchange.q // 2 * (2 * rows), 2 * rows)
        table, block = tables[:, pl.ds(base, 2 * rows)], buf[slot, pl.ds(base, 2 * rows), :]
    both = jnp.dot(table, block, preferred_element_type=F32).astype(BF16)
    width = both.shape[1]
    uv[pl.ds(place, rows), :width] = both[:rows]
    uv[pl.ds(place, rows), width:] = both[rows:]


def group_at(i, near_groups, count):
    if near_groups == 0:
        return count - 1 - i
    return jnp.where(i < near_groups, count - near_groups + i, count - 1 - i)


def forward_kernel(cfg, *refs):
    sizes, far_slots, slots, group, agrees = cfg
    if agrees:
        choice_o, (mine, theirs, say_sem, hear_sem) = refs[agrees], refs[-4:]
        refs = refs[:agrees] + refs[agrees + 1 : -4]
    vec_refs, refs = refs[2:8], refs[:2] + refs[8:]
    (
        count_ref, length_ref, x_hbm, cot_hbm, wi_hbm, wo_hbm, sc_hbm, hc_hbm,
        act_o, dg_o, nrm_o, sum_o, gs_o, gb_o, lo_o, part_o,
        perm_s, slen_s, x_v, cot_v, wi_v, wo_v, sc_v, hc_v, buf, uv, sum_v, nrm_v, act_v, dg_v, gs_v, gb_v, lo_v, br_v, vec_ref,
        load_sem, out_sem, send_sem, recv_sem,
    ) = refs
    rows, _, features = x_v.shape
    wide = wi_v.shape[1]
    seq_total = rows * sizes[1]
    scale = 1.0 / math.sqrt(features * seq_total)
    exchange = Exchange(sizes[1], rows, buf, send_sem, recv_sem)
    q = exchange.q
    first = q * rows
    gain_one, shift_one, bias_out, gain_two, shift_two = (lambda i=i: vec_ref[i : i + 1, :] for i in range(5))
    loads = [
        pltpu.make_async_copy(x_hbm, x_v, load_sem.at[0]),
        pltpu.make_async_copy(sc_hbm.at[q], sc_v, load_sem.at[1]),
        pltpu.make_async_copy(hc_hbm, hc_v, load_sem.at[2]),
        pltpu.make_async_copy(wi_hbm, wi_v, load_sem.at[3]),
        pltpu.make_async_copy(wo_hbm, wo_v, load_sem.at[4]),
        pltpu.make_async_copy(cot_hbm, cot_v, load_sem.at[5]),
    ]
    loads[0].start()
    partners = [(exchange.dp, flipped(q, k)) for k in exchange.order]
    peers = [(lax.rem(exchange.dp + i, sizes[0]), q) for i in range(1, sizes[0])] if agrees else []
    met = greet(partners + peers)
    row = 0
    for vec in vec_refs:
        for i in range(vec.shape[0] // features):
            vec_ref[row : row + 1, :] = vec[pl.ds(i * features, features)].reshape(1, features)
            row += 1
    rank_slots(count_ref, length_ref, perm_s, slen_s, slots)
    for load in loads[1:3]:
        load.start()
    loads[0].wait()
    loads[3].start()
    met()

    def word(i):
        return pltpu.make_async_remote_copy(
            src_ref=mine,
            dst_ref=theirs.at[i],
            send_sem=say_sem.at[i],
            recv_sem=hear_sem.at[i],
            device_id=peers[i - 1],
            device_id_type=MESH,
        )

    if agrees:
        long = 0
        for i in range(slots):
            long = long + jnp.where((i < count_ref[0]) & (length_ref[i] > 2 * rows), 1, 0)
        mine[...] = jnp.full(mine.shape, long, jnp.int32).astype(F32)
        theirs[0] = mine[...]
        for i in range(1, sizes[0]):
            word(i).start()

    def prepare(i, _):
        slot = jnp.where(i < slots - far_slots, far_slots + i, slots - 1 - i)
        value = jnp.where(live_rows(slen_s, slot, first, rows), x_v[:, perm_s[slot], :], 0.0)
        buf[slot, pl.ds(aligned(first, rows), rows), :] = value.astype(BF16)
        pl.when(slot < far_slots)(lambda: exchange.start_own(slot, True))
        if far_slots < slots:
            pl.when(slot >= far_slots)(lambda: exchange.start_own(slot, False))
        return 0

    lax.fori_loop(0, slots, prepare, 0)
    part_o[...] = jnp.zeros_like(part_o)
    for load in loads[1:3]:
        load.wait()

    batch = group * rows
    folds = 2 if wide % (2 * features) == 0 else 1
    span = folds * features
    count = slots // group
    near_groups = (slots - far_slots) // group

    def outs(base):
        place = pl.ds(base, batch)
        early = [
            pltpu.make_async_copy(nrm_v.at[place], nrm_o.at[place], out_sem.at[0]),
            pltpu.make_async_copy(sum_v.at[place], sum_o.at[place], out_sem.at[1]),
        ]
        for n in range(wide // WIDE):
            cut = pl.ds(n * WIDE, WIDE)
            early.append(pltpu.make_async_copy(act_v.at[place, cut], act_o.at[n, place], out_sem.at[4]))
            early.append(pltpu.make_async_copy(dg_v.at[place, cut], dg_o.at[n, place], out_sem.at[5]))
        late = [
            pltpu.make_async_copy(gs_v.at[place], gs_o.at[place], out_sem.at[2]),
            pltpu.make_async_copy(lo_v.at[place], lo_o.at[place], out_sem.at[3]),
            pltpu.make_async_copy(gb_v.at[place], gb_o.at[place], out_sem.at[6]),
        ]
        return early, late

    def bring(slot0):
        for k in reversed(range(group)):
            exchange.forward(slot0 + k)

    def mixing(slot0, far):
        for k in reversed(range(group)):
            exchange.wait_near(slot0 + k, far)
            mix_slot(slot0 + k, far, exchange, sc_v, buf, uv, k * rows)

    def work(i, _):
        slot0 = group_at(i, near_groups, count) * group
        base = aligned(slot0 * rows, batch)
        place = pl.ds(base, batch)
        if near_groups < count:
            pl.when(i >= near_groups)(lambda: mixing(slot0, True))
        if near_groups > 0:
            pl.when(i < near_groups)(lambda: mixing(slot0, False))
        br_v[...] = jnp.dot(uv[...], hc_v[...], preferred_element_type=F32)

        for k in range(group):
            here = pl.ds(aligned(base + k * rows, rows), rows)
            mixed = (br_v[k * rows : (k + 1) * rows, :] * scale).astype(BF16).astype(F32)
            live = live_rows(slen_s, slot0 + k, first, rows)
            total = jnp.where(live, x_v[:, perm_s[slot0 + k], :], 0.0) + mixed
            sum_v[here, :] = total
            hat, _ = normalize(total)
            nrm_v[here, :] = (hat * gain_one() + shift_one()).astype(BF16)

        @pl.when(i == 0)
        def _():
            loads[3].wait()
            for load in loads[4:]:
                load.start()

        def expand(n, _):
            cut = pl.ds(aligned(n * span, span), span)
            bias = [vec_ref[pl.ds(5 + folds * n + i, 1), :] for i in range(folds)]
            hidden = jnp.dot(nrm_v[place, :], wi_v[:, cut], preferred_element_type=F32) + jnp.concatenate(bias, axis=1)
            gate = 0.5 + 0.5 * lax.erf(hidden * math.sqrt(0.5))
            slope = gate + hidden * (jnp.exp(hidden * hidden * -0.5) * (1.0 / math.sqrt(2.0 * math.pi)))
            act_v[place, cut] = (hidden * gate).astype(BF16)
            dg_v[place, cut] = slope.astype(BF16)
            return 0

        lax.fori_loop(0, wide // span, expand, 0)
        for copy in outs(base)[0]:
            copy.start()
        if near_groups < count:

            @pl.when((i + 1 >= near_groups) & (i + 1 < count))
            def _():
                bring(group_at(i + 1, near_groups, count) * group)

        pl.when(i == 0)(loads[4].wait)
        br_v[...] = jnp.dot(act_v[place, :], wo_v[...], preferred_element_type=F32)

        def norm_two(k, _):
            here = pl.ds(aligned(base + k * rows, rows), rows)
            local = pl.ds(aligned(k * rows, rows), rows)
            slot = slot0 + k
            live = live_rows(slen_s, slot, first, rows)
            hat, inverse = normalize(sum_v[here, :] + (br_v[local, :] + bias_out()))
            grad = jnp.where(live, cot_v[:, perm_s[slot], :], 0.0)
            lo_v[here, :] = jnp.where(live, hat * gain_two() + shift_two(), 0.0).astype(BF16)
            part_o[0:8, :] = part_o[0:8, :] + fold8(grad * hat)
            part_o[8:16, :] = part_o[8:16, :] + fold8(grad)
            second = norm_back(grad * gain_two(), hat, inverse)
            low = second.astype(BF16)
            gs_v[here, :] = second
            gb_v[here, :] = low
            part_o[16:24, :] = part_o[16:24, :] + fold8(low.astype(F32))
            return 0

        pl.when(i == 0)(loads[5].wait)
        lax.fori_loop(0, group, norm_two, 0)
        for copy in outs(base)[1]:
            copy.start()
        return 0

    if near_groups == 0:
        bring((count - 1) * group)
    lax.fori_loop(0, count, work, 0)

    def finish(slot, _):
        pl.when(slot < far_slots)(lambda: exchange.wait_sends(slot, True))
        if far_slots < slots:
            pl.when(slot >= far_slots)(lambda: exchange.wait_sends(slot, False))
        return 0

    lax.fori_loop(0, slots, finish, 0)

    if agrees:
        for i in range(1, sizes[0]):
            word(i).wait()
        choice_o[0] = jnp.where(jnp.max(theirs[...]) > far_slots, 1, 0)

    def flush(g, _):
        for copies in outs(aligned(g * batch, batch)):
            for copy in copies:
                copy.wait()
        return 0

    lax.fori_loop(0, count, flush, 0)


def backward_kernel(cfg, *refs):
    sizes, far_slots, slots, group, parts, mids, lags, plan = cfg
    cube = Cube(sizes, mids)
    S = cube.stages
    (
        count_ref, length_ref, gain_ref, part_ref,
        act_hbm, dg_hbm, nrm_hbm, sum_hbm, gs_hbm, gb_hbm, wi_hbm, wo_hbm, sc_hbm, hc_hbm,
        full_o, ig_o, small_o,
        perm_s, slen_s, gs_v, sum_v, nrm_v, gb_v, gh_v, gn_v, act_v, dg_v, wi_v, wo_v, sc_v, hc_v, buf, uv, mix_v, ig_v,
        bin_v, one_v, small_v, gain_v, part_v, full,
    ) = refs[:41]
    landed = refs[41 : 41 + S]
    (
        small_recv, load_sem, sum_sem, stream_sem, out_sem, ig_sem, send_sem, recv_sem,
        rs_s, rs_r, ag_s, ag_r, sm_s, sm_r,
    ) = refs[41 + S :]
    ticks, tick_rows, _ = part_v.shape
    message = tick_rows // parts
    chunks = act_hbm.shape[0]
    per_tick = chunks // ticks
    features = nrm_v.shape[1]
    rows = gs_v.shape[0] // slots
    batch = group * rows
    scale = 1.0 / math.sqrt(features * rows * sizes[1])
    exchange = Exchange(sizes[1], rows, buf, send_sem, recv_sem)
    q = exchange.q
    first = q * rows
    loads = [
        pltpu.make_async_copy(gb_hbm, gb_v, load_sem.at[0]),
        pltpu.make_async_copy(nrm_hbm, nrm_v, load_sem.at[1]),
        pltpu.make_async_copy(gs_hbm, gs_v, load_sem.at[2]),
        pltpu.make_async_copy(sc_hbm.at[q], sc_v, load_sem.at[3]),
        pltpu.make_async_copy(hc_hbm, hc_v, load_sem.at[4]),
    ]

    def turn(i):
        return jnp.where(i < far_slots, far_slots - 1 - i, i) if far_slots < slots else slots - 1 - i

    def sum_copy(i):
        place = pl.ds(aligned(turn(i) * rows, rows), rows)
        return pltpu.make_async_copy(sum_hbm.at[place], sum_v.at[lax.rem(i, 2)], sum_sem.at[lax.rem(i, 2)])

    def streams(n, slot):
        cut = pl.ds(aligned(n * WIDE, WIDE), WIDE)
        return [
            pltpu.make_async_copy(act_hbm.at[n], act_v.at[slot], stream_sem.at[0, slot]),
            pltpu.make_async_copy(wo_hbm.at[cut], wo_v.at[slot], stream_sem.at[1, slot]),
            pltpu.make_async_copy(dg_hbm.at[n], dg_v.at[slot], stream_sem.at[2, slot]),
            pltpu.make_async_copy(wi_hbm.at[:, cut], wi_v.at[slot], stream_sem.at[3, slot]),
        ]

    loads[0].start()
    streams(0, 0)[0].start()
    met = greet([cube.partner(bit) for bit in cube.bits])
    rank_slots(count_ref, length_ref, perm_s, slen_s, slots)

    side = cube.values[cube.bits[0]]
    starts, hops = [], []
    for j in range(parts):
        twin = len(cube.orders) // 2 + j
        here, there = cube.orders[j], cube.orders[twin]
        blend = lambda a, b: a + side * (b - a)
        offsets = [blend(cube.offset(j, n, message), cube.offset(twin, n, message)) for n in range(S + 1)]
        starts.append([j * message + off for off in offsets])
        hops.append(
            [
                (
                    blend(cube.values[a], cube.values[b]),
                    tuple(blend(x, y) for x, y in zip(cube.partners[a], cube.partners[b])),
                )
                for a, b in zip(here, there)
            ]
        )

    def rs(m, t, j, s):
        value, partner = hops[j][s]
        half = message >> (s + 1)
        off = starts[j][s] + (1 - value) * half
        return pltpu.make_async_remote_copy(
            src_ref=part_v.at[t, pl.ds(aligned(off, 16), half)],
            dst_ref=landed[s].at[m],
            send_sem=rs_s.at[s],
            recv_sem=rs_r.at[s, m],
            device_id=partner,
            device_id_type=MESH,
        )

    def ag(m, t, j, s):
        _, partner = hops[j][s]
        half = message >> (s + 1)
        ref = full.at[t, pl.ds(aligned(starts[j][s + 1], 16), half)]
        return pltpu.make_async_remote_copy(
            src_ref=ref,
            dst_ref=ref,
            send_sem=ag_s.at[s],
            recv_sem=ag_r.at[s, m],
            device_id=partner,
            device_id_type=MESH,
        )

    def add(m, t, j, s):
        half = message >> (s + 1)
        place = pl.ds(aligned(starts[j][s + 1], 16), half)
        total = part_v[t, place, :].astype(F32) + landed[s][m].astype(F32)
        target = full if s == S - 1 else part_v
        target[t, place, :] = total.astype(BF16)

    def out(t, j):
        place = pl.ds(j * message, message)
        return pltpu.make_async_copy(full.at[t, place], full_o.at[t, place], out_sem.at[t, j])

    def event(k, m, t, j):
        if k == 0:
            rs(m, t, j, 0).start()
        elif k <= S:
            rs(m, t, j, k - 1).wait_recv()
            add(m, t, j, k - 1)
            (rs(m, t, j, k) if k < S else ag(m, t, j, S - 1)).start()
        elif k < 2 * S:
            s = 2 * S - k
            ag(m, t, j, s).wait_recv()
            ag(m, t, j, s - 1).start()
        else:
            ag(m, t, j, 0).wait_recv()
            out(t, j).start()

    def sends_done():
        for s in range(S):
            for sem in (rs_s.at[s], ag_s.at[s]):
                pltpu.make_async_copy(landed[s], landed[s], sem).wait()

    when = [0 if per_tick == 1 and parts == 4 else parts]
    for lag in lags:
        when.append(when[-1] + lag)

    def events(tick, j):
        for k in reversed(range(2 * S + 1)):
            t = tick + (j - when[k]) // parts
            jj = (j - when[k]) % parts
            pl.when((t >= 0) & (t < ticks))(functools.partial(event, k, t * parts + jj, t, jj))

    one_v[...] = jnp.zeros_like(one_v)
    gain_v[...] = gain_ref[...].reshape(1, features)
    small_v[...] = jnp.zeros_like(small_v)
    loads[0].wait()
    for copy in streams(0, 0)[1:]:
        copy.start()
    loads[1].start()
    met()

    def load_rest():
        for load in loads[2:]:
            load.start()
        for i in range(2):
            sum_copy(i).start()


    def contract(left, right, dims):
        return lax.dot_general(left, right, ((dims, dims), ((), ())), preferred_element_type=F32)

    def weigh_out(n, slot, t, base):
        streams(n, slot)[0].wait()
        grad = contract(act_v[slot], gb_v[...], (0,)).astype(BF16)
        for i in range(features // LANES):
            part_v[t, pl.ds(base + i * WIDE, WIDE), :] = grad[:, i * LANES : (i + 1) * LANES]

    def pull(n, slot, t, base):
        streams(n, slot)[1].wait()
        streams(n, slot)[2].wait()
        pulled = contract(gb_v[...], wo_v[slot], (1,)) * dg_v[slot].astype(F32)
        pulled = pulled.astype(BF16)
        gh_v[...] = pulled
        bin_v[n] = fold8(pulled.astype(F32))

    def weigh_in(n, slot, t, base):
        pl.when(n == 0)(loads[1].wait)
        grad = contract(nrm_v[...], gh_v[...], (0,)).astype(BF16)
        for i in range(WIDE // LANES):
            place = pl.ds(base + features // LANES * WIDE + i * features, features)
            part_v[t, place, :] = grad[:, i * LANES : (i + 1) * LANES]

    def spread(n, slot, t, base):
        streams(n, slot)[3].wait()
        for i in range(2):
            here = pl.ds(i * (slots // 2) * rows, slots // 2 * rows)
            gn_v[here, :] = gn_v[here, :] + contract(gh_v[here, :], wi_v[slot], (1,))

    steps = [weigh_out, pull, weigh_in, spread]

    def compute(tick, j):
        if j == (1 if per_tick == 1 and parts == 4 else 0):

            @pl.when(tick == 0)
            def _():
                gn_v[...] = jnp.zeros_like(gn_v)

        if per_tick == 1 and parts == 4:
            slot = lax.rem(tick, 2)
            if j == 0:
                for copy in streams(tick + 1, 1 - slot):
                    pl.when(tick + 1 < chunks)(copy.start)
            steps[j](tick, slot, tick, 0)
        elif j == 0:

            def whole(u, _):
                n = tick * per_tick + u
                slot = lax.rem(n, 2)
                for copy in streams(n + 1, 1 - slot):
                    pl.when(n + 1 < chunks)(copy.start)
                for step in steps:
                    step(n, slot, tick, aligned(u * (tick_rows // per_tick), LANES))
                return 0

            lax.fori_loop(0, per_tick, whole, 0)

    def back(i, _):
        slot = turn(i)
        here = pl.ds(aligned(slot * rows, rows), rows)
        pl.when(i == 0)(loads[2].wait)
        sum_copy(i).wait()
        hat, inverse = normalize(sum_v[lax.rem(i, 2)])
        grad = gn_v[here, :]
        one_v[0:8, :] = one_v[0:8, :] + fold8(grad * hat)
        one_v[8:16, :] = one_v[8:16, :] + fold8(grad)
        grad = gs_v[here, :] + norm_back(grad * gain_v[...], hat, inverse)
        gs_v[here, :] = grad
        buf[slot, pl.ds(aligned(first, rows), rows), :] = grad.astype(BF16)
        pl.when(i < far_slots)(lambda: exchange.start_own(slot, True))
        if far_slots < slots:
            pl.when(i >= far_slots)(lambda: exchange.start_own(slot, False))
        pl.when(i + 2 < slots)(lambda: sum_copy(i + 2).start())
        return 0

    def small_copy(s):
        return pltpu.make_async_remote_copy(
            src_ref=small_v.at[s],
            dst_ref=small_recv.at[s],
            send_sem=sm_s.at[s],
            recv_sem=sm_r.at[s],
            device_id=cube.partners[cube.bits[s]],
            device_id_type=MESH,
        )

    def small_start():
        row = 0
        vectors = [one_v[0:8, :], one_v[8:16, :]] + [bin_v[n] for n in range(chunks)]
        vectors += [part_ref[16:24, :], part_ref[0:8, :], part_ref[8:16, :]]
        for vector in vectors:
            vector = jnp.sum(vector, axis=0, keepdims=True)
            for i in range(vector.shape[1] // LANES):
                small_v[0, row : row + 1, :] = vector[:, i * LANES : (i + 1) * LANES]
                row += 1
        small_copy(0).start()

    def small_step(s):
        small_copy(s).wait()
        if s + 1 < S:
            small_v[s + 1] = small_v[s] + small_recv[s]
            small_copy(s + 1).start()
        else:
            small_o[...] = small_v[s] + small_recv[s]

    count = slots // group
    near_groups = (slots - far_slots) // group

    def grad_copy(i):
        base = aligned(group_at(i, near_groups, count) * batch, batch)
        return pltpu.make_async_copy(ig_v.at[lax.rem(i, 2)], ig_o.at[pl.ds(base, batch)], ig_sem.at[lax.rem(i, 2)])

    def mixing(i, k, far):
        slot = group_at(i, near_groups, count) * group + k
        exchange.wait_near(slot, far)
        mix_slot(slot, far, exchange, sc_v, buf, uv, k * rows)

    def hidden_mix(i):
        pl.when(i >= 2)(lambda: grad_copy(i - 2).wait())
        mix_v[...] = jnp.dot(uv[...], hc_v[...], preferred_element_type=F32)

    def finish(i):
        for k in range(group):
            slot = group_at(i, near_groups, count) * group + k
            here = pl.ds(aligned(slot * rows, rows), rows)
            local = pl.ds(k * rows, rows)
            grad = gs_v[here, :] + mix_v[local, :] * scale
            grad = jnp.where(live_rows(slen_s, slot, first, rows), grad, 0.0)
            ig_v[lax.rem(i, 2), local, :] = grad.astype(BF16)
        grad_copy(i).start()

    def bring(i):
        for k in reversed(range(group)):
            exchange.forward(group_at(i, near_groups, count) * group + k)

    small_at, near_at, far_at, lead = plan

    def drain(tick, j):
        d = tick - ticks

        @pl.when(d == 0)
        def _():
            share = -(-slots // parts)
            lax.fori_loop(min(j * share, slots), min((j + 1) * share, slots), back, 0)

        here = lambda at: pl.when(d * parts + j == at)
        if j == small_at % parts:
            here(small_at)(small_start)
        for s in range(S):
            at = small_at + 5 * (s + 1)
            if j == at % parts:
                here(at)(functools.partial(small_step, s))
        if j == 0:

            @pl.when(d == 1)
            def _():
                for load in loads[3:]:
                    load.wait()

        for far, start, low, high in ((False, near_at, 0, near_groups), (True, far_at, near_groups, count)):
            if low == high:
                continue
            i = d - start + low

            @pl.when((i >= low) & (i < high))
            def _():
                subs = [
                    lambda: mixing(i, 0, far),
                    lambda: [mixing(i, k, far) for k in range(1, group)],
                    lambda: hidden_mix(i),
                    lambda: finish(i),
                ]
                for at, sub in enumerate(subs):
                    if min(at, parts - 1) == j:
                        sub()

            if far and j == parts - 1:
                ahead = i + lead
                pl.when((ahead >= low) & (ahead < high))(lambda: bring(ahead))

    last = ticks + max(
        -(-(when[-1] + 1) // parts),
        (small_at + 5 * S) // parts + 1,
        near_at + near_groups,
        far_at + count - near_groups,
    )

    def body(tick, _):
        pl.when(tick == 1)(load_rest)
        for j in range(parts):
            pl.when(tick < ticks)(lambda: compute(tick, j))
            events(tick, j)
            pl.when(tick >= ticks)(lambda: drain(tick, j))
        return 0

    lax.fori_loop(0, last, body, 0)

    def settle(slot, _):
        pl.when(slot < far_slots)(lambda: exchange.wait_sends(slot, True))
        if far_slots < slots:
            pl.when(slot >= far_slots)(lambda: exchange.wait_sends(slot, False))
        return 0

    lax.fori_loop(0, slots, settle, 0)
    for i in range(max(0, count - 2), count):
        grad_copy(i).wait()

    def finish_out(t, _):
        for j in range(parts):
            out(t, j).wait()
        return 0

    lax.fori_loop(0, ticks, finish_out, 0)
    sends_done()


def output_kernel(slots, cuts, places, count_ref, length_ref, full_ref, lo_ref, ig_ref, small_ref, *refs):
    wi_ref, wo_ref, lo_out, ig_out = refs[:4]
    vector_refs, (perm_s, slen_s) = refs[4:-2], refs[-2:]
    step = pl.program_id(0)
    features = wi_ref.shape[0]
    for u in range(full_ref.shape[0]):
        base = u * WIDE
        for i in range(features // LANES):
            wo_ref[base : base + WIDE, i * LANES : (i + 1) * LANES] = full_ref[u, pl.ds(i * WIDE, WIDE), :].astype(F32)
        for i in range(WIDE // LANES):
            start = features // LANES * WIDE + i * features
            wi_ref[:, base + i * LANES : base + (i + 1) * LANES] = full_ref[u, pl.ds(start, features), :].astype(F32)

    @pl.when(step == 0)
    def _():
        rank_slots(count_ref, length_ref, perm_s, slen_s, slots)
        for ref, start in zip(vector_refs, cuts):
            ref[...] = small_ref[start : start + ref.shape[0], :]

    @pl.when(step < places)
    def _():
        for j in range(slots):
            lo_out[:, perm_s[j], :] = lo_ref[j].astype(F32)
            ig_out[:, perm_s[j], :] = ig_ref[j].astype(F32)


ANY = pl.BlockSpec(memory_space=pl.ANY)
SMEM = pl.BlockSpec(memory_space=pltpu.SMEM)
VMEM = pl.BlockSpec(memory_space=pltpu.VMEM)
DMA = pltpu.SemaphoreType.DMA
LAGS = [3, 5, 4, 3, 3, 3, 3, 4, 6, 3]
PLAN = (4, 1, 4, 1)
FAR_PLAN = (4, 1, 4, 1)
XYZ, YXZ, ZXY, YZX, ZYX = (0, 1, 2), (1, 0, 2), (2, 0, 1), (1, 2, 0), (2, 1, 0)
MIDS = (XYZ, YXZ, ZXY, YZX, YXZ, ZXY, YZX, XYZ)
FAR_MIDS = (YZX, ZYX, YXZ, ZXY, ZXY, YZX, XYZ, YXZ)


def run_forward(sizes, far_slots, slots, *operands, agrees=False, group=2, name="forward", cid=1):
    rows, _, features = operands[8].shape
    wide = operands[10].shape[1]
    seq_total = rows * sizes[1]
    flat, batch, chunks = rows * slots, group * rows, wide // WIDE
    shape = jax.ShapeDtypeStruct
    return pl.pallas_call(
        functools.partial(forward_kernel, (sizes, far_slots, slots, group, len(operands) + 8 if agrees else 0)),
        name=name,
        out_shape=(
            shape((chunks, flat, WIDE), BF16),
            shape((chunks, flat, WIDE), BF16),
            shape((flat, features), BF16),
            shape((flat, features), F32),
            shape((flat, features), F32),
            shape((flat, features), BF16),
            shape((flat, features), BF16),
            shape((24, features), F32),
        )
        + ((shape((1,), jnp.int32),) if agrees else ()),
        in_specs=[SMEM] * 2 + [VMEM] * 6 + [ANY] * 6,
        out_specs=[ANY] * 7 + [VMEM] + [SMEM] * agrees,
        scratch_shapes=[
            pltpu.SMEM((slots,), jnp.int32),
            pltpu.SMEM((slots,), jnp.int32),
            pltpu.VMEM((rows, slots, features), F32),
            pltpu.VMEM((rows, slots, features), F32),
            pltpu.VMEM((features, wide), BF16),
            pltpu.VMEM((wide, features), BF16),
            pltpu.VMEM((2 * rows, seq_total), BF16),
            pltpu.VMEM((2 * features, features), BF16),
            pltpu.VMEM((slots, seq_total, features), BF16),
            pltpu.VMEM((batch, 2 * features), BF16),
            pltpu.VMEM((flat, features), F32),
            pltpu.VMEM((flat, features), BF16),
            pltpu.VMEM((flat, wide), BF16),
            pltpu.VMEM((flat, wide), BF16),
            pltpu.VMEM((flat, features), F32),
            pltpu.VMEM((flat, features), BF16),
            pltpu.VMEM((flat, features), BF16),
            pltpu.VMEM((batch, features), F32),
            pltpu.VMEM((5 + wide // features, features), F32),
            DMA((6,)),
            DMA((7,)),
            DMA((slots, sizes[1])),
            DMA((slots, sizes[1])),
        ]
        + agrees * [pltpu.VMEM((8, LANES), F32), pltpu.VMEM((sizes[0], 8, LANES), F32), DMA((sizes[0],)), DMA((sizes[0],))],
        compiler_params=pltpu.CompilerParams(collective_id=cid, has_side_effects=True, vmem_limit_bytes=62 << 20),
    )(*operands)


def run_backward(sizes, far_slots, slots, ticks, tick_rows, parts, *operands, group=2, mids=None, lags=None, plan=None, name="backward", cid=2):
    devices = sizes[0] * sizes[1]
    chunks, flat, _ = operands[4].shape
    features, wide = operands[10].shape
    rows = flat // slots
    seq_total = rows * sizes[1]
    batch = group * rows
    message = tick_rows // parts
    shape = jax.ShapeDtypeStruct
    mostly_far = far_slots > slots * 5 // 8
    mids = mids or (FAR_MIDS if mostly_far else MIDS)
    plan = plan or (FAR_PLAN if mostly_far else PLAN)
    lags = lags or LAGS
    stages = devices.bit_length() - 1
    lags = (lags[:stages] + [2] * stages)[:stages] + ([2] * stages + lags[-stages:])[-stages:]
    return pl.pallas_call(
        functools.partial(backward_kernel, (sizes, far_slots, slots, group, parts, mids, lags, plan)),
        name=name,
        out_shape=(
            shape((ticks, tick_rows, LANES), BF16),
            shape((flat, features), BF16),
            shape((64, LANES), F32),
        ),
        in_specs=[SMEM] * 2 + [VMEM] * 2 + [ANY] * 10,
        out_specs=[ANY] * 2 + [VMEM],
        scratch_shapes=[
            pltpu.SMEM((slots,), jnp.int32),
            pltpu.SMEM((slots,), jnp.int32),
            pltpu.VMEM((flat, features), F32),
            pltpu.VMEM((2, rows, features), F32),
            pltpu.VMEM((flat, features), BF16),
            pltpu.VMEM((flat, features), BF16),
            pltpu.VMEM((flat, WIDE), BF16),
            pltpu.VMEM((flat, features), F32),
            pltpu.VMEM((2, flat, WIDE), BF16),
            pltpu.VMEM((2, flat, WIDE), BF16),
            pltpu.VMEM((2, features, WIDE), BF16),
            pltpu.VMEM((2, WIDE, features), BF16),
            pltpu.VMEM((2 * rows, seq_total), BF16),
            pltpu.VMEM((2 * features, features), BF16),
            pltpu.VMEM((slots, seq_total, features), BF16),
            pltpu.VMEM((batch, 2 * features), BF16),
            pltpu.VMEM((batch, features), F32),
            pltpu.VMEM((2, batch, features), BF16),
            pltpu.VMEM((chunks, 8, WIDE), F32),
            pltpu.VMEM((16, features), F32),
            pltpu.VMEM((stages, 64, LANES), F32),
            pltpu.VMEM((1, features), F32),
            pltpu.VMEM((ticks, tick_rows, LANES), BF16),
            pltpu.VMEM((ticks, tick_rows, LANES), BF16),
        ]
        + [pltpu.VMEM((ticks * parts, message >> (s + 1), LANES), BF16) for s in range(stages)]
        + [
            pltpu.VMEM((stages, 64, LANES), F32),
            DMA((5,)),
            DMA((2,)),
            DMA((4, 2)),
            DMA((ticks, parts)),
            DMA((2,)),
            DMA((slots, sizes[1])),
            DMA((slots, sizes[1])),
            DMA((stages,)),
            DMA((stages, ticks * parts)),
            DMA((stages,)),
            DMA((stages, ticks * parts)),
            DMA((stages,)),
            DMA((stages,)),
        ],
        compiler_params=pltpu.CompilerParams(collective_id=cid, has_side_effects=True, vmem_limit_bytes=62 << 20),
    )(*operands)


def cut_messages(devices, chunks, chunk_rows):
    per_tick, parts = min(
        (count, -cut)
        for count in range(1, chunks + 1)
        for cut in range(1, 5)
        if chunks % count == 0 and chunk_rows * count % (devices * 16 * cut) == 0
    )
    return per_tick, -parts


def rest_of_layer(far_slots, sizes, cid, known, inputs, item_counts, lengths, vectors, weight_in, weight_out, cotangent, seq_table, hid_table):
    rows, slots, features = inputs.shape
    wide = weight_in.shape[1]
    chunks = wide // WIDE
    chunk_rows = 2 * features * WIDE // LANES
    shape = jax.ShapeDtypeStruct
    per_tick, parts = cut_messages(sizes[0] * sizes[1], chunks, chunk_rows)
    act, dg, nrm, summed, second, low, lo, part = known or run_forward(
        sizes, far_slots, slots,
        item_counts, lengths, *vectors, inputs, cotangent, weight_in, weight_out, seq_table, hid_table,
        cid=cid,
    )
    full, grad, small = run_backward(
        sizes, far_slots, slots, chunks // per_tick, chunk_rows * per_tick, parts,
        item_counts, lengths, vectors[0], part, act, dg, nrm, summed, second, low, weight_in, weight_out, seq_table, hid_table,
        cid=cid + 1,
    )
    side = 2 if chunks % 2 == 0 else 1
    places = 1 << min((chunks // side).bit_length() - 1, 3)
    step = rows // places
    lo, grad = lo.reshape(slots, rows, features), grad.reshape(slots, rows, features)
    heights = [size // LANES for size in (features, features, wide, features, features, features)]
    cuts = [sum(heights[:i]) for i in range(len(heights))]
    slot_first = pl.BlockSpec((slots, step, features), lambda n: (0, jnp.minimum(n, places - 1), 0))
    place_first = pl.BlockSpec((step, slots, features), lambda n: (jnp.minimum(n, places - 1), 0, 0))
    wi_grad, wo_grad, layer_out, input_grad, *vectors = pl.pallas_call(
        functools.partial(output_kernel, slots, cuts, places),
        name="output",
        grid=(chunks // side,),
        out_shape=(
            shape((features, wide), F32),
            shape((wide, features), F32),
            shape(inputs.shape, F32),
            shape(inputs.shape, F32),
            *(shape((height, LANES), F32) for height in heights),
        ),
        in_specs=[SMEM] * 2 + [pl.BlockSpec((side, chunk_rows, LANES), lambda n: (n, 0, 0))] + [slot_first] * 2 + [VMEM],
        out_specs=(
            pl.BlockSpec((features, side * WIDE), lambda n: (0, n)),
            pl.BlockSpec((side * WIDE, features), lambda n: (n, 0)),
            place_first,
            place_first,
            *([VMEM] * len(heights)),
        ),
        scratch_shapes=[pltpu.SMEM((slots,), jnp.int32), pltpu.SMEM((slots,), jnp.int32)],
        compiler_params=pltpu.CompilerParams(vmem_limit_bytes=60 << 20),
    )(item_counts, lengths, full.reshape(chunks, chunk_rows, LANES), lo, grad, small)
    gain_one_grad, shift_one_grad, bias_in_grad, bias_out_grad, gain_two_grad, shift_two_grad = [v.reshape(-1) for v in vectors]
    return (
        layer_out, input_grad, gain_one_grad, shift_one_grad, wi_grad, bias_in_grad, wo_grad, bias_out_grad, gain_two_grad, shift_two_grad,
    )


def per_device(
    inputs, item_counts, lengths, gain_one, shift_one, weight_in, bias_in, weight_out, bias_out, gain_two, shift_two, cotangent
):
    rows, slots, features = inputs.shape
    wide = weight_in.shape[1]
    sizes = (lax.axis_size("dp"), lax.axis_size("seq"))
    seq_total = rows * sizes[1]
    chunks = wide // WIDE
    chunk_rows = 2 * features * WIDE // LANES
    shape = jax.ShapeDtypeStruct

    seq_cos, seq_sin = dft_tables(seq_total)
    hid_cos, hid_sin = dft_tables(features)
    seq_table = [table.reshape(sizes[1], rows, seq_total) for table in (seq_cos, seq_sin)]
    seq_table = jnp.asarray(np.concatenate(seq_table, axis=1).astype(jnp.bfloat16))
    hid_table = jnp.asarray(np.concatenate([hid_cos, -hid_sin], axis=0).astype(jnp.bfloat16))
    vectors = (gain_one, shift_one, bias_out, gain_two, shift_two, bias_in)
    operands = (inputs, item_counts, lengths, vectors, weight_in, weight_out, cotangent, seq_table, hid_table)

    few = slots // 2
    *known, choice = run_forward(
        sizes, few, slots,
        item_counts, lengths, *vectors, inputs, cotangent, weight_in, weight_out, seq_table, hid_table,
        agrees=True, cid=1,
    )
    return lax.cond(
        choice[0] == 0,
        lambda known, *given: rest_of_layer(few, sizes, 2, known, *given),
        lambda known, *given: rest_of_layer(slots, sizes, 4, None, *given),
        tuple(known), *operands,
    )


def solution(mesh):
    placed = (
        P("seq", "dp", None), P("dp"), P("dp"), P(), P(), P(), P(), P(), P(), P(), P(), P("seq", "dp", None),
    )
    wide = P("seq", "dp", None)
    return jax.shard_map(
        per_device,
        mesh=mesh,
        in_specs=placed,
        out_specs=(wide, wide, P(), P(), P(), P(), P(), P(), P(), P()),
        check_vma=False,
    )
```
